32 devices in a mesh: blk: 8 (over z, x), uly: 4 (over y, core).
Axes of the slice: x: 2, y: 2, z: 4, core: 2. Of those that a mesh axis runs over, the one named last changes fastest.
Arguments:
- tokens: bfloat16 [4096, 2048], P(('blk', 'uly')), may hold values from -6 to 6
- segments: int32 [4096], replicated, may hold values from 0 to 66, as said below
- cotangent: bfloat16 [4096, 2048], P(('blk', 'uly')), may hold values from -6 to 6
- attn_gain: float32 [2048], P('blk'), may hold values from 0.5 to 1.5
- w_query: float32 [2048, 2048], P('blk', 'uly'), may hold values from -0.125 to 0.125
- w_key: float32 [2048, 2048], P('blk', 'uly'), may hold values from -0.125 to 0.125
- w_value: float32 [2048, 2048], P('blk', 'uly'), may hold values from -0.125 to 0.125
- w_output: float32 [2048, 2048], P('blk', 'uly'), may hold values from -0.5 to 0.5
- mlp_gain: float32 [2048], P('blk'), may hold values from 0.5 to 1.5
- w_gate: float32 [2048, 8192], P('blk', 'uly'), may hold values from -0.125 to 0.125
- w_up: float32 [2048, 8192], P('blk', 'uly'), may hold values from -0.125 to 0.125
- w_down: float32 [2048, 8192], P('blk', 'uly'), may hold values from -0.0625 to 0.0625
Outputs:
- output: float32 [4096, 2048], P(('blk', 'uly'))
- grad_tokens: float32 [4096, 2048], P(('blk', 'uly'))
- grad_attn_gain: float32 [2048], P('blk')
- grad_query: float32 [2048, 2048], P('blk', 'uly')
- grad_key: float32 [2048, 2048], P('blk', 'uly')
- grad_value: float32 [2048, 2048], P('blk', 'uly')
- grad_output: float32 [2048, 2048], P('blk', 'uly')
- grad_mlp_gain: float32 [2048], P('blk')
- grad_gate: float32 [2048, 8192], P('blk', 'uly')
- grad_up: float32 [2048, 8192], P('blk', 'uly')
- grad_down: float32 [2048, 8192], P('blk', 'uly')
The draws below stay inside these ranges and needn't reach their ends.
Inputs may be any that keep to these rules, and one draw needn't show every extreme that they name: `segments`: document numbers start at 0, never fall and rise by at most one from a token to the next; one document starts within the first 512 tokens and ends within the last 512; there are exactly 3 + 2 * (32) documents.
All inputs are finite; a program needn't handle non-finite values.
Results may differ from the reference program's by a relative error of at most 0.023.
Values may be sent and summed in bfloat16 or wider, within the bound.
No kernel may reach another device: no remote copies, remote signals or barrier semaphores. Data moves between devices by JAX's collectives and lax.ppermute only.
A program may use at most 384 MiB of HBM per device.

```python
import math
import jax
import jax.numpy as jnp
from jax import lax

D = 2048
H = 32
HD = 64
FF = 8192
BLOCK = 512
SEQ = 4096


def draw_segments(key, part):
    key_start = jax.random.fold_in(key, 11)
    key_end = jax.random.fold_in(key, 12)
    key_flags = jax.random.fold_in(key, 13)
    index = jnp.arange(SEQ, dtype=jnp.int32)
    first_cut = jax.random.randint(key_start, (), BLOCK // 4, BLOCK // 2 + 1, dtype=jnp.int32)
    last_cut = jax.random.randint(key_end, (), SEQ - BLOCK // 2, SEQ - BLOCK // 4 + 1, dtype=jnp.int32)
    spread_top = max(2 ** 30 // SEQ, 2)
    noise = jax.random.randint(key_flags, (SEQ,), 0, spread_top, dtype=jnp.int32)
    score = noise * SEQ + index
    picks_count = BLOCK // 16
    head_valid = (index >= 1) & (index < first_cut)
    tail_valid = index >= last_cut + 2
    head_picks = lax_top(jnp.where(head_valid, score, -1), picks_count)
    tail_picks = lax_top(jnp.where(tail_valid, score, -1), picks_count)
    picked = jnp.any(index[:, None] == jnp.concatenate([head_picks, tail_picks])[None, :], axis=1)
    boundary = picked | (index == first_cut) | (index == last_cut + 1)
    return jnp.cumsum(boundary.astype(jnp.int32)).astype(jnp.int32)


def lax_top(values, count):
    return jax.lax.top_k(values, count)[1].astype(jnp.int32)


def levels(key, extent, pieces, least, top_value):
    level = 1.0
    for dim, parts in pieces:
        steps = jax.random.uniform(jax.random.fold_in(jax.random.fold_in(key, 6), dim), (parts,), jnp.float32, least / len(pieces), top_value / len(pieces))
        level = level * jnp.repeat(jnp.exp(steps), extent[dim] // parts).reshape((-1,) + (1,) * (len(extent) - 1 - dim))
    return level


def scatter_about(key, dims, deviation, most, shards=(), held_as=jnp.bfloat16):
    level = levels(key, dims, shards, -0.22, 0.18) if shards else 1.0
    entries = jax.random.normal(key, dims, jnp.float32) * deviation * level
    return jnp.minimum(jnp.maximum(entries, -most), most).astype(held_as)


def setup_inputs(seed: int = 0) -> dict:
    streams_of = jax.random.split(jax.random.key(seed), 13)
    return {
        "tokens": scatter_about(streams_of[0], (SEQ, D), 1.0, 6.0, ((0, 32),)),
        "segments": draw_segments(jax.random.fold_in(streams_of[12], 71), 0),
        "cotangent": scatter_about(streams_of[2], (SEQ, D), 1.0, 6.0, ((0, 32),)),
        "attn_gain": jnp.clip(1.0 + 0.1 * jax.random.normal(streams_of[3], (D,), jnp.float32), 0.5, 1.5),
        "w_query": scatter_about(streams_of[4], (D, D), D ** -0.5, 0.125, ((0, 8), (1, 4)), jnp.float32),
        "w_key": scatter_about(streams_of[5], (D, D), D ** -0.5, 0.125, ((0, 8), (1, 4)), jnp.float32),
        "w_value": scatter_about(streams_of[6], (D, D), D ** -0.5, 0.125, ((0, 8), (1, 4)), jnp.float32),
        "w_output": scatter_about(streams_of[7], (D, D), (D // 16) ** -0.5, 0.5, ((0, 8), (1, 4)), jnp.float32),
        "mlp_gain": jnp.clip(1.0 + 0.1 * jax.random.normal(streams_of[8], (D,), jnp.float32), 0.5, 1.5),
        "w_gate": scatter_about(streams_of[9], (D, FF), D ** -0.5, 0.125, ((0, 8), (1, 4)), jnp.float32),
        "w_up": scatter_about(streams_of[10], (D, FF), D ** -0.5, 0.125, ((0, 8), (1, 4)), jnp.float32),
        "w_down": scatter_about(streams_of[11], (D, FF), FF ** -0.5, 0.0625, ((0, 8), (1, 4)), jnp.float32),
    }


@jax.custom_vjp
def low(v):
    return lax.optimization_barrier(v.astype(jnp.bfloat16)).astype(jnp.float32)

@jax.custom_vjp
def low_back(v):
    return v

def low_keep(v):
    return (low(v), None)

def low_pass(kept, grad):
    return (grad,)

def back_keep(v):
    return (v, None)

def back_low(kept, grad):
    return (low(grad),)
low.defvjp(low_keep, low_pass)
low_back.defvjp(back_keep, back_low)
theta_base = 130000.0
epsilon = 1e-05
highest = lax.Precision.HIGHEST

def doc_positions(segments):
    count = segments.shape[0]
    index = jnp.arange(count, dtype=jnp.int32)
    first = jnp.concatenate([jnp.ones((1,), bool), segments[1:] != segments[:-1]])
    start = lax.cummax(jnp.where(first, index, 0), axis=0)
    return index - start

def rotary_tables(positions):
    half = HD // 2
    freqs = theta_base ** (-(jnp.arange(half, dtype=jnp.float32) * 2.0) / HD)
    angles = positions.astype(jnp.float32)[:, None] * freqs[None, :]
    return (jnp.cos(angles)[:, None, :], jnp.sin(angles)[:, None, :])

def rotate(value, cosine, sine):
    half = HD // 2
    first, second = (value[..., :half], value[..., half:])
    return jnp.concatenate([first * cosine - second * sine, second * cosine + first * sine], axis=-1)

def matmul(left, right):
    return jnp.dot(left, right, precision=highest)

def rms_scale(value):
    return lax.rsqrt(lax.optimization_barrier(jnp.mean(value * value, axis=-1, keepdims=True)) + epsilon)

def reference(tokens, segments, cotangent, attn_gain, w_query, w_key, w_value, w_output, mlp_gain, w_gate, w_up, w_down):
    seq = segments.shape[0]
    positions = doc_positions(segments)
    cosine, sine = rotary_tables(positions)
    scale = 1.0 / math.sqrt(HD)
    qblock = math.gcd(seq, 512)
    seq_index = jnp.arange(seq, dtype=jnp.int32)

    def forward(x, gain1, wq, wk, wv, wo, gain2, wg, wu, wd):
        gain1, wq, wk, wv, wo = (low(gain1), low(wq), low(wk), low(wv), low(wo))
        gain2, wg, wu, wd = (low(gain2), low(wg), low(wu), low(wd))
        normed = low(x * rms_scale(x) * gain1)
        query = low_back(low(matmul(normed, wq))).reshape(seq, H, HD)
        key = low_back(low(matmul(normed, wk))).reshape(seq, H, HD)
        value = low_back(low(matmul(normed, wv))).reshape(seq, H, HD)
        q_rot = low(rotate(query, cosine, sine))
        k_rot = low(rotate(key, cosine, sine))

        def attend(block):
            start = (block * qblock).astype(jnp.int32)
            q_part = lax.dynamic_slice_in_dim(q_rot, start, qblock, 0)
            q_seg = lax.dynamic_slice_in_dim(segments, start, qblock, 0)
            q_idx = start + jnp.arange(qblock, dtype=jnp.int32)
            scores = low_back(jnp.einsum('qhd,khd->hqk', q_part, k_rot, precision=highest) * scale)
            allowed = (q_seg[:, None] == segments[None, :]) & (seq_index[None, :] <= q_idx[:, None])
            masked = jnp.where(allowed[None], scores, -1e+30)
            top = lax.optimization_barrier(jnp.max(masked, axis=-1, keepdims=True))
            expo = jnp.where(allowed[None], jnp.exp(masked - top), 0.0)
            probs = expo / lax.optimization_barrier(jnp.sum(expo, axis=-1, keepdims=True))
            return jnp.einsum('hqk,khd->qhd', low(probs), value, precision=highest)
        blocks = lax.map(jax.checkpoint(attend), jnp.arange(seq // qblock, dtype=jnp.int32))
        attn_o = low_back(low(blocks.reshape(seq, H * HD)))
        x1 = x + low_back(matmul(attn_o, wo.T))
        normed2 = low(x1 * rms_scale(x1) * gain2)
        gate = low_back(matmul(normed2, wg))
        up = low_back(matmul(normed2, wu))
        act = low(jax.nn.sigmoid(gate) * gate * up)
        return x1 + matmul(act, wd.T)
    x = tokens.astype(jnp.float32)
    output, pullback = jax.vjp(forward, x, attn_gain, w_query, w_key, w_value, w_output, mlp_gain, w_gate, w_up, w_down)
    grads = pullback(cotangent.astype(jnp.float32))
    return (output, grads[0], grads[1], grads[2], grads[3], grads[4], grads[5], grads[6], grads[7], grads[8], grads[9])
```

```python
import functools
import math

import jax
import jax.numpy as jnp
from jax import lax
from jax.experimental import pallas as pl
from jax.experimental.pallas import tpu as pltpu
from jax.sharding import PartitionSpec as P

H = 32
HD = 64
LANES = 128

theta_base = 130000.0
epsilon = 1e-05
bf = jnp.bfloat16
f32 = jnp.float32
NEG = -1e30


def dot_t(left, right):
    return lax.dot_general(left, right, (((1,), (1,)), ((), ())), preferred_element_type=f32)


def dot_n(left, right):
    return jnp.dot(left, right, preferred_element_type=f32)


def dot_c(left, right):
    return lax.dot_general(left, right, (((0,), (0,)), ((), ())), preferred_element_type=f32)


def rms_scale(value):
    return lax.rsqrt(jnp.mean(value * value, axis=-1, keepdims=True) + epsilon)


def gather(value, axis):
    return lax.all_gather(value, axis, axis=0, tiled=True)


def scatter(value, axis):
    return lax.psum_scatter(value, axis, scatter_dimension=0, tiled=True)


def swap(value, axis):
    return lax.all_to_all(value, axis, 0, 0, tiled=True)


def allowed_block(segk_ref, seg_q, pos_q, chunk, width):
    seg_k = segk_ref[pl.ds(pl.multiple_of(chunk * width, width), width), :]
    pos_k = chunk * width + lax.broadcasted_iota(jnp.int32, (width, 1), 0)
    return (seg_k == seg_q) & (pos_k <= pos_q)


def head_lanes(rows, head):
    lane = lax.broadcasted_iota(jnp.int32, (rows, LANES), 1)
    return (lane < HD) if head == 0 else (lane >= HD)


def attend_kernel(tile, segk_ref, segq_ref, posq_ref, q_ref, k_ref, v_ref, o_ref, lse_ref, vt_ref):
    nu, nb, tok, _ = k_ref.shape
    width = nu * tok
    rows = tile * tok
    j = pl.program_id(1)

    @pl.when(j == 0)
    def _():
        for c in range(nb):
            vt_ref[c] = v_ref[:, c].reshape(width, LANES).T

    seg_q, pos_q = segq_ref[0], posq_ref[0]
    q = q_ref[...] * jnp.asarray(1.0 / math.sqrt(HD), bf)
    q_heads = [jnp.where(head_lanes(rows, h), q, jnp.zeros_like(q)) for h in range(2)]

    def step(chunk, state):
        k = k_ref[:, chunk].reshape(width, LANES)
        v_t = vt_ref[chunk]
        ok = allowed_block(segk_ref, seg_q, pos_q, chunk, width)
        new = []
        for h in range(2):
            best, total, acc = state[h]
            s = jnp.where(ok, dot_t(k, q_heads[h]), NEG)
            best_new = jnp.maximum(best, jnp.max(s, axis=0, keepdims=True))
            p = jnp.exp(s - best_new)
            factor = jnp.exp(best - best_new)
            total = total * factor + jnp.sum(p, axis=0, keepdims=True)
            acc = acc * factor + dot_n(v_t[h * HD : (h + 1) * HD], p.astype(bf))
            new.append((best_new, total, acc))
        return tuple(new)

    start = (
        jnp.full((1, rows), NEG, f32),
        jnp.zeros((1, rows), f32),
        jnp.zeros((HD, rows), f32),
    )
    state = lax.fori_loop(0, (j + 1) * tile, step, (start, start))
    o_t = jnp.concatenate([acc / total for _, total, acc in state], axis=0)
    o_ref[...] = o_t.T.astype(bf)
    lse_ref[0, 0] = jnp.concatenate([best + jnp.log(total) for best, total, _ in state], axis=0)


def attend(segments, seg_q, pos_q, q, k, v, tile):
    nu, nb, tok, feats = k.shape
    rows = tile * tok
    nq = nb // tile
    pairs = feats // LANES
    row_spec = pl.BlockSpec((1, 1, rows), lambda p, j: (j, 0, 0))
    kv_spec = pl.BlockSpec((nu, nb, tok, LANES), lambda p, j: (0, 0, 0, p))
    q_spec = pl.BlockSpec((rows, LANES), lambda p, j: (j, p))
    return pl.pallas_call(
        functools.partial(attend_kernel, tile),
        grid=(pairs, nq),
        in_specs=[
            pl.BlockSpec((nu * nb * tok, 1), lambda p, j: (0, 0)),
            row_spec,
            row_spec,
            q_spec,
            kv_spec,
            kv_spec,
        ],
        out_specs=[q_spec, pl.BlockSpec((1, 1, 2, rows), lambda p, j: (p, j, 0, 0))],
        out_shape=[
            jax.ShapeDtypeStruct((nb * tok, feats), bf),
            jax.ShapeDtypeStruct((pairs, nq, 2, rows), f32),
        ],
        scratch_shapes=[pltpu.VMEM((nb, LANES, nu * tok), bf)],
        compiler_params=pltpu.CompilerParams(vmem_limit_bytes=48 * 2**20),
        name="attend",
    )(segments, seg_q, pos_q, q, k, v)


def attend_back_kernel(
    tile,
    segk_ref,
    segq_ref,
    posq_ref,
    cos_ref,
    sin_ref,
    q_ref,
    do_ref,
    o_ref,
    lse_ref,
    k_ref,
    v_ref,
    dq_ref,
    dkv_ref,
    acc_ref,
    delta_ref,
):
    nu, _, tok, _ = k_ref.shape
    nq = segq_ref.shape[0]
    width = nu * tok
    rows = tile * tok
    chunk = pl.program_id(1)
    scale = jnp.asarray(1.0 / math.sqrt(HD), bf)

    @pl.when(chunk == 0)
    def _():
        acc_ref[...] = jnp.zeros_like(acc_ref)
        lane = lax.broadcasted_iota(jnp.int32, (8, LANES), 1)
        row = lax.broadcasted_iota(jnp.int32, (8, LANES), 0)
        pick = jnp.where(lane // HD == row, 1.0, 0.0).astype(f32)
        for j in range(nq):
            part = do_ref[pl.ds(j * rows, rows), :].astype(f32) * o_ref[
                pl.ds(j * rows, rows), :
            ].astype(f32)
            delta_ref[j] = lax.dot_general(
                pick,
                part,
                (((1,), (1,)), ((), ())),
                preferred_element_type=f32,
                precision=lax.Precision.HIGHEST,
            )

    k = k_ref[:, 0].reshape(width, LANES)
    v = v_ref[:, 0].reshape(width, LANES)

    def step(j, state):
        dk, dv = state
        at = pl.ds(pl.multiple_of(j * rows, rows), rows)
        q = q_ref[at, :] * scale
        do = do_ref[at, :]
        ok = allowed_block(segk_ref, segq_ref[j], posq_ref[j], chunk, width)
        parts = []
        for h in range(2):
            mine = head_lanes(rows, h)
            q_h = jnp.where(mine, q, jnp.zeros_like(q))
            do_h = jnp.where(mine, do, jnp.zeros_like(do))
            p = jnp.exp(jnp.where(ok, dot_t(k, q_h) - lse_ref[0, j, h : h + 1], NEG))
            ds = (p * (dot_t(v, do_h) - delta_ref[j, h : h + 1])).astype(bf)
            dv = dv + dot_n(p.astype(bf), do_h)
            dk = dk + dot_n(ds, q_h)
            parts.append(dot_c(ds, k))
        acc_ref[at, :] = acc_ref[at, :] + jnp.where(head_lanes(rows, 0), parts[0], parts[1])
        return dk, dv

    zero = jnp.zeros((width, LANES), f32)
    dk, dv = lax.fori_loop(chunk // tile, nq, step, (zero, zero))
    dkv_ref[:, 0, 0] = dk.astype(bf).reshape(nu, tok, LANES)
    dkv_ref[:, 1, 0] = dv.astype(bf).reshape(nu, tok, LANES)

    @pl.when(chunk == pl.num_programs(1) - 1)
    def _():
        dq = acc_ref[...] * (1.0 / math.sqrt(HD))
        lane = lax.broadcasted_iota(jnp.int32, dq.shape, 1)
        other = jnp.where(
            lane % HD < HD // 2,
            pltpu.roll(dq, LANES - HD // 2, 1),
            pltpu.roll(dq, HD // 2, 1),
        )
        dq_ref[...] = (dq * cos_ref[...] - other * sin_ref[...]).astype(bf)


def attend_back(segments, seg_q, pos_q, cosine, sine, q, do, o, lse, k, v, tile):
    nu, nb, tok, feats = k.shape
    rows = tile * tok
    nq = nb // tile
    pairs = feats // LANES
    whole_rows = pl.BlockSpec((nq, 1, rows), lambda p, c: (0, 0, 0))
    table = pl.BlockSpec((nb * tok, LANES), lambda p, c: (0, 0))
    q_spec = pl.BlockSpec((nb * tok, LANES), lambda p, c: (0, p))
    kv_spec = pl.BlockSpec((nu, 1, tok, LANES), lambda p, c: (0, c, 0, p))
    return pl.pallas_call(
        functools.partial(attend_back_kernel, tile),
        grid=(pairs, nb),
        in_specs=[
            pl.BlockSpec((nu * nb * tok, 1), lambda p, c: (0, 0)),
            whole_rows,
            whole_rows,
            table,
            table,
            q_spec,
            q_spec,
            q_spec,
            pl.BlockSpec((1, nq, 2, rows), lambda p, c: (p, 0, 0, 0)),
            kv_spec,
            kv_spec,
        ],
        out_specs=[
            q_spec,
            pl.BlockSpec((nu, 2, 1, tok, LANES), lambda p, c: (0, 0, c, 0, p)),
        ],
        out_shape=[
            jax.ShapeDtypeStruct((nb * tok, feats), bf),
            jax.ShapeDtypeStruct((nu, 2, nb, tok, feats), bf),
        ],
        scratch_shapes=[pltpu.VMEM((nb * tok, LANES), f32), pltpu.VMEM((nq, 8, rows), f32)],
        compiler_params=pltpu.CompilerParams(vmem_limit_bytes=48 * 2**20),
        name="attend_back",
    )(segments, seg_q, pos_q, cosine, sine, q, do, o, lse, k, v)


def to_group(parts, strided):
    n, feats_u, rows = parts.shape
    nb, nu = lax.axis_size("blk"), lax.axis_size("uly")
    group = feats_u * nu // nb
    if strided:
        piece = feats_u // nb
        sent = jnp.transpose(parts.reshape(n, nb, piece, rows), (1, 0, 2, 3))
        got = gather(swap(sent, "blk")[None], "uly")
        return jnp.transpose(got, (2, 0, 3, 1, 4)).reshape(n, group, nb * rows)
    full = gather(parts[None], "uly")
    sent = jnp.transpose(full, (0, 2, 1, 3)).reshape(nb, group, n, rows)
    return jnp.transpose(swap(sent, "blk"), (2, 1, 0, 3)).reshape(n, group, nb * rows)


def from_group(grads, strided):
    n, group, all_rows = grads.shape
    nb, nu = lax.axis_size("blk"), lax.axis_size("uly")
    rows = all_rows // nb
    feats_u = group * nb // nu
    if strided:
        piece = group // nu
        mine = scatter(
            jnp.transpose(grads.reshape(n, nu, piece, nb, rows), (1, 3, 0, 2, 4)), "uly"
        )
        got = swap(mine[0], "blk")
        return jnp.transpose(got, (1, 0, 2, 3)).reshape(n, feats_u, rows)
    got = swap(jnp.transpose(grads.reshape(n, group, nb, rows), (2, 1, 0, 3)), "blk")
    mine = scatter(got.reshape(nu, feats_u, n, rows), "uly")
    return jnp.transpose(mine[0], (1, 0, 2))


def on_device(
    tokens,
    segments,
    cotangent,
    attn_gain,
    w_query,
    w_key,
    w_value,
    w_output,
    mlp_gain,
    w_gate,
    w_up,
    w_down,
):
    nb, nu = lax.axis_size("blk"), lax.axis_size("uly")
    b, u = lax.axis_index("blk"), lax.axis_index("uly")
    tok, dim = tokens.shape
    seq = segments.shape[0]
    rows = w_query.shape[0]
    feats_u = w_query.shape[1]
    heads_u = feats_u // HD
    strided = heads_u % nb == 0
    group = feats_u * nu // nb
    padded = -(-group // LANES) * LANES
    count = nb * tok
    tile = 2 if nb % 2 == 0 else 1
    both = ("blk", "uly")

    x_all = gather(tokens, "blk")
    flipped = [jnp.transpose(w.astype(bf)) for w in (w_query, w_key, w_value, w_output)]
    w_qkv = to_group(jnp.stack(flipped[:3]), strided).reshape(3 * group, dim)
    gains = gather(jnp.stack([attn_gain, mlp_gain]).astype(bf)[None], "blk")
    gain1, gain2 = [
        jnp.transpose(gains, (1, 0, 2)).reshape(2, dim)[i].astype(f32) for i in range(2)
    ]
    w_out = gather(flipped[3][None], both).reshape(nb, nu, feats_u, rows)
    if strided:
        piece = feats_u // nb
        w_out = jnp.transpose(
            w_out.reshape(nb, nu, nb, piece, rows), (2, 1, 3, 0, 4)
        ).reshape(dim, dim)
    else:
        w_out = jnp.transpose(w_out, (1, 2, 0, 3)).reshape(dim, dim)
    cot_all = gather(cotangent, "blk")
    ff_u = w_gate.shape[1]
    ff_piece = ff_u // nb
    hidden = ff_piece * nu
    w_ff = jnp.stack([w.astype(bf) for w in (w_gate, w_up, w_down)])
    w_ff = jnp.transpose(w_ff.reshape(3, rows, nb, ff_piece), (2, 0, 1, 3))
    w_ff = gather(swap(w_ff, "blk")[None], "uly")
    w_ff = jnp.transpose(w_ff, (2, 1, 3, 0, 4)).reshape(3, dim, hidden)

    seg_mine = lax.dynamic_index_in_dim(segments.reshape(nb, nu, tok), u, 1, False).reshape(count)
    index = (
        jnp.arange(nb, dtype=jnp.int32)[:, None] * (nu * tok)
        + u * tok
        + jnp.arange(tok, dtype=jnp.int32)[None, :]
    ).reshape(count)
    first = jnp.sum((segments[None, :] < seg_mine[:, None]).astype(jnp.int32), axis=1)
    lane = jnp.arange(LANES, dtype=jnp.int32)
    freq = theta_base ** (-((lane % (HD // 2)).astype(f32) * 2.0) / HD)
    angles = (index - first).astype(f32)[:, None] * freq[None, :]
    cosine = jnp.cos(angles)
    sine = jnp.sin(angles) * jnp.where(lane % HD < HD // 2, -1.0, 1.0)[None, :]
    feat = jnp.arange(padded, dtype=jnp.int32)
    partner = jnp.where(feat % HD < HD // 2, feat + HD // 2, feat - HD // 2)
    turn = (feat[:, None] == partner[None, :]).astype(bf)
    cos_wide = jnp.tile(cosine, (1, padded // LANES))
    sin_wide = jnp.tile(sine, (1, padded // LANES))
    seg_col = segments[:, None]
    seg_rows = seg_mine.reshape(nb // tile, 1, tile * tok)
    pos_rows = index.reshape(nb // tile, 1, tile * tok)

    x = x_all.astype(f32)
    r1 = rms_scale(x)
    normed = (x * r1 * gain1).astype(bf)
    qkv = dot_t(normed, w_qkv).astype(bf)

    def part(i):
        return jnp.pad(qkv[:, i * group : (i + 1) * group], ((0, 0), (0, padded - group)))

    def rotate(value):
        return (value.astype(f32) * cos_wide + dot_n(value, turn) * sin_wide).astype(bf)

    q_rot, k_rot = rotate(part(0)), rotate(part(1))
    keys = gather(k_rot.reshape(1, nb, tok, padded), "uly")
    values = gather(part(2).reshape(1, nb, tok, padded), "uly")
    o, lse = attend(seg_col, seg_rows, pos_rows, q_rot, keys, values, tile)
    o_all = gather(o[:, :group][None], "blk")
    o_wide = jnp.transpose(o_all, (1, 0, 2)).reshape(count, dim)
    x1 = x + dot_n(o_wide, w_out)

    r2 = rms_scale(x1)
    normed2 = (x1 * r2 * gain2).astype(bf)
    gate = dot_n(normed2, w_ff[0])
    up = dot_n(normed2, w_ff[1])
    sigma = jax.nn.sigmoid(gate)
    silu_gate = gate * sigma
    act = (silu_gate * up).astype(bf)
    d_act = dot_n(cot_all, w_ff[2])
    d_gate = (d_act * up * (sigma * (1.0 + gate * (1.0 - sigma)))).astype(bf)
    d_up = (d_act * silu_gate).astype(bf)
    d_norm2 = scatter(
        (dot_t(d_gate, w_ff[0]) + dot_t(d_up, w_ff[1])).astype(bf), "blk"
    ).astype(f32)
    mlp_out = scatter(dot_t(act, w_ff[2]).astype(bf), "blk").astype(f32)
    x1_own = lax.dynamic_slice_in_dim(x1, b * tok, tok, 0)
    output = x1_own + mlp_out

    ff_grads = jnp.stack([dot_c(normed2, d_gate), dot_c(normed2, d_up), dot_c(cot_all, act)])
    ff_grads = jnp.transpose(
        ff_grads.astype(bf).reshape(3, nb, rows, nu, ff_piece), (3, 1, 0, 2, 4)
    )
    ff_grads = swap(scatter(ff_grads, "uly")[0], "blk")
    ff_grads = jnp.transpose(ff_grads, (1, 2, 0, 3)).reshape(3, rows, ff_u).astype(f32)

    r2_own = rms_scale(x1_own)
    gain2_part = jnp.sum(d_norm2 * x1_own * r2_own, axis=0)
    z_two = gain2 * d_norm2
    dx1 = (
        cotangent.astype(f32)
        + r2_own * z_two
        - x1_own * r2_own * r2_own * r2_own * jnp.mean(z_two * x1_own, axis=-1, keepdims=True)
    )
    d_attn = dx1.astype(bf)
    d_o = dot_t(d_attn, w_out).astype(bf)
    d_o = swap(jnp.transpose(d_o.reshape(tok, nb, group), (1, 0, 2)), "blk").reshape(count, group)
    d_o = jnp.pad(d_o, ((0, 0), (0, padded - group)))
    d_attn_all = gather(d_attn, "blk")
    dq, dkv = attend_back(
        seg_col, seg_rows, pos_rows, cosine, sine, q_rot, d_o, o, lse, keys, values, tile
    )
    dkv = scatter(dkv, "uly")[0]
    dk = dkv[0].reshape(count, padded)
    dv = dkv[1].reshape(count, padded)
    dk = (dk.astype(f32) * cos_wide - dot_n(dk, turn) * sin_wide).astype(bf)
    dqkv = jnp.concatenate([dq[:, :group], dk[:, :group], dv[:, :group]], axis=1)
    d_norm1_part = dot_n(dqkv, w_qkv)
    gain1_part = jnp.sum(d_norm1_part * x * r1, axis=0)
    d_norm1 = scatter(d_norm1_part.astype(bf), "blk").astype(f32)
    x_own = tokens.astype(f32)
    r1_own = rms_scale(x_own)
    z_one = gain1 * d_norm1
    grad_tokens = (
        dx1
        + r1_own * z_one
        - x_own * r1_own * r1_own * r1_own * jnp.mean(z_one * x_own, axis=-1, keepdims=True)
    )
    attn_grads = jnp.concatenate(
        [
            dot_c(dqkv, normed).astype(bf).reshape(3, group, dim),
            dot_c(o[:, :group], d_attn_all).astype(bf)[None],
        ]
    )
    attn_grads = jnp.transpose(from_group(attn_grads, strided), (0, 2, 1)).astype(f32)
    gain_sums = lax.psum(jnp.stack([gain1_part, gain2_part]), both)
    gain_own = lax.dynamic_slice_in_dim(gain_sums, b * rows, rows, 1)
    return (
        output,
        grad_tokens,
        gain_own[0],
        attn_grads[0],
        attn_grads[1],
        attn_grads[2],
        attn_grads[3],
        gain_own[1],
        ff_grads[0],
        ff_grads[1],
        ff_grads[2],
    )


def solution(mesh):
    tokens_split = P(("blk", "uly"), None)
    weights = P("blk", "uly")
    return jax.shard_map(
        on_device,
        mesh=mesh,
        in_specs=(
            tokens_split,
            P(),
            tokens_split,
            P("blk"),
            weights,
            weights,
            weights,
            weights,
            P("blk"),
            weights,
            weights,
            weights,
        ),
        out_specs=(
            tokens_split,
            tokens_split,
            P("blk"),
            weights,
            weights,
            weights,
            weights,
            P("blk"),
            weights,
            weights,
            weights,
        ),
        check_vma=False,
    )
```

```python
import functools
import math

import jax
import jax.numpy as jnp
from jax import lax
from jax.experimental import pallas as pl
from jax.experimental.pallas import tpu as pltpu
from jax.sharding import PartitionSpec as P

H = 32
HD = 64
LANES = 128
PAD = 16

theta_base = 130000.0
epsilon = 1e-05
bf = jnp.bfloat16
f32 = jnp.float32
NEG = -1e30


def dot_t(left, right):
    return lax.dot_general(left, right, (((1,), (1,)), ((), ())), preferred_element_type=f32)


def dot_n(left, right):
    return jnp.dot(left, right, preferred_element_type=f32)


def dot_c(left, right):
    return lax.dot_general(left, right, (((0,), (0,)), ((), ())), preferred_element_type=f32)


def rms_scale(value):
    return lax.rsqrt(jnp.mean(value * value, axis=-1, keepdims=True) + epsilon)


def params(mib=56):
    return pltpu.CompilerParams(vmem_limit_bytes=mib * 2**20)


def cost(micros):
    return pl.CostEstimate(flops=int(micros * 0.25 * 1.1e9), bytes_accessed=0, transcendentals=0)


def full(shape):
    return pl.BlockSpec(shape, lambda *grid: (0,) * len(shape))


def after(value, *others):
    return lax.optimization_barrier((value, *others))[0]


def hop(value, axis, slow, fast):
    size = lax.axis_size(axis)
    ring = size // 2
    pairs = [(i, ((i // 2 + slow) % ring) * 2 + (i % 2 ^ fast)) for i in range(size)]
    return lax.ppermute(value, axis, pairs)


def near(axis, slow, fast):
    ring = lax.axis_size(axis) // 2
    i = lax.axis_index(axis)
    return ((i // 2 + slow + ring) % ring) * 2 + (i % 2 ^ fast)


def place(out, piece, at):
    return lax.dynamic_update_slice_in_dim(out, piece[None], at, 0)


def pick(parts, at):
    return lax.dynamic_index_in_dim(parts, at, 0, False)


def together(*plans):
    results = [None] * len(plans)
    sent = {i: None for i in range(len(plans))}
    while sent:
        waiting = {}
        for i, value in sent.items():
            try:
                waiting[i] = list(plans[i].send(value))
            except StopIteration as end:
                results[i] = end.value
        flat = [v for values in waiting.values() for v in values]
        if flat:
            flat = list(lax.optimization_barrier(tuple(flat)))
        sent = {}
        for i, values in waiting.items():
            sent[i] = [flat.pop(0) for _ in values]
    return results


def chain(first, *rest):
    value = yield from first
    for plan in rest:
        value = yield from plan(value)
    return value


def gather_plan(value, axis):
    size = lax.axis_size(axis)
    ring = size // 2
    out = jnp.zeros((size, *value.shape), value.dtype)
    fresh = {0: value}
    crossed = {}
    for s in range(1, ring // 2 + 2):
        for at, piece in fresh.items():
            out = place(out, piece, near(axis, at, 0))
            crossed[at] = hop(piece, axis, 0, 1)
        arriving = {}
        if s <= ring // 2:
            arriving[-s] = hop(fresh[1 - s], axis, 1, 0)
        if s <= (ring - 1) // 2:
            arriving[s] = hop(fresh[s - 1], axis, -1, 0)
        if arriving:
            fresh = dict(zip(arriving, (yield list(arriving.values()))))
    landed = dict(zip(crossed, (yield list(crossed.values()))))
    for at, piece in landed.items():
        out = place(out, piece, near(axis, at, 1))
    return out


def scatter_plan(parts, axis):
    ring = lax.axis_size(axis) // 2
    far, back = ring // 2, (ring - 1) // 2
    order = []
    for s in range(far, 0, -1):
        order.append((s, 1))
        if s <= back:
            order.append((s, -1))
    crossing = {
        s * way: hop(pick(parts, near(axis, s * way, 1)), axis, 0, 1) for s, way in order
    }
    crossing[0] = hop(pick(parts, near(axis, 0, 1)), axis, 0, 1)
    carried = {1: None, -1: None}
    for s, way in order:
        wait = [crossing[s * way]] + ([] if carried[way] is None else [carried[way]])
        total = pick(parts, near(axis, s * way, 0)).astype(f32)
        for piece in (yield wait):
            total = total + piece.astype(f32)
        carried[way] = hop(total.astype(bf), axis, way, 0)
    total = pick(parts, near(axis, 0, 0)).astype(f32)
    for piece in (yield [crossing[0]] + [v for v in carried.values() if v is not None]):
        total = total + piece.astype(f32)
    return total


def swap_plan(parts, axis):
    ring = lax.axis_size(axis) // 2
    fast = lax.axis_index(axis) % 2
    slow = lax.axis_index(axis) // 2
    columns = jnp.swapaxes(parts.reshape(ring, 2, *parts.shape[1:]), 0, 1)
    kept = pick(columns, fast)
    (given,) = yield [hop(pick(columns, 1 - fast), axis, 0, 1)]
    pairs = jnp.stack([jnp.where(fast == 0, kept, given), jnp.where(fast == 0, given, kept)], 1)
    out = place(jnp.zeros_like(pairs), pick(pairs, slow), slow)
    arrived = yield [hop(pick(pairs, (slow + s) % ring), axis, s, 0) for s in range(1, ring)]
    for s, piece in enumerate(arrived, 1):
        out = place(out, piece, (slow - s + ring) % ring)
    return out.reshape(parts.shape)


def exchange(part, axis):
    got, places = [], []
    for slow in range(lax.axis_size(axis) // 2):
        for fast in range(2):
            piece = part(near(axis, slow, fast))
            got.append(hop(piece, axis, slow, fast) if slow or fast else piece)
            places.append(near(axis, -slow, fast))
    return got, places


def gather_near_plan(value, axis, spare=0):
    ring = lax.axis_size(axis) // 2
    crossed = [hop(value, axis, 0, 1)]
    got = [hop(value, axis, s, 0) for s in range(1, ring)]
    for _ in range(spare):
        yield []
    got = yield got
    crossed += [hop(piece, axis, 0, 1) for piece in got]
    crossed = yield crossed
    return [value, *got, *crossed]


def scatter_near_plan(parts, axis):
    ring = lax.axis_size(axis) // 2
    crossed = yield [hop(part, axis, 0, 1) for part in parts[ring:]]
    sums = [mine.astype(f32) + piece.astype(f32) for mine, piece in zip(parts, crossed)]
    total = sums[0]
    for piece in (yield [hop(sums[s].astype(bf), axis, -s, 0) for s in range(1, ring)]):
        total = total + piece.astype(f32)
    return total.astype(bf)


def gather(value, axis):
    return lax.all_gather(value, axis, axis=0, tiled=True)


def scatter(value, axis):
    return lax.psum_scatter(value, axis, scatter_dimension=0, tiled=True)


def turned(value):
    width = value.shape[1]
    lane = lax.broadcasted_iota(jnp.int32, value.shape, 1)
    return jnp.where(
        lane % HD < HD // 2,
        pltpu.roll(value, width - HD // 2, 1),
        pltpu.roll(value, HD // 2, 1),
    )


def wide(table, width):
    return jnp.concatenate([table] * (width // LANES), axis=1)


def weight_block(w_ref, block, part, piece):
    w = w_ref[:, block, part * piece : (part + 1) * piece, :]
    return w.reshape(w.shape[0] * piece, w.shape[2])


def project_kernel(piece, x_ref, w_ref, cos_ref, sin_ref, q_ref, kv_ref, normed_ref):
    blocks, width = w_ref.shape[1], w_ref.shape[3]
    x = x_ref[...].astype(f32)
    r1 = rms_scale(x)
    total = [0.0, 0.0, 0.0]
    for block in range(blocks):
        at = slice(block * width, (block + 1) * width)
        gain = w_ref[0, block, 3 * piece : 3 * piece + PAD, :][0:1].astype(f32)
        normed = (x[:, at] * r1 * gain).astype(bf)
        normed_ref[:, at] = normed
        for part in range(3):
            total[part] = total[part] + dot_t(normed, weight_block(w_ref, block, part, piece))
    feats = total[0].shape[1]
    cosine, sine = wide(cos_ref[...], feats), wide(sin_ref[...], feats)

    def rotate(value):
        value = value.astype(bf).astype(f32)
        return (value * cosine + turned(value) * sine).astype(bf)

    q_ref[...] = rotate(total[0])
    kv_ref[0] = rotate(total[1])
    kv_ref[1] = total[2].astype(bf)


def project(x_all, w, cosine, sine, piece, rows):
    count, dim = x_all.shape
    feats = w.shape[0] * piece
    tiled = lambda n: pl.BlockSpec((rows, n), lambda i: (i, 0))
    return pl.pallas_call(
        functools.partial(project_kernel, piece),
        grid=(count // rows,),
        in_specs=[tiled(dim), full(w.shape), tiled(LANES), tiled(LANES)],
        out_specs=[
            tiled(feats),
            pl.BlockSpec((2, rows, feats), lambda i: (0, i, 0)),
            tiled(dim),
        ],
        out_shape=[
            jax.ShapeDtypeStruct((count, feats), bf),
            jax.ShapeDtypeStruct((2, count, feats), bf),
            jax.ShapeDtypeStruct((count, dim), bf),
        ],
        compiler_params=params(),
        cost_estimate=cost(count * 0.009),
        name="project",
    )(x_all, w, cosine, sine)


def flip_kernel(piece, q_ref, k_ref, v_ref, o_ref, ga_ref, gm_ref, sent_ref, out_ref):
    size = sent_ref.shape[0]
    for i, ref in enumerate((q_ref, k_ref, v_ref)):
        sent_ref[:, i * piece : (i + 1) * piece, :] = (
            ref[...].T.astype(bf).reshape(size, piece, ref.shape[0])
        )
    row = lax.broadcasted_iota(jnp.int32, (PAD, q_ref.shape[0]), 0)
    gains = jnp.where(row == 0, ga_ref[...], gm_ref[...]).astype(bf)
    for j in range(size):
        sent_ref[j, 3 * piece :, :] = gains
    out_ref[...] = o_ref[...].T.astype(bf)


def flip(w_query, w_key, w_value, w_output, attn_gain, mlp_gain, size):
    rows, feats = w_query.shape
    piece = feats // size
    return pl.pallas_call(
        functools.partial(flip_kernel, piece),
        out_shape=[
            jax.ShapeDtypeStruct((size, 3 * piece + PAD, rows), bf),
            jax.ShapeDtypeStruct((feats, rows), bf),
        ],
        compiler_params=params(),
        cost_estimate=cost(5),
        name="flip",
    )(w_query, w_key, w_value, w_output, attn_gain[None], mlp_gain[None])


def allowed_block(segk_ref, seg_q, pos_q, chunk, width):
    seg_k = segk_ref[pl.ds(pl.multiple_of(chunk * width, width), width), :]
    pos_k = chunk * width + lax.broadcasted_iota(jnp.int32, (width, 1), 0)
    return (seg_k == seg_q) & (pos_k <= pos_q)


def head_lanes(rows, head):
    lane = lax.broadcasted_iota(jnp.int32, (rows, LANES), 1)
    return (lane < HD) if head == 0 else (lane >= HD)


def attend_kernel(tile, segk_ref, segq_ref, posq_ref, q_ref, kv_ref, o_ref, lse_ref, vt_ref):
    nu, _, nb, tok, _ = kv_ref.shape
    width = nu * tok
    rows = tile * tok
    j = pl.program_id(1)

    @pl.when(j == 0)
    def _():
        for c in range(nb):
            vt_ref[c] = kv_ref[:, 1, c].reshape(width, LANES).T

    seg_q, pos_q = segq_ref[0], posq_ref[0]
    q = q_ref[...] * jnp.asarray(1.0 / math.sqrt(HD), bf)
    q_heads = [jnp.where(head_lanes(rows, h), q, jnp.zeros_like(q)) for h in range(2)]

    def step(chunk, state):
        k = kv_ref[:, 0, chunk].reshape(width, LANES)
        v_t = vt_ref[chunk]
        ok = allowed_block(segk_ref, seg_q, pos_q, chunk, width)
        new = []
        for h in range(2):
            best, total, acc = state[h]
            s = jnp.where(ok, dot_t(k, q_heads[h]), NEG)
            best_new = jnp.maximum(best, jnp.max(s, axis=0, keepdims=True))
            p = jnp.exp(s - best_new)
            factor = jnp.exp(best - best_new)
            total = total * factor + jnp.sum(p, axis=0, keepdims=True)
            acc = acc * factor + dot_n(v_t[h * HD : (h + 1) * HD], p.astype(bf))
            new.append((best_new, total, acc))
        return tuple(new)

    start = (
        jnp.full((1, rows), NEG, f32),
        jnp.zeros((1, rows), f32),
        jnp.zeros((HD, rows), f32),
    )
    state = lax.fori_loop(0, (j + 1) * tile, step, (start, start))
    o_t = jnp.concatenate([acc / total for _, total, acc in state], axis=0)
    o_ref[...] = o_t.T.astype(bf)
    lse_ref[0, 0] = jnp.concatenate([best + jnp.log(total) for best, total, _ in state], axis=0)


def attend(segments, seg_q, pos_q, q, kv, tile):
    nu, _, nb, tok, feats = kv.shape
    rows = tile * tok
    nq = nb // tile
    pairs = feats // LANES
    row_spec = pl.BlockSpec((1, 1, rows), lambda p, j: (j, 0, 0))
    q_spec = pl.BlockSpec((rows, LANES), lambda p, j: (j, p))
    return pl.pallas_call(
        functools.partial(attend_kernel, tile),
        grid=(pairs, nq),
        in_specs=[
            full(segments.shape),
            row_spec,
            row_spec,
            q_spec,
            pl.BlockSpec((nu, 2, nb, tok, LANES), lambda p, j: (0, 0, 0, 0, p)),
        ],
        out_specs=[q_spec, pl.BlockSpec((1, 1, 2, rows), lambda p, j: (p, j, 0, 0))],
        out_shape=[
            jax.ShapeDtypeStruct((nb * tok, feats), bf),
            jax.ShapeDtypeStruct((pairs, nq, 2, rows), f32),
        ],
        scratch_shapes=[pltpu.VMEM((nb, LANES, nu * tok), bf)],
        compiler_params=params(),
        cost_estimate=cost(44 * nb * tok * nb / 8192),
        name="attend",
    )(segments, seg_q, pos_q, q, kv)


def attend_back_kernel(
    tile,
    segk_ref,
    segq_ref,
    posq_ref,
    cos_ref,
    sin_ref,
    q_ref,
    do_ref,
    o_ref,
    lse_ref,
    kv_ref,
    dq_ref,
    dkv_ref,
    acc_ref,
    delta_ref,
):
    nu, _, _, tok, _ = kv_ref.shape
    nq = segq_ref.shape[0]
    width = nu * tok
    rows = tile * tok
    chunk = pl.program_id(1)
    scale = jnp.asarray(1.0 / math.sqrt(HD), bf)

    @pl.when(chunk == 0)
    def _():
        acc_ref[...] = jnp.zeros_like(acc_ref)
        lane = lax.broadcasted_iota(jnp.int32, (8, LANES), 1)
        row = lax.broadcasted_iota(jnp.int32, (8, LANES), 0)
        mine = jnp.where(lane // HD == row, 1.0, 0.0).astype(f32)
        for j in range(nq):
            part = do_ref[pl.ds(j * rows, rows), :].astype(f32) * o_ref[
                pl.ds(j * rows, rows), :
            ].astype(f32)
            delta_ref[j] = lax.dot_general(
                mine,
                part,
                (((1,), (1,)), ((), ())),
                preferred_element_type=f32,
                precision=lax.Precision.HIGHEST,
            )

    k = kv_ref[:, 0, 0].reshape(width, LANES)
    v = kv_ref[:, 1, 0].reshape(width, LANES)

    def step(j, state):
        dk, dv = state
        at = pl.ds(pl.multiple_of(j * rows, rows), rows)
        q = q_ref[at, :] * scale
        do = do_ref[at, :]
        ok = allowed_block(segk_ref, segq_ref[j], posq_ref[j], chunk, width)
        parts = []
        for h in range(2):
            mine = head_lanes(rows, h)
            q_h = jnp.where(mine, q, jnp.zeros_like(q))
            do_h = jnp.where(mine, do, jnp.zeros_like(do))
            p = jnp.exp(jnp.where(ok, dot_t(k, q_h) - lse_ref[0, j, h : h + 1], NEG))
            ds = (p * (dot_t(v, do_h) - delta_ref[j, h : h + 1])).astype(bf)
            dv = dv + dot_n(p.astype(bf), do_h)
            dk = dk + dot_n(ds, q_h)
            parts.append(dot_c(ds, k))
        acc_ref[at, :] = acc_ref[at, :] + jnp.where(head_lanes(rows, 0), parts[0], parts[1])
        return dk, dv

    zero = jnp.zeros((width, LANES), f32)
    dk, dv = lax.fori_loop(chunk // tile, nq, step, (zero, zero))
    dkv_ref[:, 0, 0] = dk.astype(bf).reshape(nu, tok, LANES)
    dkv_ref[:, 1, 0] = dv.astype(bf).reshape(nu, tok, LANES)

    @pl.when(chunk == pl.num_programs(1) - 1)
    def _():
        dq = acc_ref[...] * (1.0 / math.sqrt(HD))
        dq_ref[...] = (dq * cos_ref[...] - turned(dq) * sin_ref[...]).astype(bf)


def attend_back(segments, seg_q, pos_q, cosine, sine, q, do, o, lse, kv, tile):
    nu, _, nb, tok, feats = kv.shape
    rows = tile * tok
    nq = nb // tile
    pairs = feats // LANES
    whole_rows = full((nq, 1, rows))
    table = full((nb * tok, LANES))
    q_spec = pl.BlockSpec((nb * tok, LANES), lambda p, c: (0, p))
    kv_spec = pl.BlockSpec((nu, 2, 1, tok, LANES), lambda p, c: (0, 0, c, 0, p))
    return pl.pallas_call(
        functools.partial(attend_back_kernel, tile),
        grid=(pairs, nb),
        in_specs=[
            full(segments.shape),
            whole_rows,
            whole_rows,
            table,
            table,
            q_spec,
            q_spec,
            q_spec,
            pl.BlockSpec((1, nq, 2, rows), lambda p, c: (p, 0, 0, 0)),
            kv_spec,
        ],
        out_specs=[q_spec, kv_spec],
        out_shape=[
            jax.ShapeDtypeStruct((nb * tok, feats), bf),
            jax.ShapeDtypeStruct((nu, 2, nb, tok, feats), bf),
        ],
        scratch_shapes=[pltpu.VMEM((nb * tok, LANES), f32), pltpu.VMEM((nq, 8, rows), f32)],
        compiler_params=params(),
        cost_estimate=cost(50 * nb * tok * nb / 8192),
        name="attend_back",
    )(segments, seg_q, pos_q, cosine, sine, q, do, o, lse, kv)


def output_kernel(x_ref, o_ref, w_ref, gain_ref, x1_ref, normed_ref):
    blocks, pieces, groups, piece, width = w_ref.shape
    square = 0.0
    for block in range(blocks):
        at = slice(block * width, (block + 1) * width)
        total = x_ref[:, at].astype(f32)
        for g in range(groups):
            total = total + dot_n(o_ref[g], w_ref[block, :, g].reshape(pieces * piece, width))
        x1_ref[:, at] = total
        square = square + jnp.sum(total * total, axis=1, keepdims=True)
    r2 = lax.rsqrt(square * (1.0 / (blocks * width)) + epsilon)
    normed_ref[...] = (x1_ref[...] * r2 * gain_ref[...]).astype(bf)


def output_project(x_all, o_all, w_out, gain, rows):
    count, dim = x_all.shape
    groups, _, feats = o_all.shape
    tiled = pl.BlockSpec((rows, dim), lambda i: (i, 0))
    return pl.pallas_call(
        output_kernel,
        grid=(count // rows,),
        in_specs=[
            tiled,
            pl.BlockSpec((groups, rows, feats), lambda i: (0, i, 0)),
            full(w_out.shape),
            full(gain.shape),
        ],
        out_specs=[tiled, tiled],
        out_shape=[
            jax.ShapeDtypeStruct((count, dim), f32),
            jax.ShapeDtypeStruct((count, dim), bf),
        ],
        compiler_params=params(),
        cost_estimate=cost(count * 0.015),
        name="output_project",
    )(x_all, o_all, w_out, gain)


def output_back_kernel(d_ref, w_ref, out_ref):
    blocks, pieces, _, piece, width = w_ref.shape
    total = 0.0
    for block in range(blocks):
        at = slice(block * width, (block + 1) * width)
        total = total + dot_t(d_ref[:, at], w_ref[block, :, 0].reshape(pieces * piece, width))
    out_ref[0] = total.astype(bf)


def output_back(d_attn, w_out):
    tok, dim = d_attn.shape
    blocks, pieces, groups, piece, width = w_out.shape
    return pl.pallas_call(
        output_back_kernel,
        grid=(groups,),
        in_specs=[
            full(d_attn.shape),
            pl.BlockSpec((blocks, pieces, 1, piece, width), lambda g: (0, 0, g, 0, 0)),
        ],
        out_specs=pl.BlockSpec((1, tok, pieces * piece), lambda g: (g, 0, 0)),
        out_shape=jax.ShapeDtypeStruct((groups, tok, pieces * piece), bf),
        compiler_params=params(),
        cost_estimate=cost(8),
        name="output_back",
    )(d_attn, w_out)


def project_back_kernel(
    piece, x_ref, w_ref, cos_ref, sin_ref, dq_ref, dkv_ref, dk_ref, dn_ref, gain_ref
):
    blocks, width = w_ref.shape[1], w_ref.shape[3]
    feats = dq_ref.shape[1]
    cosine, sine = wide(cos_ref[...], feats), wide(sin_ref[...], feats)
    dk = dkv_ref[0].astype(f32)
    dk = (dk * cosine - turned(dk) * sine).astype(bf)
    dk_ref[...] = dk
    x = x_ref[...].astype(f32)
    r1 = rms_scale(x)
    parts = (dq_ref[...], dk, dkv_ref[1])

    @pl.when(pl.program_id(0) == 0)
    def _():
        gain_ref[...] = jnp.zeros_like(gain_ref)

    for block in range(blocks):
        at = slice(block * width, (block + 1) * width)
        total = 0.0
        for part in range(3):
            total = total + dot_n(parts[part], weight_block(w_ref, block, part, piece))
        dn_ref[:, at] = total.astype(bf)
        gain_ref[:, at] = gain_ref[:, at] + jnp.sum(total * (x[:, at] * r1), axis=0, keepdims=True)


def project_back(x_all, w, cosine, sine, dq, dkv, piece, rows):
    count, dim = x_all.shape
    feats = dq.shape[1]
    tiled = lambda n: pl.BlockSpec((rows, n), lambda i: (i, 0))
    return pl.pallas_call(
        functools.partial(project_back_kernel, piece),
        grid=(count // rows,),
        in_specs=[
            tiled(dim),
            full(w.shape),
            tiled(LANES),
            tiled(LANES),
            tiled(feats),
            pl.BlockSpec((2, rows, feats), lambda i: (0, i, 0)),
        ],
        out_specs=[tiled(feats), tiled(dim), full((1, dim))],
        out_shape=[
            jax.ShapeDtypeStruct((count, feats), bf),
            jax.ShapeDtypeStruct((count, dim), bf),
            jax.ShapeDtypeStruct((1, dim), f32),
        ],
        compiler_params=params(),
        cost_estimate=cost(count * 0.01),
        name="project_back",
    )(x_all, w, cosine, sine, dq, dkv)


def projection_grads_kernel(pieces, n, *refs):
    lefts, (right_ref, gain_ref, out_ref, turned_ref) = refs[:n], refs[n:]

    @pl.when(pl.program_id(0) == 0)
    def _():
        for i in range(n):
            turned_ref[i] = lefts[i][...].T

    feats = turned_ref.shape[1]
    piece = feats // pieces
    right = right_ref[...]
    width = right.shape[1]
    for i in range(n):
        grad = dot_n(turned_ref[i], right).astype(bf)
        out_ref[:, 0, i * piece : (i + 1) * piece, :] = grad.reshape(pieces, piece, width)
    gain = gain_ref[...].astype(bf)
    for u in range(pieces):
        out_ref[u, 0, n * piece :, :] = gain


def projection_grads(lefts, right, gain, pieces, width):
    n = len(lefts)
    count, feats = lefts[0].shape
    dim = right.shape[1]
    rows = n * (feats // pieces) + PAD
    return pl.pallas_call(
        functools.partial(projection_grads_kernel, pieces, n),
        grid=(dim // width,),
        in_specs=[full((count, feats))] * n
        + [
            pl.BlockSpec((count, width), lambda i: (0, i)),
            pl.BlockSpec((PAD, width), lambda i: (0, i)),
        ],
        out_specs=pl.BlockSpec((pieces, 1, rows, width), lambda i: (0, i, 0, 0)),
        out_shape=jax.ShapeDtypeStruct((pieces, dim // width, rows, width), bf),
        scratch_shapes=[pltpu.VMEM((n, feats, count), bf)],
        compiler_params=params(),
        cost_estimate=cost(2.5 * n),
        name="projection_grads",
    )(*lefts, right, gain)


def output_grads_kernel(o_ref, d_ref, out_ref):
    pieces, _, piece, width = out_ref.shape
    grad = dot_n(o_ref[0].T, d_ref[...])
    out_ref[:, 0] = grad.astype(bf).reshape(pieces, piece, width)


def output_grads(o_all, d_columns, pieces):
    groups, count, feats = o_all.shape
    width = d_columns.shape[1]
    shape = (pieces, groups, feats // pieces, width)
    return pl.pallas_call(
        output_grads_kernel,
        grid=(groups,),
        in_specs=[
            pl.BlockSpec((1, count, feats), lambda g: (g, 0, 0)),
            full(d_columns.shape),
        ],
        out_specs=pl.BlockSpec((pieces, 1, *shape[2:]), lambda g: (0, g, 0, 0)),
        out_shape=jax.ShapeDtypeStruct(shape, bf),
        compiler_params=params(),
        cost_estimate=cost(6),
        name="output_grads",
    )(o_all, d_columns)


def prepare_kernel(wg_ref, wu_ref, wd_ref, out_ref):
    for i, ref in enumerate((wg_ref, wu_ref, wd_ref)):
        out_ref[0, i] = ref[...].astype(bf)


def prepare(w_gate, w_up, w_down, size):
    rows, columns = w_gate.shape
    width = columns // size
    if width % LANES:
        stacked = jnp.stack([w.astype(bf) for w in (w_gate, w_up, w_down)])
        return jnp.transpose(stacked.reshape(3, rows, size, width), (2, 0, 1, 3))
    spec = pl.BlockSpec((rows, width), lambda i: (0, i))
    return pl.pallas_call(
        prepare_kernel,
        grid=(size,),
        in_specs=[spec] * 3,
        out_specs=pl.BlockSpec((1, 3, rows, width), lambda i: (i, 0, 0, 0)),
        out_shape=jax.ShapeDtypeStruct((size, 3, rows, width), bf),
        compiler_params=params(),
        cost_estimate=cost(4),
        name="prepare",
    )(w_gate, w_up, w_down)


def assemble_kernel(n, at_ref, *refs):
    rows = refs[0].shape[1]
    for k in range(n):
        at = pl.ds(pl.multiple_of(at_ref[k] * rows, rows), rows)
        refs[n][:, at, :] = refs[k][...]


def assemble(parts, places):
    n = len(parts)
    _, rows, width = parts[0].shape
    return pl.pallas_call(
        functools.partial(assemble_kernel, n),
        grid_spec=pltpu.PrefetchScalarGridSpec(
            num_scalar_prefetch=1,
            grid=(1,),
            in_specs=[full(parts[0].shape)] * n,
            out_specs=full((3, n * rows, width)),
        ),
        out_shape=jax.ShapeDtypeStruct((3, n * rows, width), bf),
        compiler_params=params(),
        cost_estimate=cost(4),
        name="assemble",
    )(jnp.stack(places).astype(jnp.int32), *parts)


def finish_kernel(n, at_ref, *refs):
    width = refs[0].shape[2]
    for k in range(n):
        at = pl.ds(pl.multiple_of(at_ref[k] * width, width), width)
        for i in range(3):
            refs[n + i][:, at] = refs[k][i].astype(f32)


def finish(parts, places):
    n = len(parts)
    _, rows, width = parts[0].shape
    if width % LANES:
        out = jnp.zeros((n, *parts[0].shape), bf)
        for part, at in zip(parts, places):
            out = place(out, part, at)
        out = jnp.transpose(out, (1, 2, 0, 3)).reshape(3, rows, n * width).astype(f32)
        return [out[i] for i in range(3)]
    return pl.pallas_call(
        functools.partial(finish_kernel, n),
        grid_spec=pltpu.PrefetchScalarGridSpec(
            num_scalar_prefetch=1,
            grid=(1,),
            in_specs=[full(parts[0].shape)] * n,
            out_specs=[full((rows, n * width))] * 3,
        ),
        out_shape=[jax.ShapeDtypeStruct((rows, n * width), f32)] * 3,
        compiler_params=params(),
        cost_estimate=cost(5),
        name="finish",
    )(jnp.stack(places).astype(jnp.int32), *parts)


def hidden_kernel(n, *refs):
    n_ref, g_ref = refs[:2]
    act_ref, dg_ref, du_ref = refs[2 + n :]
    normed, cot = n_ref[...], g_ref[...]
    for i in range(n):
        w_ref = refs[2 + i]
        gate = dot_n(normed, w_ref[0])
        up = dot_n(normed, w_ref[1])
        d_act = dot_n(cot, w_ref[2])
        sigma = jax.nn.sigmoid(gate)
        silu = gate * sigma
        act_ref[i] = (silu * up).astype(bf)
        du_ref[i] = (d_act * silu).astype(bf)
        dg_ref[i] = (d_act * up * (sigma * (1.0 + gate * (1.0 - sigma)))).astype(bf)


def hidden(normed, cot, weights, rows):
    count, dim = normed.shape
    n = len(weights)
    width = weights[0].shape[2]
    tiled = pl.BlockSpec((rows, dim), lambda i: (i, 0))
    out = pl.BlockSpec((n, rows, width), lambda i: (0, i, 0))
    return pl.pallas_call(
        functools.partial(hidden_kernel, n),
        grid=(count // rows,),
        in_specs=[tiled, tiled] + [full(w.shape) for w in weights],
        out_specs=[out] * 3,
        out_shape=[jax.ShapeDtypeStruct((n, count, width), bf)] * 3,
        compiler_params=params(),
        cost_estimate=cost(20),
        name="hidden",
    )(normed, cot, *weights)


def mix_kernel(which, n, *refs):
    lefts, weights, out_ref = refs[: len(which)], refs[len(which) : -1], refs[-1]
    total = 0.0
    for k in range(len(which)):
        for i in range(n):
            total = total + dot_t(lefts[k][i], weights[i][k])
    out_ref[...] = total.astype(bf)


def mix(lefts, weights, which, rows):
    n, count, width = lefts[0].shape
    dim = weights[0].shape[1]
    chosen = pl.BlockSpec((len(which), dim, width), lambda i: (which[0] // len(which), 0, 0))
    return pl.pallas_call(
        functools.partial(mix_kernel, which, n),
        grid=(count // rows,),
        in_specs=[pl.BlockSpec((n, rows, width), lambda i: (0, i, 0))] * len(which)
        + [chosen] * n,
        out_specs=pl.BlockSpec((rows, dim), lambda i: (i, 0)),
        out_shape=jax.ShapeDtypeStruct((count, dim), bf),
        compiler_params=params(),
        cost_estimate=cost(8 * len(which)),
        name="mix",
    )(*lefts, *weights)


def hidden_grads_kernel(n_ref, g_ref, dg_ref, du_ref, act_ref, *outs):
    normed, cot = n_ref[...].T, g_ref[...].T
    for i, out_ref in enumerate(outs):
        out_ref[0] = dot_n(normed, dg_ref[i]).astype(bf)
        out_ref[1] = dot_n(normed, du_ref[i]).astype(bf)
        out_ref[2] = dot_n(cot, act_ref[i]).astype(bf)


def hidden_grads(normed, cot, d_gate, d_up, act, block):
    count, dim = normed.shape
    n, _, width = act.shape
    columns = pl.BlockSpec((count, block), lambda i: (0, i))
    return pl.pallas_call(
        hidden_grads_kernel,
        grid=(dim // block,),
        in_specs=[columns, columns] + [full(act.shape)] * 3,
        out_specs=[pl.BlockSpec((3, block, width), lambda i: (0, i, 0))] * n,
        out_shape=[jax.ShapeDtypeStruct((3, dim, width), bf)] * n,
        compiler_params=params(),
        cost_estimate=cost(25),
        name="hidden_grads",
    )(normed, cot, d_gate, d_up, act)


def on_device(
    tokens,
    segments,
    cotangent,
    attn_gain,
    w_query,
    w_key,
    w_value,
    w_output,
    mlp_gain,
    w_gate,
    w_up,
    w_down,
):
    nb, nu = lax.axis_size("blk"), lax.axis_size("uly")
    b, u = lax.axis_index("blk"), lax.axis_index("uly")
    tok, dim = tokens.shape
    seq = segments.shape[0]
    rows, feats_u = w_query.shape
    group = feats_u * nu // nb
    strided = (feats_u // HD) % nb == 0 and rows % LANES == 0
    count = nb * tok
    tile = 2
    both = ("blk", "uly")
    block = rows if strided else 2 * LANES
    blocks = dim // block
    pieces = nu if strided else 1
    piece = group // nu if strided else -(-group // LANES) * LANES
    feats = pieces * piece
    step = 2 * tok

    seg_mine = pick(jnp.swapaxes(segments.reshape(nb, nu, tok), 0, 1), u).reshape(count)
    index = (
        jnp.arange(nb, dtype=jnp.int32)[:, None] * (nu * tok)
        + u * tok
        + jnp.arange(tok, dtype=jnp.int32)[None, :]
    ).reshape(count)
    first = jnp.sum((segments[None, :] < seg_mine[:, None]).astype(jnp.int32), axis=1)
    lane = jnp.arange(LANES, dtype=jnp.int32)
    freq = theta_base ** (-((lane % (HD // 2)).astype(f32) * 2.0) / HD)
    angles = (index - first).astype(f32)[:, None] * freq[None, :]
    cosine = jnp.cos(angles)
    sine = jnp.sin(angles) * jnp.where(lane % HD < HD // 2, -1.0, 1.0)[None, :]
    seg_col = segments[:, None]
    seg_rows = seg_mine.reshape(nb // tile, 1, tile * tok)
    pos_rows = index.reshape(nb // tile, 1, tile * tok)

    ff_u = w_gate.shape[1]
    ff_piece = ff_u // nb
    tokens_plan = gather_plan(tokens, "blk")

    def prepared():
        (value,) = yield [prepare(w_gate, w_up, w_down, nb)]
        return value

    if strided:
        sent, out_flipped = flip(w_query, w_key, w_value, w_output, attn_gain, mlp_gain, nb)
        x_all, ff_sent, w_qkv = together(
            tokens_plan,
            prepared(),
            chain(swap_plan(sent, "blk"), lambda got: gather_plan(got, "uly")),
        )
    else:
        gains = jnp.stack([attn_gain, mlp_gain]).astype(bf)
        flipped = [jnp.transpose(w.astype(bf)) for w in (w_query, w_key, w_value, w_output)]
        out_flipped = flipped[3]
        sent = gather(jnp.stack(flipped[:3])[None], "uly")
        sent = jnp.transpose(sent, (0, 2, 1, 3)).reshape(nb, group, 3, rows)
        x_all, ff_sent, got = together(tokens_plan, prepared(), swap_plan(sent, "blk"))
        got = jnp.transpose(got, (2, 1, 0, 3)).reshape(3, group, dim)
        got = jnp.pad(got, ((0, 0), (0, piece - group), (0, 0))).reshape(3 * piece, dim)
        all_gains = jnp.transpose(gather(gains[None], "blk"), (1, 0, 2)).reshape(2, dim)
        got = jnp.concatenate([got, jnp.pad(all_gains, ((0, PAD - 2), (0, 0)))])
        w_qkv = jnp.transpose(got.reshape(3 * piece + PAD, blocks, block), (1, 0, 2))[None]
    x_all = x_all.reshape(count, dim)
    gain1, gain2 = [
        w_qkv[0, :, 3 * piece + i, :].reshape(1, dim).astype(f32) for i in range(2)
    ]

    ff_sent = after(ff_sent, x_all)
    ff_got, ff_places = exchange(lambda i: pick(ff_sent, i), "blk")
    w_out = gather(after(out_flipped, x_all)[None], both)
    cot_all = gather(after(cotangent, x_all, w_out), "blk")
    if strided:
        w_out = w_out.reshape(nb, nu, nb, piece, rows)
    else:
        w_out = jnp.transpose(w_out.reshape(nb, nu * feats_u, rows), (1, 0, 2))
        w_out = jnp.pad(
            w_out.reshape(nb, group, dim), ((0, 0), (0, piece - group), (0, 0))
        )
        w_out = jnp.transpose(w_out.reshape(nb, piece, blocks, block), (2, 0, 1, 3))[:, None]

    q, kv, normed = project(x_all, w_qkv, cosine, sine, piece, step)
    (kv_all,) = together(gather_plan(kv.reshape(2, nb, tok, feats), "uly"))
    o, lse = attend(seg_col, seg_rows, pos_rows, q, kv_all, tile)
    *ff_got, o = lax.optimization_barrier((*ff_got, o))
    w_ff, o_all = together(
        gather_near_plan(assemble(ff_got, ff_places), "uly", nb // 4), gather_plan(o, "blk")
    )
    x1, normed2 = output_project(x_all, o_all, w_out, gain2, step)

    act, d_gate, d_up = hidden(normed2, cot_all, w_ff, step)
    d_norm2 = mix([d_gate, d_up], w_ff, (0, 1), step)

    def meanwhile():
        (out,) = yield [mix([after(act, d_norm2)], w_ff, (2,), step)]
        grads = yield hidden_grads(after(normed2, out), cot_all, d_gate, d_up, act, block)
        return out, grads

    d_norm2, (mlp_out, ff_grads) = together(
        scatter_plan(d_norm2.reshape(nb, tok, dim), "blk"), meanwhile()
    )
    x1_own = lax.dynamic_slice_in_dim(x1, b * tok, tok, 0)
    mlp_out = scatter(after(mlp_out, d_norm2), "blk")
    r2_own = rms_scale(x1_own)
    gain2_part = jnp.sum(d_norm2 * x1_own * r2_own, axis=0, keepdims=True)
    z_two = gain2 * d_norm2
    dx1 = (
        cotangent.astype(f32)
        + r2_own * z_two
        - x1_own * r2_own * r2_own * r2_own * jnp.mean(z_two * x1_own, axis=-1, keepdims=True)
    )
    d_attn = dx1.astype(bf)

    d_o = output_back(d_attn, w_out)
    d_columns = jnp.transpose(d_attn.reshape(tok, nb, rows), (1, 0, 2))
    (d_o,) = together(swap_plan(d_o, "blk"))
    (ff_mine,) = together(scatter_near_plan(ff_grads, "uly"))
    d_o = d_o.reshape(count, feats)
    ff_mine = ff_mine.reshape(3, nb, rows, ff_piece)
    ff_got, ff_places = exchange(lambda i: lax.dynamic_index_in_dim(ff_mine, i, 1, False), "blk")
    d_got, d_places = exchange(lambda i: pick(d_columns, i), "blk")
    dq, dkv = attend_back(
        seg_col, seg_rows, pos_rows, cosine, sine, q, d_o, o, lse, kv_all, tile
    )
    *d_got, dkv = lax.optimization_barrier((*d_got, dkv))
    d_columns = jnp.zeros_like(d_columns)
    for got, at in zip(d_got, d_places):
        d_columns = place(d_columns, got, at)
    out_grads = output_grads(o_all, d_columns.reshape(count, rows), pieces)
    if not strided:
        out_grads = out_grads[:, :, :group]
    dkv, out_grads = together(
        scatter_plan(dkv, "uly"), scatter_plan(out_grads.reshape(nu, feats_u, rows), "uly")
    )
    grad_output = jnp.transpose(out_grads)
    dkv = dkv.astype(bf).reshape(2, count, feats)
    *ff_got, dkv = lax.optimization_barrier((*ff_got, dkv))
    ff_grads = finish(ff_got, ff_places)
    dk, d_norm1, gain1_part = project_back(x_all, w_qkv, cosine, sine, dq, dkv, piece, step)
    gain_parts = jnp.pad(jnp.concatenate([gain1_part, gain2_part]), ((0, PAD - 2), (0, 0)))
    grads = projection_grads(
        [dq, dk, dkv[1]], after(normed, d_norm1), gain_parts, pieces, block
    )
    last = scatter_plan(d_norm1.reshape(nb, tok, dim), "blk")
    if strided:
        d_norm1, got = together(
            last,
            chain(
                scatter_plan(grads, "uly"), lambda mine: swap_plan(mine.astype(bf), "blk")
            ),
        )
        gain_sums = jnp.sum(got[:, 3 * piece : 3 * piece + 2].astype(f32), axis=0)
        heads = [got[:, i * piece : (i + 1) * piece].reshape(feats_u, rows) for i in range(3)]
    else:
        wanted = grads[0, :, : 3 * piece].reshape(blocks, 3, piece, block)[:, :, :group]
        wanted = jnp.transpose(wanted, (1, 2, 0, 3)).reshape(3, group, nb, rows)
        d_norm1, got = together(last, swap_plan(jnp.transpose(wanted, (2, 1, 0, 3)), "blk"))
        got = scatter(got.reshape(nu, feats_u, 3, rows), "uly")[0]
        heads = [got[:, i] for i in range(3)]
        gain_sums = lax.dynamic_slice_in_dim(lax.psum(gain_parts[:2], both), b * rows, rows, 1)
    grad_query, grad_key, grad_value = [jnp.transpose(h).astype(f32) for h in heads]
    x_own = tokens.astype(f32)
    r1_own = rms_scale(x_own)
    z_one = gain1 * d_norm1
    grad_tokens = (
        dx1
        + r1_own * z_one
        - x_own * r1_own * r1_own * r1_own * jnp.mean(z_one * x_own, axis=-1, keepdims=True)
    )
    mlp_out, d_norm1 = lax.optimization_barrier((mlp_out, d_norm1))
    output = x1_own + mlp_out.astype(f32)
    return (
        output,
        grad_tokens,
        gain_sums[0],
        grad_query,
        grad_key,
        grad_value,
        grad_output,
        gain_sums[1],
        *ff_grads,
    )


def solution(mesh):
    tokens_split = P(("blk", "uly"), None)
    weights = P("blk", "uly")
    return jax.shard_map(
        on_device,
        mesh=mesh,
        in_specs=(
            tokens_split,
            P(),
            tokens_split,
            P("blk"),
            weights,
            weights,
            weights,
            weights,
            P("blk"),
            weights,
            weights,
            weights,
        ),
        out_specs=(
            tokens_split,
            tokens_split,
            P("blk"),
            weights,
            weights,
            weights,
            weights,
            P("blk"),
            weights,
            weights,
            weights,
        ),
        check_vma=False,
    )
```

```python
import functools
import math

import jax
import jax.numpy as jnp
from jax import lax
from jax.experimental import pallas as pl
from jax.experimental.pallas import tpu as pltpu
from jax.sharding import PartitionSpec as P

H = 32
HD = 64
LANES = 128
PAD = 16

theta_base = 130000.0
epsilon = 1e-05
bf = jnp.bfloat16
f32 = jnp.float32
NEG = -1e30


def dot_t(left, right):
    return lax.dot_general(left, right, (((1,), (1,)), ((), ())), preferred_element_type=f32)


def dot_n(left, right):
    return jnp.dot(left, right, preferred_element_type=f32)


def dot_c(left, right):
    return lax.dot_general(left, right, (((0,), (0,)), ((), ())), preferred_element_type=f32)


def rms_scale(value):
    return lax.rsqrt(jnp.mean(value * value, axis=-1, keepdims=True) + epsilon)


def params(mib=56):
    return pltpu.CompilerParams(vmem_limit_bytes=mib * 2**20)


def cost(micros):
    return pl.CostEstimate(flops=int(micros * 0.25 * 1.1e9), bytes_accessed=0, transcendentals=0)


def full(shape):
    return pl.BlockSpec(shape, lambda *grid: (0,) * len(shape))


def after(value, *others):
    return lax.optimization_barrier((value, *others))[0]


def hop(value, axis, slow, fast):
    size = lax.axis_size(axis)
    ring = size // 2
    pairs = [(i, ((i // 2 + slow) % ring) * 2 + (i % 2 ^ fast)) for i in range(size)]
    return lax.ppermute(value, axis, pairs)


def near(axis, slow, fast):
    ring = lax.axis_size(axis) // 2
    i = lax.axis_index(axis)
    return ((i // 2 + slow + ring) % ring) * 2 + (i % 2 ^ fast)


def place(out, piece, at):
    return lax.dynamic_update_slice_in_dim(out, piece[None], at, 0)


def pick(parts, at):
    return lax.dynamic_index_in_dim(parts, at, 0, False)


class Rounds:
    def __init__(self):
        self.live, self.results = {}, {}

    def add(self, **plans):
        for name, plan in plans.items():
            self.advance(name, plan, None)

    def advance(self, name, plan, value):
        try:
            self.live[name] = (plan, list(plan.send(value)))
        except StopIteration as end:
            self.live.pop(name, None)
            self.results[name] = end.value

    def round(self, *also):
        waiting = list(self.live.items())
        flat = [v for _, (_, values) in waiting for v in values] + list(also)
        if flat:
            flat = list(lax.optimization_barrier(tuple(flat)))
        for name, (plan, values) in waiting:
            self.advance(name, plan, [flat.pop(0) for _ in values])
        return flat

    def until(self, *names):
        while any(name in self.live for name in names):
            self.round()
        return [self.results[name] for name in names]


def together(*plans):
    rounds = Rounds()
    names = [str(i) for i in range(len(plans))]
    rounds.add(**dict(zip(names, plans)))
    return rounds.until(*names)


def idle(count):
    for _ in range(count):
        yield []


def chain(first, *rest):
    value = yield from first
    for plan in rest:
        value = yield from plan(value)
    return value


def gather_plan(value, axis):
    size = lax.axis_size(axis)
    ring = size // 2
    out = jnp.zeros((size, *value.shape), value.dtype)
    fresh = {0: value}
    crossing = {0: hop(value, axis, 0, 1)}
    for s in range(1, ring // 2 + 1):
        arriving = {-s: hop(fresh[1 - s], axis, 1, 0)}
        if s <= (ring - 1) // 2:
            arriving[s] = hop(fresh[s - 1], axis, -1, 0)
        got = yield [*arriving.values(), *crossing.values()]
        for at, piece in zip(crossing, got[len(arriving) :]):
            out = place(out, piece, near(axis, at, 1))
        fresh = dict(zip(arriving, got))
        for at, piece in fresh.items():
            out = place(out, piece, near(axis, at, 0))
        crossing = {at: hop(piece, axis, 0, 1) for at, piece in fresh.items()}
        if s == 1:
            out = place(out, value, near(axis, 0, 0))
    got = yield list(crossing.values())
    for at, piece in zip(crossing, got):
        out = place(out, piece, near(axis, at, 1))
    return out


def scatter_plan(parts, axis):
    ring = lax.axis_size(axis) // 2
    far, back = ring // 2, (ring - 1) // 2

    def column(offsets, fast):
        return jnp.stack([pick(parts, near(axis, s, fast)) for s in offsets])

    steps = [[s] + ([-s] if s <= back else []) for s in range(far, 0, -1)]
    if ring == 4:
        steps = [[2, -1], [1]]
    steps[-1] = steps[-1] + [0]
    up = down = None
    for offsets in steps:
        crossed = hop(column(offsets, 1), axis, 0, 1)
        got = yield [crossed, *[v for v in (up, down) if v is not None]]
        crossed, carried = got[0], got[1:]
        totals = {
            s: pick(parts, near(axis, s, 0)).astype(f32) + crossed[k].astype(f32)
            for k, s in enumerate(offsets)
        }
        if up is not None:
            up = carried.pop(0).astype(f32)
        if down is not None:
            down = carried.pop(0).astype(f32)
        ups = [s for s in offsets if s > 0]
        downs = [s for s in offsets if s < 0]
        held = down
        if ups:
            total = totals[ups[0]] if up is None else totals[ups[0]] + up
            up = hop(total.astype(bf), axis, 1, 0)
        if downs:
            total = totals[downs[0]] if down is None else totals[downs[0]] + down
            down = hop(total.astype(bf), axis, -1, 0)
            held = None
        own = totals.get(0)
    if held is not None:
        own = own + held
        down = None
    for piece in (yield [v for v in (up, down) if v is not None]):
        own = own + piece.astype(f32)
    return own


def swap_plan(parts, axis):
    ring = lax.axis_size(axis) // 2
    fast = lax.axis_index(axis) % 2
    slow = lax.axis_index(axis) // 2
    columns = jnp.swapaxes(parts.reshape(ring, 2, *parts.shape[1:]), 0, 1)
    kept = pick(columns, fast)
    (given,) = yield [hop(pick(columns, 1 - fast), axis, 0, 1)]
    pairs = jnp.stack([jnp.where(fast == 0, kept, given), jnp.where(fast == 0, given, kept)], 1)
    out = place(jnp.zeros_like(pairs), pick(pairs, slow), slow)
    arrived = yield [hop(pick(pairs, (slow + s) % ring), axis, s, 0) for s in range(1, ring)]
    for s, piece in enumerate(arrived, 1):
        out = place(out, piece, (slow - s + ring) % ring)
    return out.reshape(parts.shape)


def gather_near_plan(value, axis, spare=0):
    ring = lax.axis_size(axis) // 2
    crossed = [hop(value, axis, 0, 1)]
    got = [hop(value, axis, s, 0) for s in range(1, ring)]
    yield from idle(spare)
    got = yield got
    crossed += [hop(piece, axis, 0, 1) for piece in got]
    crossed = yield crossed
    return [value, *got, *crossed]


def scatter_near_plan(parts, axis, spare=0):
    ring = lax.axis_size(axis) // 2
    crossed = yield [hop(part, axis, 0, 1) for part in parts[ring:]]
    sums = [mine.astype(f32) + piece.astype(f32) for mine, piece in zip(parts, crossed)]
    total = sums[0].astype(bf)
    total, *given = yield [total, *[part.astype(bf) for part in sums[1:]]]
    got = [hop(part, axis, -s, 0) for s, part in enumerate(given, 1)]
    yield from idle(spare)
    total = total.astype(f32)
    for piece in (yield got):
        total = total + piece.astype(f32)
    return total.astype(bf)


def swap(parts, axis):
    return lax.all_to_all(parts, axis, 0, 0, tiled=True)


def gather(value, axis):
    return lax.all_gather(value, axis, axis=0, tiled=True)


def scatter(value, axis):
    return lax.psum_scatter(value, axis, scatter_dimension=0, tiled=True)


def turned(value):
    width = value.shape[1]
    lane = lax.broadcasted_iota(jnp.int32, value.shape, 1)
    return jnp.where(
        lane % HD < HD // 2,
        pltpu.roll(value, width - HD // 2, 1),
        pltpu.roll(value, HD // 2, 1),
    )


def wide(table, width):
    return jnp.concatenate([table] * (width // LANES), axis=1)


def weight_block(w_ref, block, part, piece):
    w = w_ref[:, block, part * piece : (part + 1) * piece, :]
    return w.reshape(w.shape[0] * piece, w.shape[2])


def project_kernel(piece, x_ref, w_ref, cos_ref, sin_ref, q_ref, kv_ref, normed_ref):
    blocks, width = w_ref.shape[1], w_ref.shape[3]
    x = x_ref[...].astype(f32)
    r1 = rms_scale(x)
    total = [0.0, 0.0, 0.0]
    for block in range(blocks):
        at = slice(block * width, (block + 1) * width)
        gain = w_ref[0, block, 3 * piece : 3 * piece + PAD, :][0:1].astype(f32)
        normed = (x[:, at] * r1 * gain).astype(bf)
        normed_ref[:, at] = normed
        for part in range(3):
            total[part] = total[part] + dot_t(normed, weight_block(w_ref, block, part, piece))
    feats = total[0].shape[1]
    cosine, sine = wide(cos_ref[...], feats), wide(sin_ref[...], feats)

    def rotate(value):
        value = value.astype(bf).astype(f32)
        return (value * cosine + turned(value) * sine).astype(bf)

    q_ref[...] = rotate(total[0])
    kv_ref[0] = rotate(total[1])
    kv_ref[1] = total[2].astype(bf)


def project(x_all, w, cosine, sine, piece, rows):
    count, dim = x_all.shape
    feats = w.shape[0] * piece
    tiled = lambda n: pl.BlockSpec((rows, n), lambda i: (i, 0))
    return pl.pallas_call(
        functools.partial(project_kernel, piece),
        grid=(count // rows,),
        in_specs=[tiled(dim), full(w.shape), tiled(LANES), tiled(LANES)],
        out_specs=[
            tiled(feats),
            pl.BlockSpec((2, rows, feats), lambda i: (0, i, 0)),
            tiled(dim),
        ],
        out_shape=[
            jax.ShapeDtypeStruct((count, feats), bf),
            jax.ShapeDtypeStruct((2, count, feats), bf),
            jax.ShapeDtypeStruct((count, dim), bf),
        ],
        compiler_params=params(),
        cost_estimate=cost(count * 0.009),
        name="project",
    )(x_all, w, cosine, sine)


def flip_kernel(piece, q_ref, k_ref, v_ref, o_ref, ga_ref, gm_ref, sent_ref, out_ref):
    size = sent_ref.shape[0]
    for i, ref in enumerate((q_ref, k_ref, v_ref)):
        sent_ref[:, i * piece : (i + 1) * piece, :] = (
            ref[...].T.astype(bf).reshape(size, piece, ref.shape[0])
        )
    row = lax.broadcasted_iota(jnp.int32, (PAD, q_ref.shape[0]), 0)
    gains = jnp.where(row == 0, ga_ref[...], gm_ref[...]).astype(bf)
    for j in range(size):
        sent_ref[j, 3 * piece :, :] = gains
    out_ref[...] = o_ref[...].T.astype(bf)


def flip(w_query, w_key, w_value, w_output, attn_gain, mlp_gain, size):
    rows, feats = w_query.shape
    piece = feats // size
    return pl.pallas_call(
        functools.partial(flip_kernel, piece),
        out_shape=[
            jax.ShapeDtypeStruct((size, 3 * piece + PAD, rows), bf),
            jax.ShapeDtypeStruct((feats, rows), bf),
        ],
        compiler_params=params(),
        cost_estimate=cost(5),
        name="flip",
    )(w_query, w_key, w_value, w_output, attn_gain[None], mlp_gain[None])


def allowed_block(segk_ref, seg_q, pos_q, chunk, width):
    seg_k = segk_ref[pl.ds(pl.multiple_of(chunk * width, width), width), :]
    pos_k = chunk * width + lax.broadcasted_iota(jnp.int32, (width, 1), 0)
    return (seg_k == seg_q) & (pos_k <= pos_q)


def head_lanes(rows, head):
    lane = lax.broadcasted_iota(jnp.int32, (rows, LANES), 1)
    return (lane < HD) if head == 0 else (lane >= HD)


def attend_kernel(tile, segk_ref, segq_ref, posq_ref, q_ref, kv_ref, o_ref, lse_ref, vt_ref):
    nu, _, nb, tok, _ = kv_ref.shape
    width = nu * tok
    rows = tile * tok
    j = pl.program_id(1)

    @pl.when(j == 0)
    def _():
        for c in range(nb):
            vt_ref[c] = kv_ref[:, 1, c].reshape(width, LANES).T

    seg_q, pos_q = segq_ref[0], posq_ref[0]
    q = q_ref[...] * jnp.asarray(1.0 / math.sqrt(HD), bf)
    q_heads = [jnp.where(head_lanes(rows, h), q, jnp.zeros_like(q)) for h in range(2)]

    def step(chunk, state):
        k = kv_ref[:, 0, chunk].reshape(width, LANES)
        v_t = vt_ref[chunk]
        ok = allowed_block(segk_ref, seg_q, pos_q, chunk, width)
        new = []
        for h in range(2):
            best, total, acc = state[h]
            s = jnp.where(ok, dot_t(k, q_heads[h]), NEG)
            best_new = jnp.maximum(best, jnp.max(s, axis=0, keepdims=True))
            p = jnp.exp(s - best_new)
            factor = jnp.exp(best - best_new)
            total = total * factor + jnp.sum(p, axis=0, keepdims=True)
            acc = acc * factor + dot_n(v_t[h * HD : (h + 1) * HD], p.astype(bf))
            new.append((best_new, total, acc))
        return tuple(new)

    start = (
        jnp.full((1, rows), NEG, f32),
        jnp.zeros((1, rows), f32),
        jnp.zeros((HD, rows), f32),
    )
    state = lax.fori_loop(0, (j + 1) * tile, step, (start, start))
    o_t = jnp.concatenate([acc / total for _, total, acc in state], axis=0)
    o_ref[...] = o_t.T.astype(bf)
    lse_ref[0, 0] = jnp.concatenate([best + jnp.log(total) for best, total, _ in state], axis=0)


def attend(segments, seg_q, pos_q, q, kv, tile):
    nu, _, nb, tok, feats = kv.shape
    rows = tile * tok
    nq = nb // tile
    pairs = feats // LANES
    row_spec = pl.BlockSpec((1, 1, rows), lambda p, j: (j, 0, 0))
    q_spec = pl.BlockSpec((rows, LANES), lambda p, j: (j, p))
    return pl.pallas_call(
        functools.partial(attend_kernel, tile),
        grid=(pairs, nq),
        in_specs=[
            full(segments.shape),
            row_spec,
            row_spec,
            q_spec,
            pl.BlockSpec((nu, 2, nb, tok, LANES), lambda p, j: (0, 0, 0, 0, p)),
        ],
        out_specs=[q_spec, pl.BlockSpec((1, 1, 2, rows), lambda p, j: (p, j, 0, 0))],
        out_shape=[
            jax.ShapeDtypeStruct((nb * tok, feats), bf),
            jax.ShapeDtypeStruct((pairs, nq, 2, rows), f32),
        ],
        scratch_shapes=[pltpu.VMEM((nb, LANES, nu * tok), bf)],
        compiler_params=params(),
        cost_estimate=cost(44 * nb * tok * nb / 8192),
        name="attend",
    )(segments, seg_q, pos_q, q, kv)


def attend_back_kernel(
    tile,
    first_ref,
    clear_ref,
    segk_ref,
    segq_ref,
    posq_ref,
    cos_ref,
    sin_ref,
    q_ref,
    do_ref,
    o_ref,
    lse_ref,
    kv_ref,
    dq_ref,
    dkv_ref,
    acc_ref,
    delta_ref,
):
    nu, _, _, tok, _ = kv_ref.shape
    nq = segq_ref.shape[0]
    width = nu * tok
    rows = tile * tok
    chunk = pl.program_id(0)
    nb = pl.num_programs(0)
    scale = jnp.asarray(1.0 / math.sqrt(HD), bf)

    @pl.when(chunk == 0)
    def _():
        acc_ref[...] = jnp.zeros_like(acc_ref)
        lane = lax.broadcasted_iota(jnp.int32, (8, LANES), 1)
        row = lax.broadcasted_iota(jnp.int32, (8, LANES), 0)
        mine = jnp.where(lane // HD == row, 1.0, 0.0).astype(f32)
        for j in range(nq):
            part = do_ref[pl.ds(j * rows, rows), :].astype(f32) * o_ref[
                pl.ds(j * rows, rows), :
            ].astype(f32)
            delta_ref[j] = lax.dot_general(
                mine,
                part,
                (((1,), (1,)), ((), ())),
                preferred_element_type=f32,
                precision=lax.Precision.HIGHEST,
            )

    k = kv_ref[:, 0, 0].reshape(width, LANES)
    v = kv_ref[:, 1, 0].reshape(width, LANES)

    def step(masked, j, state):
        dk, dv = state
        at = pl.ds(pl.multiple_of(j * rows, rows), rows)
        q = q_ref[at, :] * scale
        do = do_ref[at, :]
        if masked:
            ok = allowed_block(segk_ref, segq_ref[j], posq_ref[j], chunk, width)
        parts = []
        for h in range(2):
            mine = head_lanes(rows, h)
            q_h = jnp.where(mine, q, jnp.zeros_like(q))
            do_h = jnp.where(mine, do, jnp.zeros_like(do))
            s = dot_t(k, q_h) - lse_ref[0, j, h : h + 1]
            p = jnp.exp(jnp.where(ok, s, NEG) if masked else s)
            ds = (p * (dot_t(v, do_h) - delta_ref[j, h : h + 1])).astype(bf)
            dv = dv + dot_n(p.astype(bf), do_h)
            dk = dk + dot_n(ds, q_h)
            parts.append(dot_c(ds, k))
        acc_ref[at, :] = acc_ref[at, :] + jnp.where(head_lanes(rows, 0), parts[0], parts[1])
        return dk, dv

    zero = jnp.zeros((width, LANES), f32)
    dk, dv = lax.fori_loop(chunk // tile, nq, functools.partial(step, True), (zero, zero))
    dkv_ref[:, 0, 0] = dk.astype(bf).reshape(nu, tok, LANES)
    dkv_ref[:, 1, 0] = dv.astype(bf).reshape(nu, tok, LANES)

    @pl.when(chunk == nb - 1)
    def _():
        dq = acc_ref[...] * (1.0 / math.sqrt(HD))
        dq_ref[...] = (dq * cos_ref[...] - turned(dq) * sin_ref[...]).astype(bf)


def attend_back(where, cosine, sine, q, do, o, lse, kv, pair, tile):
    nu, _, nb, tok, _ = kv.shape
    first, clear, segments, seg_q, pos_q = where
    rows = tile * tok
    nq = nb // tile
    whole_rows = full((nq, 1, rows))
    table = full((nb * tok, LANES))
    pair_spec = pl.BlockSpec((nb * tok, LANES), lambda c, *_: (0, pair))
    return pl.pallas_call(
        functools.partial(attend_back_kernel, tile),
        grid_spec=pltpu.PrefetchScalarGridSpec(
            num_scalar_prefetch=2,
            grid=(nb,),
            in_specs=[
                full(segments.shape),
                whole_rows,
                whole_rows,
                table,
                table,
                pair_spec,
                pair_spec,
                pair_spec,
                pl.BlockSpec((1, nq, 2, rows), lambda c, *_: (pair, 0, 0, 0)),
                pl.BlockSpec((nu, 2, 1, tok, LANES), lambda c, *_: (0, 0, c, 0, pair)),
            ],
            out_specs=[
                table,
                pl.BlockSpec((nu, 2, 1, tok, LANES), lambda c, *_: (0, 0, c, 0, 0)),
            ],
            scratch_shapes=[
                pltpu.VMEM((nb * tok, LANES), f32),
                pltpu.VMEM((nq, 8, rows), f32),
            ],
        ),
        out_shape=[
            jax.ShapeDtypeStruct((nb * tok, LANES), bf),
            jax.ShapeDtypeStruct((nu, 2, nb, tok, LANES), bf),
        ],
        compiler_params=params(),
        cost_estimate=cost(25 * nb * tok * nb / 8192),
        name="attend_back",
    )(first, clear, segments, seg_q, pos_q, cosine, sine, q, do, o, lse, kv)


def output_kernel(x_ref, o_ref, w_ref, gain_ref, x1_ref, normed_ref):
    blocks, pieces, groups, piece, width = w_ref.shape
    square = 0.0
    for block in range(blocks):
        at = slice(block * width, (block + 1) * width)
        total = x_ref[:, at].astype(f32)
        for g in range(groups):
            total = total + dot_n(o_ref[g], w_ref[block, :, g].reshape(pieces * piece, width))
        x1_ref[:, at] = total
        square = square + jnp.sum(total * total, axis=1, keepdims=True)
    r2 = lax.rsqrt(square * (1.0 / (blocks * width)) + epsilon)
    normed_ref[...] = (x1_ref[...] * r2 * gain_ref[...]).astype(bf)


def output_project(x_all, o_all, w_out, gain, rows):
    count, dim = x_all.shape
    groups, _, feats = o_all.shape
    tiled = pl.BlockSpec((rows, dim), lambda i: (i, 0))
    return pl.pallas_call(
        output_kernel,
        grid=(count // rows,),
        in_specs=[
            tiled,
            pl.BlockSpec((groups, rows, feats), lambda i: (0, i, 0)),
            full(w_out.shape),
            full(gain.shape),
        ],
        out_specs=[tiled, tiled],
        out_shape=[
            jax.ShapeDtypeStruct((count, dim), f32),
            jax.ShapeDtypeStruct((count, dim), bf),
        ],
        compiler_params=params(),
        cost_estimate=cost(count * 0.015),
        name="output_project",
    )(x_all, o_all, w_out, gain)


def output_back_kernel(d_ref, w_ref, out_ref):
    blocks, pieces, _, piece, width = w_ref.shape
    total = 0.0
    for block in range(blocks):
        at = slice(block * width, (block + 1) * width)
        total = total + dot_t(d_ref[:, at], w_ref[block, :, 0].reshape(pieces * piece, width))
    out_ref[0] = total.astype(bf)


def output_back(d_attn, w_out):
    tok, dim = d_attn.shape
    blocks, pieces, groups, piece, width = w_out.shape
    return pl.pallas_call(
        output_back_kernel,
        grid=(groups,),
        in_specs=[
            full(d_attn.shape),
            pl.BlockSpec((blocks, pieces, 1, piece, width), lambda g: (0, 0, g, 0, 0)),
        ],
        out_specs=pl.BlockSpec((1, tok, pieces * piece), lambda g: (g, 0, 0)),
        out_shape=jax.ShapeDtypeStruct((groups, tok, pieces * piece), bf),
        compiler_params=params(),
        cost_estimate=cost(8),
        name="output_back",
    )(d_attn, w_out)


def project_back_kernel(piece, n, x_ref, w_ref, cos_ref, sin_ref, *refs):
    dq_refs, dkv_refs, (all_ref, dn_ref, gain_ref) = refs[:n], refs[n : 2 * n], refs[2 * n :]
    blocks, width = w_ref.shape[1], w_ref.shape[3]
    feats = n * LANES
    cosine, sine = wide(cos_ref[...], feats), wide(sin_ref[...], feats)
    dk = jnp.concatenate([ref[0] for ref in dkv_refs], axis=1).astype(f32)
    parts = (
        jnp.concatenate([ref[...] for ref in dq_refs], axis=1),
        (dk * cosine - turned(dk) * sine).astype(bf),
        jnp.concatenate([ref[1] for ref in dkv_refs], axis=1),
    )
    for i in range(3):
        all_ref[i] = parts[i]
    x = x_ref[...].astype(f32)
    r1 = rms_scale(x)

    @pl.when(pl.program_id(0) == 0)
    def _():
        gain_ref[...] = jnp.zeros_like(gain_ref)

    for block in range(blocks):
        at = slice(block * width, (block + 1) * width)
        total = 0.0
        for part in range(3):
            total = total + dot_n(parts[part], weight_block(w_ref, block, part, piece))
        dn_ref[:, at] = total.astype(bf)
        gain_ref[:, at] = gain_ref[:, at] + jnp.sum(total * (x[:, at] * r1), axis=0, keepdims=True)


def project_back(x_all, w, cosine, sine, dq, dkv, piece, rows):
    count, dim = x_all.shape
    n = len(dq)
    feats = n * LANES
    tiled = lambda width: pl.BlockSpec((rows, width), lambda i: (i, 0))
    return pl.pallas_call(
        functools.partial(project_back_kernel, piece, n),
        grid=(count // rows,),
        in_specs=[
            tiled(dim),
            full(w.shape),
            tiled(LANES),
            tiled(LANES),
            *[tiled(LANES)] * n,
            *[pl.BlockSpec((2, rows, LANES), lambda i: (0, i, 0))] * n,
        ],
        out_specs=[
            pl.BlockSpec((3, rows, feats), lambda i: (0, i, 0)),
            tiled(dim),
            full((1, dim)),
        ],
        out_shape=[
            jax.ShapeDtypeStruct((3, count, feats), bf),
            jax.ShapeDtypeStruct((count, dim), bf),
            jax.ShapeDtypeStruct((1, dim), f32),
        ],
        compiler_params=params(),
        cost_estimate=cost(count * 0.01),
        name="project_back",
    )(x_all, w, cosine, sine, *dq, *dkv)


def projection_grads_kernel(left_ref, right_ref, gain_ref, out_ref, turned_ref):
    n, feats, _ = turned_ref.shape
    pieces = out_ref.shape[0]

    @pl.when(pl.program_id(0) == 0)
    def _():
        for i in range(n):
            turned_ref[i] = left_ref[i].T

    piece = feats // pieces
    right = right_ref[...]
    width = right.shape[1]
    for i in range(n):
        grad = dot_n(turned_ref[i], right).astype(bf)
        out_ref[:, 0, i * piece : (i + 1) * piece, :] = grad.reshape(pieces, piece, width)
    gain = gain_ref[...].astype(bf)
    for u in range(pieces):
        out_ref[u, 0, n * piece :, :] = gain


def projection_grads(lefts, right, gain, pieces, width):
    n, count, feats = lefts.shape
    dim = right.shape[1]
    rows = n * (feats // pieces) + PAD
    return pl.pallas_call(
        projection_grads_kernel,
        grid=(dim // width,),
        in_specs=[
            full(lefts.shape),
            pl.BlockSpec((count, width), lambda i: (0, i)),
            pl.BlockSpec((PAD, width), lambda i: (0, i)),
        ],
        out_specs=pl.BlockSpec((pieces, 1, rows, width), lambda i: (0, i, 0, 0)),
        out_shape=jax.ShapeDtypeStruct((pieces, dim // width, rows, width), bf),
        scratch_shapes=[pltpu.VMEM((n, feats, count), bf)],
        compiler_params=params(),
        cost_estimate=cost(2.5 * n),
        name="projection_grads",
    )(lefts, right, gain)


def output_grads_kernel(o_ref, d_ref, out_ref):
    pieces, _, piece, width = out_ref.shape
    grad = dot_n(o_ref[0].T, d_ref[...])
    out_ref[:, 0] = grad.astype(bf).reshape(pieces, piece, width)


def output_grads(o_all, d_columns, pieces):
    groups, count, feats = o_all.shape
    width = d_columns.shape[1]
    shape = (pieces, groups, feats // pieces, width)
    return pl.pallas_call(
        output_grads_kernel,
        grid=(groups,),
        in_specs=[
            pl.BlockSpec((1, count, feats), lambda g: (g, 0, 0)),
            full(d_columns.shape),
        ],
        out_specs=pl.BlockSpec((pieces, 1, *shape[2:]), lambda g: (0, g, 0, 0)),
        out_shape=jax.ShapeDtypeStruct(shape, bf),
        compiler_params=params(),
        cost_estimate=cost(6),
        name="output_grads",
    )(o_all, d_columns)


def prepare_kernel(wg_ref, wu_ref, wd_ref, out_ref):
    for i, ref in enumerate((wg_ref, wu_ref, wd_ref)):
        out_ref[0, i] = ref[...].astype(bf)


def prepare(w_gate, w_up, w_down, size):
    rows, columns = w_gate.shape
    width = columns // size
    if width % LANES:
        stacked = jnp.stack([w.astype(bf) for w in (w_gate, w_up, w_down)])
        return jnp.transpose(stacked.reshape(3, rows, size, width), (2, 0, 1, 3))
    spec = pl.BlockSpec((rows, width), lambda i: (0, i))
    return pl.pallas_call(
        prepare_kernel,
        grid=(size,),
        in_specs=[spec] * 3,
        out_specs=pl.BlockSpec((1, 3, rows, width), lambda i: (i, 0, 0, 0)),
        out_shape=jax.ShapeDtypeStruct((size, 3, rows, width), bf),
        compiler_params=params(),
        cost_estimate=cost(4),
        name="prepare",
    )(w_gate, w_up, w_down)


def finish_kernel(in_ref, *outs):
    n, _, _, width = in_ref.shape
    for k in range(n):
        for i in range(3):
            outs[i][:, k * width : (k + 1) * width] = in_ref[k, i].astype(f32)


def finish(parts):
    n, _, rows, width = parts.shape
    if width % LANES:
        out = jnp.transpose(parts, (1, 2, 0, 3)).reshape(3, rows, n * width).astype(f32)
        return [out[i] for i in range(3)]
    return pl.pallas_call(
        finish_kernel,
        out_shape=[jax.ShapeDtypeStruct((rows, n * width), f32)] * 3,
        compiler_params=params(),
        cost_estimate=cost(5),
        name="finish",
    )(parts)


def whole_weight(ref, k):
    w = ref[:, k]
    return w.reshape(w.shape[0] * w.shape[1], w.shape[2])


def hidden_kernel(n, *refs):
    n_ref, g_ref = refs[:2]
    act_ref, dg_ref, du_ref = refs[2 + n :]
    normed, cot = n_ref[...], g_ref[...]
    for i in range(n):
        w_ref = refs[2 + i]
        gate = dot_n(normed, whole_weight(w_ref, 0))
        up = dot_n(normed, whole_weight(w_ref, 1))
        d_act = dot_n(cot, whole_weight(w_ref, 2))
        sigma = jax.nn.sigmoid(gate)
        silu = gate * sigma
        act_ref[i] = (silu * up).astype(bf)
        du_ref[i] = (d_act * silu).astype(bf)
        dg_ref[i] = (d_act * up * (sigma * (1.0 + gate * (1.0 - sigma)))).astype(bf)


def hidden(normed, cot, weights, rows):
    count, dim = normed.shape
    n = len(weights)
    width = weights[0].shape[3]
    tiled = pl.BlockSpec((rows, dim), lambda i: (i, 0))
    out = pl.BlockSpec((n, rows, width), lambda i: (0, i, 0))
    return pl.pallas_call(
        functools.partial(hidden_kernel, n),
        grid=(count // rows,),
        in_specs=[tiled, tiled] + [full(w.shape) for w in weights],
        out_specs=[out] * 3,
        out_shape=[jax.ShapeDtypeStruct((n, count, width), bf)] * 3,
        compiler_params=params(),
        cost_estimate=cost(20),
        name="hidden",
    )(normed, cot, *weights)


def mix_kernel(which, n, *refs):
    lefts, weights, out_ref = refs[: len(which)], refs[len(which) : -1], refs[-1]
    total = 0.0
    for k in range(len(which)):
        for i in range(n):
            total = total + dot_t(lefts[k][i], whole_weight(weights[i], k))
    out_ref[...] = total.astype(bf)


def mix(lefts, weights, which, rows):
    n, count, width = lefts[0].shape
    blocks, _, rows_w, _ = weights[0].shape
    dim = blocks * rows_w
    chosen = pl.BlockSpec(
        (blocks, len(which), rows_w, width), lambda i: (0, which[0] // len(which), 0, 0)
    )
    return pl.pallas_call(
        functools.partial(mix_kernel, which, n),
        grid=(count // rows,),
        in_specs=[pl.BlockSpec((n, rows, width), lambda i: (0, i, 0))] * len(which)
        + [chosen] * n,
        out_specs=pl.BlockSpec((rows, dim), lambda i: (i, 0)),
        out_shape=jax.ShapeDtypeStruct((count, dim), bf),
        compiler_params=params(),
        cost_estimate=cost(8 * len(which)),
        name="mix",
    )(*lefts, *weights)


def hidden_grads_kernel(n_ref, g_ref, dg_ref, du_ref, act_ref, *outs):
    normed, cot = n_ref[...].T, g_ref[...].T
    for i, out_ref in enumerate(outs):
        for k, grad in enumerate(
            (dot_n(normed, dg_ref[i]), dot_n(normed, du_ref[i]), dot_n(cot, act_ref[i]))
        ):
            out_ref[:, k] = grad.astype(bf).reshape(out_ref.shape[0], *out_ref.shape[2:])


def hidden_grads(normed, cot, d_gate, d_up, act, rows):
    count, dim = normed.shape
    block = max(rows, LANES)
    n, _, width = act.shape
    columns = pl.BlockSpec((count, block), lambda i: (0, i))
    return pl.pallas_call(
        hidden_grads_kernel,
        grid=(dim // block,),
        in_specs=[columns, columns] + [full(act.shape)] * 3,
        out_specs=[pl.BlockSpec((block // rows, 3, rows, width), lambda i: (i, 0, 0, 0))] * n,
        out_shape=[jax.ShapeDtypeStruct((dim // rows, 3, rows, width), bf)] * n,
        compiler_params=params(),
        cost_estimate=cost(25),
        name="hidden_grads",
    )(normed, cot, d_gate, d_up, act)


def on_device(
    tokens,
    segments,
    cotangent,
    attn_gain,
    w_query,
    w_key,
    w_value,
    w_output,
    mlp_gain,
    w_gate,
    w_up,
    w_down,
):
    nb, nu = lax.axis_size("blk"), lax.axis_size("uly")
    b, u = lax.axis_index("blk"), lax.axis_index("uly")
    tok, dim = tokens.shape
    seq = segments.shape[0]
    rows, feats_u = w_query.shape
    group = feats_u * nu // nb
    strided = (feats_u // HD) % nb == 0 and rows % LANES == 0
    count = nb * tok
    tile = 2
    both = ("blk", "uly")
    block = rows if strided else 2 * LANES
    blocks = dim // block
    pieces = nu if strided else 1
    piece = group // nu if strided else -(-group // LANES) * LANES
    feats = pieces * piece
    step = 2 * tok

    seg_mine = pick(jnp.swapaxes(segments.reshape(nb, nu, tok), 0, 1), u).reshape(count)
    index = (
        jnp.arange(nb, dtype=jnp.int32)[:, None] * (nu * tok)
        + u * tok
        + jnp.arange(tok, dtype=jnp.int32)[None, :]
    ).reshape(count)
    first = jnp.sum((segments[None, :] < seg_mine[:, None]).astype(jnp.int32), axis=1)
    lane = jnp.arange(LANES, dtype=jnp.int32)
    freq = theta_base ** (-((lane % (HD // 2)).astype(f32) * 2.0) / HD)
    angles = (index - first).astype(f32)[:, None] * freq[None, :]
    cosine = jnp.cos(angles)
    sine = jnp.sin(angles) * jnp.where(lane % HD < HD // 2, -1.0, 1.0)[None, :]
    width = nu * tok
    rows_q = tile * tok
    seg_rows = seg_mine.reshape(nb // tile, 1, rows_q)
    pos_rows = index.reshape(nb // tile, 1, rows_q)
    seg_k = segments.reshape(nb, width)
    low_q, high_q = seg_rows[:, 0, :1], seg_rows[:, 0, -1:]
    first_chunk = jnp.sum((seg_k[None, :, -1] < low_q).astype(jnp.int32), axis=1)
    clear = (
        (low_q == high_q)
        & (seg_k[None, :, 0] == low_q)
        & (seg_k[None, :, -1] == low_q)
        & (jnp.arange(1, nb + 1, dtype=jnp.int32)[None, :] * width <= pos_rows[:, 0, :1])
    )
    where = (first_chunk, clear.astype(jnp.int32).reshape(-1), segments[:, None], seg_rows, pos_rows)

    ff_u = w_gate.shape[1]
    ff_piece = ff_u // nb
    tokens_plan = gather_plan(tokens, "blk")

    def prepared():
        yield []
        (value,) = yield [prepare(w_gate, w_up, w_down, nb)]
        return value

    def swapped(parts, spare=0):
        got = swap(parts, "blk")
        yield from idle(spare)
        (got,) = yield [got]
        return got

    if strided:
        sent, out_flipped = flip(w_query, w_key, w_value, w_output, attn_gain, mlp_gain, nb)
        x_all, ff_sent, w_qkv = together(
            tokens_plan,
            prepared(),
            chain(swapped(sent, 1), lambda got: gather_plan(got, "uly")),
        )
    else:
        gains = jnp.stack([attn_gain, mlp_gain]).astype(bf)
        flipped = [jnp.transpose(w.astype(bf)) for w in (w_query, w_key, w_value, w_output)]
        out_flipped = flipped[3]
        sent = gather(jnp.stack(flipped[:3])[None], "uly")
        sent = jnp.transpose(sent, (0, 2, 1, 3)).reshape(nb, group, 3, rows)
        x_all, ff_sent, got = together(tokens_plan, prepared(), swapped(sent))
        got = jnp.transpose(got, (2, 1, 0, 3)).reshape(3, group, dim)
        got = jnp.pad(got, ((0, 0), (0, piece - group), (0, 0))).reshape(3 * piece, dim)
        all_gains = jnp.transpose(gather(gains[None], "blk"), (1, 0, 2)).reshape(2, dim)
        got = jnp.concatenate([got, jnp.pad(all_gains, ((0, PAD - 2), (0, 0)))])
        w_qkv = jnp.transpose(got.reshape(3 * piece + PAD, blocks, block), (1, 0, 2))[None]
    x_all = x_all.reshape(count, dim)
    gain1, gain2 = [
        w_qkv[0, :, 3 * piece + i, :].reshape(1, dim).astype(f32) for i in range(2)
    ]

    ff_got = swap(after(ff_sent, x_all), "blk")
    w_out = gather(after(out_flipped, x_all)[None], both)
    cot_all = gather(after(cotangent, x_all, w_out), "blk")
    if strided:
        w_out = w_out.reshape(nb, nu, nb, piece, rows)
    else:
        w_out = jnp.transpose(w_out.reshape(nb, nu * feats_u, rows), (1, 0, 2))
        w_out = jnp.pad(
            w_out.reshape(nb, group, dim), ((0, 0), (0, piece - group), (0, 0))
        )
        w_out = jnp.transpose(w_out.reshape(nb, piece, blocks, block), (2, 0, 1, 3))[:, None]

    q, kv, normed = project(x_all, w_qkv, cosine, sine, piece, step)
    (kv_all,) = together(gather_plan(kv.reshape(2, nb, tok, feats), "uly"))
    o, lse = attend(*where[2:], q, kv_all, tile)
    ff_got, o = lax.optimization_barrier((ff_got, o))
    rounds = Rounds()
    rounds.add(o=gather_plan(o, "blk"), ff=gather_near_plan(ff_got, "uly", nb // 4))
    (o_all,) = rounds.until("o")
    x1, normed2 = output_project(x_all, o_all, w_out, gain2, step)

    (w_ff,) = rounds.until("ff")

    act, d_gate, d_up = hidden(normed2, cot_all, w_ff, step)
    d_norm2 = mix([d_gate, d_up], w_ff, (0, 1), step)

    def mlp_plan():
        (out,) = yield [mix([act], w_ff, (2,), step)]
        return out

    def hidden_grads_plan():
        yield []
        grads = yield hidden_grads(
            after(normed2, d_norm2), cot_all, d_gate, d_up, act, rows
        )
        return (yield from scatter_near_plan(grads, "uly", 2 * nb))

    rounds = Rounds()
    rounds.add(
        d_norm2=scatter_plan(d_norm2.reshape(nb, tok, dim), "blk"),
        mlp=mlp_plan(),
        ff=hidden_grads_plan(),
    )
    d_norm2, mlp_out = rounds.until("d_norm2", "mlp")
    x1_own = lax.dynamic_slice_in_dim(x1, b * tok, tok, 0)
    mlp_out = scatter(after(mlp_out, d_norm2), "blk")
    r2_own = rms_scale(x1_own)
    gain2_part = jnp.sum(d_norm2 * x1_own * r2_own, axis=0, keepdims=True)
    z_two = gain2 * d_norm2
    dx1 = (
        cotangent.astype(f32)
        + r2_own * z_two
        - x1_own * r2_own * r2_own * r2_own * jnp.mean(z_two * x1_own, axis=-1, keepdims=True)
    )
    d_attn = dx1.astype(bf)

    d_o = output_back(d_attn, w_out)
    d_columns = jnp.transpose(d_attn.reshape(tok, nb, rows), (1, 0, 2))
    rounds.add(d_o=swap_plan(d_o, "blk"))
    (got,) = rounds.until("d_o")
    d_o = got.reshape(count, feats)
    d_columns = swap(after(d_columns, d_o), "blk")
    pairs = feats // LANES
    dq = []
    for pair in range(pairs):
        dq_pair, dkv = attend_back(where, cosine, sine, q, d_o, o, lse, kv_all, pair, tile)
        if pair == 0:
            dkv, d_o, d_columns = lax.optimization_barrier((dkv, d_o, d_columns))
            (ff_mine,) = rounds.until("ff")
            ff_mine, d_o, d_columns = lax.optimization_barrier((ff_mine, d_o, d_columns))
            ff_got = swap(ff_mine, "blk")
        rounds.add(**{f"dkv{pair}": scatter_plan(dkv, "uly")})
        dq.append(dq_pair)
    mlp_out, d_columns = rounds.round(mlp_out, d_columns)
    out_grads = output_grads(o_all, d_columns.reshape(count, rows), pieces)
    if not strided:
        out_grads = out_grads[:, :, :group]
    dkv = rounds.until(*[f"dkv{pair}" for pair in range(pairs)])
    *dkv, out_grads, ff_got = lax.optimization_barrier((*dkv, out_grads, ff_got))
    rounds.add(out=scatter_plan(out_grads.reshape(nu, feats_u, rows), "uly"))
    dkv = [part.astype(bf).reshape(2, count, LANES) for part in dkv]
    d_qkv, d_norm1, gain1_part = project_back(x_all, w_qkv, cosine, sine, dq, dkv, piece, step)
    gain_parts = jnp.pad(jnp.concatenate([gain1_part, gain2_part]), ((0, PAD - 2), (0, 0)))
    grads = projection_grads(d_qkv, after(normed, d_norm1), gain_parts, pieces, block)
    last = scatter_plan(d_norm1.reshape(nb, tok, dim), "blk")
    if strided:
        rounds.add(
            last=last,
            grads=chain(scatter_plan(grads, "uly"), lambda mine: swapped(mine.astype(bf))),
        )
        d_norm1, got, out_grads = rounds.until("last", "grads", "out")
        gain_sums = jnp.sum(got[:, 3 * piece : 3 * piece + 2].astype(f32), axis=0)
        heads = [got[:, i * piece : (i + 1) * piece].reshape(feats_u, rows) for i in range(3)]
    else:
        wanted = grads[0, :, : 3 * piece].reshape(blocks, 3, piece, block)[:, :, :group]
        wanted = jnp.transpose(wanted, (1, 2, 0, 3)).reshape(3, group, nb, rows)
        rounds.add(last=last, grads=swapped(jnp.transpose(wanted, (2, 1, 0, 3))))
        d_norm1, got, out_grads = rounds.until("last", "grads", "out")
        got = scatter(got.reshape(nu, feats_u, 3, rows), "uly")[0]
        heads = [got[:, i] for i in range(3)]
        gain_sums = lax.dynamic_slice_in_dim(lax.psum(gain_parts[:2], both), b * rows, rows, 1)
    grad_output = jnp.transpose(out_grads)
    grad_query, grad_key, grad_value = [jnp.transpose(h).astype(f32) for h in heads]
    x_own = tokens.astype(f32)
    r1_own = rms_scale(x_own)
    z_one = gain1 * d_norm1
    grad_tokens = (
        dx1
        + r1_own * z_one
        - x_own * r1_own * r1_own * r1_own * jnp.mean(z_one * x_own, axis=-1, keepdims=True)
    )
    output = x1_own + mlp_out.astype(f32)
    return (
        output,
        grad_tokens,
        gain_sums[0],
        grad_query,
        grad_key,
        grad_value,
        grad_output,
        gain_sums[1],
        *finish(ff_got),
    )


def solution(mesh):
    tokens_split = P(("blk", "uly"), None)
    weights = P("blk", "uly")
    return jax.shard_map(
        on_device,
        mesh=mesh,
        in_specs=(
            tokens_split,
            P(),
            tokens_split,
            P("blk"),
            weights,
            weights,
            weights,
            weights,
            P("blk"),
            weights,
            weights,
            weights,
        ),
        out_specs=(
            tokens_split,
            tokens_split,
            P("blk"),
            weights,
            weights,
            weights,
            weights,
            P("blk"),
            weights,
            weights,
            weights,
        ),
        check_vma=False,
    )
```

```python
import functools
import math

import jax
import jax.numpy as jnp
from jax import lax
from jax.experimental import pallas as pl
from jax.experimental.pallas import tpu as pltpu
from jax.sharding import PartitionSpec as P

H = 32
HD = 64
LANES = 128
PAD = 16

theta_base = 130000.0
epsilon = 1e-05
bf = jnp.bfloat16
f32 = jnp.float32
NEG = -1e30


def dot_t(left, right):
    return lax.dot_general(left, right, (((1,), (1,)), ((), ())), preferred_element_type=f32)


def dot_n(left, right):
    return jnp.dot(left, right, preferred_element_type=f32)


def dot_c(left, right):
    return lax.dot_general(left, right, (((0,), (0,)), ((), ())), preferred_element_type=f32)


def rms_scale(value):
    return lax.rsqrt(jnp.mean(value * value, axis=-1, keepdims=True) + epsilon)


def params(mib=56):
    return pltpu.CompilerParams(vmem_limit_bytes=mib * 2**20)


def cost(micros):
    return pl.CostEstimate(flops=int(micros * 0.25 * 1.1e9), bytes_accessed=0, transcendentals=0)


def full(shape):
    return pl.BlockSpec(shape, lambda *grid: (0,) * len(shape))


def after(value, *others):
    return lax.optimization_barrier((value, *others))[0]


def hop(value, axis, slow, fast):
    size = lax.axis_size(axis)
    ring = size // 2
    pairs = [(i, ((i // 2 + slow) % ring) * 2 + (i % 2 ^ fast)) for i in range(size)]
    return lax.ppermute(value, axis, pairs)


def near(axis, slow, fast):
    ring = lax.axis_size(axis) // 2
    i = lax.axis_index(axis)
    return ((i // 2 + slow + ring) % ring) * 2 + (i % 2 ^ fast)


def place(out, piece, at):
    return lax.dynamic_update_slice_in_dim(out, piece[None], at, 0)


def pick(parts, at):
    return lax.dynamic_index_in_dim(parts, at, 0, False)


class Rounds:
    def __init__(self):
        self.live, self.results = {}, {}

    def add(self, **plans):
        for name, plan in plans.items():
            self.advance(name, plan, None)

    def advance(self, name, plan, value):
        try:
            self.live[name] = (plan, list(plan.send(value)))
        except StopIteration as end:
            self.live.pop(name, None)
            self.results[name] = end.value

    def round(self, *also):
        waiting = list(self.live.items())
        flat = [v for _, (_, values) in waiting for v in values] + list(also)
        if flat:
            flat = list(lax.optimization_barrier(tuple(flat)))
        for name, (plan, values) in waiting:
            self.advance(name, plan, [flat.pop(0) for _ in values])
        return flat

    def until(self, *names):
        while any(name in self.live for name in names):
            self.round()
        return [self.results[name] for name in names]


def together(*plans):
    rounds = Rounds()
    names = [str(i) for i in range(len(plans))]
    rounds.add(**dict(zip(names, plans)))
    return rounds.until(*names)


def idle(count):
    for _ in range(count):
        yield []


def chain(first, *rest):
    value = yield from first
    for plan in rest:
        value = yield from plan(value)
    return value


def gather_plan(value, axis):
    size = lax.axis_size(axis)
    ring = size // 2
    out = jnp.zeros((size, *value.shape), value.dtype)
    fresh = {0: value}
    crossing = {0: hop(value, axis, 0, 1)}
    for s in range(1, ring // 2 + 1):
        arriving = {-s: hop(fresh[1 - s], axis, 1, 0)}
        if s <= (ring - 1) // 2:
            arriving[s] = hop(fresh[s - 1], axis, -1, 0)
        got = yield [*arriving.values(), *crossing.values()]
        for at, piece in zip(crossing, got[len(arriving) :]):
            out = place(out, piece, near(axis, at, 1))
        fresh = dict(zip(arriving, got))
        for at, piece in fresh.items():
            out = place(out, piece, near(axis, at, 0))
        crossing = {at: hop(piece, axis, 0, 1) for at, piece in fresh.items()}
        if s == 1:
            out = place(out, value, near(axis, 0, 0))
    got = yield list(crossing.values())
    for at, piece in zip(crossing, got):
        out = place(out, piece, near(axis, at, 1))
    return out


def scatter_steps(axis):
    ring = lax.axis_size(axis) // 2
    far, back = ring // 2, (ring - 1) // 2
    steps = [[s] + ([-s] if s <= back else []) for s in range(far, 0, -1)]
    if ring == 4:
        steps = [[2, -1], [1]]
    steps[-1] = steps[-1] + [0]
    return steps


def scatter_order(axis):
    steps = sum(scatter_steps(axis), [])
    return jnp.stack([near(axis, s, fast) for fast in (1, 0) for s in steps]).astype(jnp.int32)


def scatter_plan(parts, axis, ordered=False):
    steps = scatter_steps(axis)
    places = sum(steps, [])

    def part(s, fast):
        if ordered:
            return parts[places.index(s) + (0 if fast else len(places))]
        return pick(parts, near(axis, s, fast))

    def column(offsets, fast):
        if ordered:
            at = places.index(offsets[0])
            return parts[at : at + len(offsets)]
        return jnp.stack([part(s, fast) for s in offsets])

    up = down = None
    for offsets in steps:
        crossed = hop(column(offsets, 1), axis, 0, 1)
        got = yield [crossed, *[v for v in (up, down) if v is not None]]
        crossed, carried = got[0], got[1:]
        totals = {
            s: part(s, 0).astype(f32) + crossed[k].astype(f32)
            for k, s in enumerate(offsets)
        }
        if up is not None:
            up = carried.pop(0).astype(f32)
        if down is not None:
            down = carried.pop(0).astype(f32)
        ups = [s for s in offsets if s > 0]
        downs = [s for s in offsets if s < 0]
        held = down
        if ups:
            total = totals[ups[0]] if up is None else totals[ups[0]] + up
            up = hop(total.astype(bf), axis, 1, 0)
        if downs:
            total = totals[downs[0]] if down is None else totals[downs[0]] + down
            down = hop(total.astype(bf), axis, -1, 0)
            held = None
        own = totals.get(0)
    if held is not None:
        own = own + held
        down = None
    for piece in (yield [v for v in (up, down) if v is not None]):
        own = own + piece.astype(f32)
    return own


def swap_plan(parts, axis):
    ring = lax.axis_size(axis) // 2
    fast = lax.axis_index(axis) % 2
    slow = lax.axis_index(axis) // 2
    columns = jnp.swapaxes(parts.reshape(ring, 2, *parts.shape[1:]), 0, 1)
    kept = pick(columns, fast)
    (given,) = yield [hop(pick(columns, 1 - fast), axis, 0, 1)]
    pairs = jnp.stack([jnp.where(fast == 0, kept, given), jnp.where(fast == 0, given, kept)], 1)
    out = place(jnp.zeros_like(pairs), pick(pairs, slow), slow)
    arrived = yield [hop(pick(pairs, (slow + s) % ring), axis, s, 0) for s in range(1, ring)]
    for s, piece in enumerate(arrived, 1):
        out = place(out, piece, (slow - s + ring) % ring)
    return out.reshape(parts.shape)


def gather_near_plan(value, axis, spare=0):
    ring = lax.axis_size(axis) // 2
    crossed = [hop(value, axis, 0, 1)]
    got = [hop(value, axis, s, 0) for s in range(1, ring)]
    yield from idle(spare)
    got = yield got
    crossed += [hop(piece, axis, 0, 1) for piece in got]
    crossed = yield crossed
    return [value, *got, *crossed]


def scatter_near_plan(parts, axis, spare=0):
    ring = lax.axis_size(axis) // 2
    crossed = yield [hop(part, axis, 0, 1) for part in parts[ring:]]
    sums = [mine.astype(f32) + piece.astype(f32) for mine, piece in zip(parts, crossed)]
    total = sums[0].astype(bf)
    got = [hop(sums[s].astype(bf), axis, -s, 0) for s in range(1, ring)]
    yield from idle(spare)
    total = total.astype(f32)
    for piece in (yield got):
        total = total + piece.astype(f32)
    return total.astype(bf)


def swap(parts, axis):
    return lax.all_to_all(parts, axis, 0, 0, tiled=True)


def gather(value, axis):
    return lax.all_gather(value, axis, axis=0, tiled=True)


def scatter(value, axis):
    return lax.psum_scatter(value, axis, scatter_dimension=0, tiled=True)


def turned(value):
    width = value.shape[1]
    lane = lax.broadcasted_iota(jnp.int32, value.shape, 1)
    return jnp.where(
        lane % HD < HD // 2,
        pltpu.roll(value, width - HD // 2, 1),
        pltpu.roll(value, HD // 2, 1),
    )


def wide(table, width):
    return jnp.concatenate([table] * (width // LANES), axis=1)


def weight_block(w_ref, block, part, piece):
    w = w_ref[:, block, part * piece : (part + 1) * piece, :]
    return w.reshape(w.shape[0] * piece, w.shape[2])


def project_kernel(piece, x_ref, w_ref, cos_ref, sin_ref, q_ref, kv_ref, normed_ref):
    blocks, width = w_ref.shape[1], w_ref.shape[3]
    x = x_ref[...].astype(f32)
    r1 = rms_scale(x)
    total = [0.0, 0.0, 0.0]
    for block in range(blocks):
        at = slice(block * width, (block + 1) * width)
        gain = w_ref[0, block, 3 * piece : 3 * piece + PAD, :][0:1].astype(f32)
        normed = (x[:, at] * r1 * gain).astype(bf)
        normed_ref[:, at] = normed
        for part in range(3):
            total[part] = total[part] + dot_t(normed, weight_block(w_ref, block, part, piece))
    feats = total[0].shape[1]
    cosine, sine = wide(cos_ref[...], feats), wide(sin_ref[...], feats)

    def rotate(value):
        value = value.astype(bf).astype(f32)
        return (value * cosine + turned(value) * sine).astype(bf)

    q_ref[...] = rotate(total[0])
    kv_ref[0] = rotate(total[1])
    kv_ref[1] = total[2].astype(bf)


def project(x_all, w, cosine, sine, piece, rows):
    count, dim = x_all.shape
    feats = w.shape[0] * piece
    tiled = lambda n: pl.BlockSpec((rows, n), lambda i: (i, 0))
    return pl.pallas_call(
        functools.partial(project_kernel, piece),
        grid=(count // rows,),
        in_specs=[tiled(dim), full(w.shape), tiled(LANES), tiled(LANES)],
        out_specs=[
            tiled(feats),
            pl.BlockSpec((2, rows, feats), lambda i: (0, i, 0)),
            tiled(dim),
        ],
        out_shape=[
            jax.ShapeDtypeStruct((count, feats), bf),
            jax.ShapeDtypeStruct((2, count, feats), bf),
            jax.ShapeDtypeStruct((count, dim), bf),
        ],
        compiler_params=params(),
        cost_estimate=cost(count * 0.009),
        name="project",
    )(x_all, w, cosine, sine)


def flip_kernel(piece, q_ref, k_ref, v_ref, o_ref, ga_ref, gm_ref, sent_ref, out_ref):
    size = sent_ref.shape[0]
    for i, ref in enumerate((q_ref, k_ref, v_ref)):
        sent_ref[:, i * piece : (i + 1) * piece, :] = (
            ref[...].T.astype(bf).reshape(size, piece, ref.shape[0])
        )
    row = lax.broadcasted_iota(jnp.int32, (PAD, q_ref.shape[0]), 0)
    gains = jnp.where(row == 0, ga_ref[...], gm_ref[...]).astype(bf)
    for j in range(size):
        sent_ref[j, 3 * piece :, :] = gains
    out_ref[...] = o_ref[...].T.astype(bf)


def flip(w_query, w_key, w_value, w_output, attn_gain, mlp_gain, size):
    rows, feats = w_query.shape
    piece = feats // size
    return pl.pallas_call(
        functools.partial(flip_kernel, piece),
        out_shape=[
            jax.ShapeDtypeStruct((size, 3 * piece + PAD, rows), bf),
            jax.ShapeDtypeStruct((feats, rows), bf),
        ],
        compiler_params=params(),
        cost_estimate=cost(5),
        name="flip",
    )(w_query, w_key, w_value, w_output, attn_gain[None], mlp_gain[None])


def head_lanes(rows, head):
    lane = lax.broadcasted_iota(jnp.int32, (rows, LANES), 1)
    return (lane < HD) if head == 0 else (lane >= HD)


def attend_kernel(tile, low_ref, high_ref, q_ref, kv_ref, o_ref, lse_ref, vt_ref):
    nu, _, nb, tok, feats = kv_ref.shape
    width = nu * tok
    rows = tile * tok
    pairs = feats // LANES
    heads = range(2 * pairs)
    lanes = [slice(h // 2 * LANES, (h // 2 + 1) * LANES) for h in heads]
    j = pl.program_id(0)

    @pl.when(j == 0)
    def _():
        for c in range(nb):
            vt_ref[c] = kv_ref[:, 1, c].reshape(width, feats).T

    low, high = low_ref[0], high_ref[0]
    q = q_ref[...] * jnp.asarray(1.0 / math.sqrt(HD), bf)
    q_heads = [
        jnp.where(head_lanes(rows, h % 2), q[:, lanes[h]], jnp.zeros((rows, LANES), bf))
        for h in heads
    ]
    place_k = lax.broadcasted_iota(jnp.int32, (width, rows), 0)

    def step(chunk, state):
        k = kv_ref[:, 0, chunk].reshape(width, feats)
        start = chunk * width
        ok = (place_k >= low - start) & (place_k <= high - start)
        scores = [jnp.where(ok, dot_t(k[:, lanes[h]], q_heads[h]), NEG) for h in heads]
        new = []
        for h in heads:
            best, total, acc = state[h]
            best_new = jnp.maximum(best, jnp.max(scores[h], axis=0, keepdims=True))
            p = jnp.exp(scores[h] - best_new)
            factor = jnp.exp(best - best_new)
            total = total * factor + jnp.sum(p, axis=0, keepdims=True)
            acc = acc * factor + dot_n(vt_ref[chunk, h * HD : (h + 1) * HD], p.astype(bf))
            new.append((best_new, total, acc))
        return tuple(new)

    start = (
        jnp.full((1, rows), NEG, f32),
        jnp.zeros((1, rows), f32),
        jnp.zeros((HD, rows), f32),
    )
    state = lax.fori_loop(0, (j + 1) * tile, step, (start,) * len(heads))
    o_ref[...] = jnp.concatenate([acc / total for _, total, acc in state], axis=0).T.astype(bf)
    lse_ref[0] = jnp.concatenate([best + jnp.log(total) for best, total, _ in state], axis=0)


def attend(low, high, q, kv, tile):
    nu, _, nb, tok, feats = kv.shape
    rows = tile * tok
    nq = nb // tile
    heads = feats // HD
    row_spec = pl.BlockSpec((1, 1, rows), lambda j: (j, 0, 0))
    q_spec = pl.BlockSpec((rows, feats), lambda j: (j, 0))
    return pl.pallas_call(
        functools.partial(attend_kernel, tile),
        grid=(nq,),
        in_specs=[row_spec, row_spec, q_spec, full(kv.shape)],
        out_specs=[q_spec, pl.BlockSpec((1, heads, rows), lambda j: (j, 0, 0))],
        out_shape=[
            jax.ShapeDtypeStruct((nb * tok, feats), bf),
            jax.ShapeDtypeStruct((nq, heads, rows), f32),
        ],
        scratch_shapes=[pltpu.VMEM((nb, feats, nu * tok), bf)],
        compiler_params=params(),
        cost_estimate=cost(27 * nb * tok * nb / 8192),
        name="attend",
    )(low, high, q, kv)


def attend_back_kernel(
    tile,
    low_ref,
    high_ref,
    cos_ref,
    sin_ref,
    q_ref,
    do_ref,
    o_ref,
    lse_ref,
    kv_ref,
    dq_ref,
    dkv_ref,
    acc_ref,
    delta_ref,
    sums_ref,
):
    nu, _, _, tok, feats = kv_ref.shape
    nq, heads, rows = lse_ref.shape
    width = nu * tok
    pairs = feats // LANES
    chunk = pl.program_id(0)
    scale = jnp.asarray(1.0 / math.sqrt(HD), bf)

    @pl.when(chunk == 0)
    def _():
        acc_ref[...] = jnp.zeros_like(acc_ref)
        lane = lax.broadcasted_iota(jnp.int32, (8, feats), 1)
        row = lax.broadcasted_iota(jnp.int32, (8, feats), 0)
        mine = jnp.where(lane // HD == row, 1.0, 0.0).astype(f32)
        for j in range(nq):
            at = pl.ds(j * rows, rows)
            delta_ref[j] = lax.dot_general(
                mine,
                do_ref[at, :].astype(f32) * o_ref[at, :].astype(f32),
                (((1,), (1,)), ((), ())),
                preferred_element_type=f32,
                precision=lax.Precision.HIGHEST,
            )

    k_all = kv_ref[:, 0, 0].reshape(width, feats)
    v_all = kv_ref[:, 1, 0].reshape(width, feats)
    lanes = [slice(p * LANES, (p + 1) * LANES) for p in range(pairs)]
    k = [k_all[:, at] for at in lanes]
    v = [v_all[:, at] for at in lanes]
    k_turned = [part.T for part in k]
    place_k = lax.broadcasted_iota(jnp.int32, (width, rows), 0)
    start = chunk * width
    sums_ref[...] = jnp.zeros_like(sums_ref)

    def step(j, _):
        at = pl.ds(pl.multiple_of(j * rows, rows), rows)
        q = q_ref[at, :] * scale
        do = do_ref[at, :]
        ok = (place_k >= low_ref[j] - start) & (place_k <= high_ref[j] - start)
        q_heads, do_heads = [
            [
                jnp.where(head_lanes(rows, h % 2), part[:, lanes[h // 2]], jnp.zeros((rows, LANES), bf))
                for h in range(2 * pairs)
            ]
            for part in (q, do)
        ]
        scores = [dot_t(k[h // 2], q_heads[h]) for h in range(2 * pairs)]
        d_probs = [dot_t(v[h // 2], do_heads[h]) for h in range(2 * pairs)]
        for pair in range(pairs):
            dk = dv = 0.0
            dq = []
            for i in range(2):
                h = 2 * pair + i
                p = jnp.exp(jnp.where(ok, scores[h] - lse_ref[j, h : h + 1], NEG))
                ds = (p * (d_probs[h] - delta_ref[j, h : h + 1])).astype(bf)
                dv = dv + dot_n(p.astype(bf), do_heads[h])
                dk = dk + dot_n(ds, q_heads[h])
                dq.append(dot_n(k_turned[pair][i * HD : (i + 1) * HD], ds))
            acc_ref[j, lanes[pair]] = acc_ref[j, lanes[pair]] + jnp.concatenate(dq, axis=0)
            sums_ref[0, pair] = sums_ref[0, pair] + dk
            sums_ref[1, pair] = sums_ref[1, pair] + dv
        return 0

    lax.fori_loop(chunk // tile, nq, step, 0)
    for i in range(2):
        for pair in range(pairs):
            dkv_ref[:, i, 0, :, lanes[pair]] = (
                sums_ref[i, pair].astype(bf).reshape(nu, tok, LANES)
            )

    @pl.when(chunk == pl.num_programs(0) - 1)
    def _():
        dq = jnp.concatenate([acc_ref[j].T for j in range(nq)], axis=0) * (1.0 / math.sqrt(HD))
        cosine, sine = wide(cos_ref[...], feats), wide(sin_ref[...], feats)
        dq_ref[...] = (dq * cosine - turned(dq) * sine).astype(bf)


def attend_back(low, high, cosine, sine, q, do, o, lse, kv, tile):
    nu, _, nb, tok, feats = kv.shape
    rows = tile * tok
    nq = nb // tile
    kv_spec = pl.BlockSpec((nu, 2, 1, tok, feats), lambda c: (0, 0, c, 0, 0))
    return pl.pallas_call(
        functools.partial(attend_back_kernel, tile),
        grid=(nb,),
        in_specs=[
            *[full(part.shape) for part in (low, high, cosine, sine, q, do, o, lse)],
            kv_spec,
        ],
        out_specs=[full(q.shape), kv_spec],
        out_shape=[
            jax.ShapeDtypeStruct(q.shape, bf),
            jax.ShapeDtypeStruct(kv.shape, bf),
        ],
        scratch_shapes=[
            pltpu.VMEM((nq, feats, rows), f32),
            pltpu.VMEM((nq, 8, rows), f32),
            pltpu.VMEM((2, feats // LANES, nu * tok, LANES), f32),
        ],
        compiler_params=params(),
        cost_estimate=cost(41 * nb * tok * nb / 8192),
        name="attend_back",
    )(low, high, cosine, sine, q, do, o, lse, kv)


def output_kernel(x_ref, o_ref, w_ref, gain_ref, x1_ref, normed_ref):
    blocks, pieces, groups, piece, width = w_ref.shape
    square = 0.0
    for block in range(blocks):
        at = slice(block * width, (block + 1) * width)
        total = x_ref[:, at].astype(f32)
        for g in range(groups):
            total = total + dot_n(o_ref[g], w_ref[block, :, g].reshape(pieces * piece, width))
        x1_ref[:, at] = total
        square = square + jnp.sum(total * total, axis=1, keepdims=True)
    r2 = lax.rsqrt(square * (1.0 / (blocks * width)) + epsilon)
    normed_ref[...] = (x1_ref[...] * r2 * gain_ref[...]).astype(bf)


def output_project(x_all, o_all, w_out, gain, rows):
    count, dim = x_all.shape
    groups, _, feats = o_all.shape
    tiled = pl.BlockSpec((rows, dim), lambda i: (i, 0))
    return pl.pallas_call(
        output_kernel,
        grid=(count // rows,),
        in_specs=[
            tiled,
            pl.BlockSpec((groups, rows, feats), lambda i: (0, i, 0)),
            full(w_out.shape),
            full(gain.shape),
        ],
        out_specs=[tiled, tiled],
        out_shape=[
            jax.ShapeDtypeStruct((count, dim), f32),
            jax.ShapeDtypeStruct((count, dim), bf),
        ],
        compiler_params=params(),
        cost_estimate=cost(count * 0.015),
        name="output_project",
    )(x_all, o_all, w_out, gain)


def output_back_kernel(d_ref, w_ref, out_ref):
    blocks, pieces, _, piece, width = w_ref.shape
    total = 0.0
    for block in range(blocks):
        at = slice(block * width, (block + 1) * width)
        total = total + dot_t(d_ref[:, at], w_ref[block, :, 0].reshape(pieces * piece, width))
    out_ref[0] = total.astype(bf)


def output_back(d_attn, w_out):
    tok, dim = d_attn.shape
    blocks, pieces, groups, piece, width = w_out.shape
    return pl.pallas_call(
        output_back_kernel,
        grid=(groups,),
        in_specs=[
            full(d_attn.shape),
            pl.BlockSpec((blocks, pieces, 1, piece, width), lambda g: (0, 0, g, 0, 0)),
        ],
        out_specs=pl.BlockSpec((1, tok, pieces * piece), lambda g: (g, 0, 0)),
        out_shape=jax.ShapeDtypeStruct((groups, tok, pieces * piece), bf),
        compiler_params=params(),
        cost_estimate=cost(8),
        name="output_back",
    )(d_attn, w_out)


def project_back_kernel(
    piece, _, x_ref, w_ref, cos_ref, sin_ref, dq_ref, dkv_ref, all_ref, dn_ref, gain_ref
):
    blocks, width = w_ref.shape[1], w_ref.shape[3]
    feats = dq_ref.shape[1]
    cosine, sine = wide(cos_ref[...], feats), wide(sin_ref[...], feats)
    dk = dkv_ref[0].astype(f32)
    parts = (
        dq_ref[...],
        (dk * cosine - turned(dk) * sine).astype(bf),
        dkv_ref[1],
    )
    for i in range(3):
        all_ref[i] = parts[i]
    x = x_ref[...].astype(f32)
    r1 = rms_scale(x)

    @pl.when(pl.program_id(0) == 0)
    def _():
        gain_ref[...] = jnp.zeros_like(gain_ref)

    for block in range(blocks):
        at = slice(block * width, (block + 1) * width)
        total = 0.0
        for part in range(3):
            total = total + dot_n(parts[part], weight_block(w_ref, block, part, piece))
        dn_ref[0, :, at] = total.astype(bf)
        gain_ref[:, at] = gain_ref[:, at] + jnp.sum(total * (x[:, at] * r1), axis=0, keepdims=True)


def project_back(x_all, w, cosine, sine, dq, dkv, piece, order):
    count, dim = x_all.shape
    size = order.shape[0]
    rows = count // size
    feats = dq.shape[1]
    tiled = lambda width: pl.BlockSpec((rows, width), lambda i, at: (at[i], 0))
    return pl.pallas_call(
        functools.partial(project_back_kernel, piece),
        grid_spec=pltpu.PrefetchScalarGridSpec(
            num_scalar_prefetch=1,
            grid=(size,),
            in_specs=[
                tiled(dim),
                full(w.shape),
                tiled(LANES),
                tiled(LANES),
                tiled(feats),
                pl.BlockSpec((2, rows, feats), lambda i, at: (0, at[i], 0)),
            ],
            out_specs=[
                pl.BlockSpec((3, rows, feats), lambda i, at: (0, at[i], 0)),
                pl.BlockSpec((1, rows, dim), lambda i, _: (i, 0, 0)),
                full((1, dim)),
            ],
        ),
        out_shape=[
            jax.ShapeDtypeStruct((3, count, feats), bf),
            jax.ShapeDtypeStruct((size, rows, dim), bf),
            jax.ShapeDtypeStruct((1, dim), f32),
        ],
        compiler_params=params(),
        cost_estimate=cost(count * 0.01),
        name="project_back",
    )(order, x_all, w, cosine, sine, dq, dkv)


def projection_grads_kernel(left_ref, right_ref, gain_ref, out_ref, turned_ref):
    n, feats, _ = turned_ref.shape
    pieces = out_ref.shape[0]

    @pl.when(pl.program_id(0) == 0)
    def _():
        for i in range(n):
            turned_ref[i] = left_ref[i].T

    piece = feats // pieces
    right = right_ref[...]
    width = right.shape[1]
    for i in range(n):
        grad = dot_n(turned_ref[i], right).astype(bf)
        out_ref[:, 0, i * piece : (i + 1) * piece, :] = grad.reshape(pieces, piece, width)
    gain = gain_ref[...].astype(bf)
    for u in range(pieces):
        out_ref[u, 0, n * piece :, :] = gain


def projection_grads(lefts, right, gain, pieces, width):
    n, count, feats = lefts.shape
    dim = right.shape[1]
    rows = n * (feats // pieces) + PAD
    return pl.pallas_call(
        projection_grads_kernel,
        grid=(dim // width,),
        in_specs=[
            full(lefts.shape),
            pl.BlockSpec((count, width), lambda i: (0, i)),
            pl.BlockSpec((PAD, width), lambda i: (0, i)),
        ],
        out_specs=pl.BlockSpec((pieces, 1, rows, width), lambda i: (0, i, 0, 0)),
        out_shape=jax.ShapeDtypeStruct((pieces, dim // width, rows, width), bf),
        scratch_shapes=[pltpu.VMEM((n, feats, count), bf)],
        compiler_params=params(),
        cost_estimate=cost(2.5 * n),
        name="projection_grads",
    )(lefts, right, gain)


def output_grads_kernel(o_ref, d_ref, out_ref):
    pieces, _, piece, width = out_ref.shape
    grad = dot_n(o_ref[0].T, d_ref[...])
    out_ref[:, 0] = grad.astype(bf).reshape(pieces, piece, width)


def output_grads(o_all, d_columns, pieces):
    groups, count, feats = o_all.shape
    width = d_columns.shape[1]
    shape = (pieces, groups, feats // pieces, width)
    return pl.pallas_call(
        output_grads_kernel,
        grid=(groups,),
        in_specs=[
            pl.BlockSpec((1, count, feats), lambda g: (g, 0, 0)),
            full(d_columns.shape),
        ],
        out_specs=pl.BlockSpec((pieces, 1, *shape[2:]), lambda g: (0, g, 0, 0)),
        out_shape=jax.ShapeDtypeStruct(shape, bf),
        compiler_params=params(),
        cost_estimate=cost(6),
        name="output_grads",
    )(o_all, d_columns)


def prepare_kernel(wg_ref, wu_ref, wd_ref, out_ref):
    for i, ref in enumerate((wg_ref, wu_ref, wd_ref)):
        out_ref[0, i] = ref[...].astype(bf)


def prepare(w_gate, w_up, w_down, size):
    rows, columns = w_gate.shape
    width = columns // size
    if width % LANES:
        stacked = jnp.stack([w.astype(bf) for w in (w_gate, w_up, w_down)])
        return jnp.transpose(stacked.reshape(3, rows, size, width), (2, 0, 1, 3))
    spec = pl.BlockSpec((rows, width), lambda i: (0, i))
    return pl.pallas_call(
        prepare_kernel,
        grid=(size,),
        in_specs=[spec] * 3,
        out_specs=pl.BlockSpec((1, 3, rows, width), lambda i: (i, 0, 0, 0)),
        out_shape=jax.ShapeDtypeStruct((size, 3, rows, width), bf),
        compiler_params=params(),
        cost_estimate=cost(4),
        name="prepare",
    )(w_gate, w_up, w_down)


def finish_kernel(in_ref, *outs):
    n, _, _, width = in_ref.shape
    for k in range(n):
        for i in range(3):
            outs[i][:, k * width : (k + 1) * width] = in_ref[k, i].astype(f32)


def finish(parts):
    n, _, rows, width = parts.shape
    if width % LANES:
        out = jnp.transpose(parts, (1, 2, 0, 3)).reshape(3, rows, n * width).astype(f32)
        return [out[i] for i in range(3)]
    return pl.pallas_call(
        finish_kernel,
        out_shape=[jax.ShapeDtypeStruct((rows, n * width), f32)] * 3,
        compiler_params=params(),
        cost_estimate=cost(5),
        name="finish",
    )(parts)


def whole_weight(ref, k):
    w = ref[:, k]
    return w.reshape(w.shape[0] * w.shape[1], w.shape[2])


def hidden_kernel(n, *refs):
    n_ref, g_ref = refs[:2]
    act_ref, dg_ref, du_ref = refs[2 + n :]
    normed, cot = n_ref[...], g_ref[...]
    for i in range(n):
        w_ref = refs[2 + i]
        gate = dot_n(normed, whole_weight(w_ref, 0))
        up = dot_n(normed, whole_weight(w_ref, 1))
        d_act = dot_n(cot, whole_weight(w_ref, 2))
        sigma = jax.nn.sigmoid(gate)
        silu = gate * sigma
        act_ref[i] = (silu * up).astype(bf)
        du_ref[i] = (d_act * silu).astype(bf)
        dg_ref[i] = (d_act * up * (sigma * (1.0 + gate * (1.0 - sigma)))).astype(bf)


def hidden(normed, cot, weights, rows):
    count, dim = normed.shape
    n = len(weights)
    width = weights[0].shape[3]
    tiled = pl.BlockSpec((rows, dim), lambda i: (i, 0))
    out = pl.BlockSpec((n, rows, width), lambda i: (0, i, 0))
    return pl.pallas_call(
        functools.partial(hidden_kernel, n),
        grid=(count // rows,),
        in_specs=[tiled, tiled] + [full(w.shape) for w in weights],
        out_specs=[out] * 3,
        out_shape=[jax.ShapeDtypeStruct((n, count, width), bf)] * 3,
        compiler_params=params(),
        cost_estimate=cost(20),
        name="hidden",
    )(normed, cot, *weights)


def mix_kernel(which, n, _, *refs):
    m = len(which)
    lefts, weights, out_ref = refs[: 2 * m], refs[2 * m : -1], refs[-1]
    total = 0.0
    for k in range(m):
        for i in range(n):
            left = jnp.concatenate([lefts[2 * k][i], lefts[2 * k + 1][i]], axis=0)
            total = total + dot_t(left, whole_weight(weights[i], k))
    out_ref[...] = total.astype(bf).reshape(out_ref.shape)


def mix(lefts, weights, which, order):
    n, count, width = lefts[0].shape
    size = order.shape[0]
    rows = count // size
    blocks, _, rows_w, _ = weights[0].shape
    dim = blocks * rows_w
    chosen = pl.BlockSpec(
        (blocks, len(which), rows_w, width), lambda i, _: (0, which[0] // len(which), 0, 0)
    )
    pair = [
        pl.BlockSpec((n, rows, width), lambda i, at: (0, at[2 * i], 0)),
        pl.BlockSpec((n, rows, width), lambda i, at: (0, at[2 * i + 1], 0)),
    ]
    return pl.pallas_call(
        functools.partial(mix_kernel, which, n),
        grid_spec=pltpu.PrefetchScalarGridSpec(
            num_scalar_prefetch=1,
            grid=(size // 2,),
            in_specs=pair * len(which) + [chosen] * n,
            out_specs=pl.BlockSpec((2, rows, dim), lambda i, _: (i, 0, 0)),
        ),
        out_shape=jax.ShapeDtypeStruct((size, rows, dim), bf),
        compiler_params=params(),
        cost_estimate=cost(8 * len(which)),
        name="mix",
    )(order, *[left for left in lefts for _ in range(2)], *weights)


def hidden_grads_kernel(n_ref, g_ref, dg_ref, du_ref, act_ref, *outs):
    normed, cot = n_ref[...].T, g_ref[...].T
    for i, out_ref in enumerate(outs):
        for k, grad in enumerate(
            (dot_n(normed, dg_ref[i]), dot_n(normed, du_ref[i]), dot_n(cot, act_ref[i]))
        ):
            out_ref[:, k] = grad.astype(bf).reshape(out_ref.shape[0], *out_ref.shape[2:])


def hidden_grads(normed, cot, d_gate, d_up, act, rows):
    count, dim = normed.shape
    block = max(rows, LANES)
    n, _, width = act.shape
    columns = pl.BlockSpec((count, block), lambda i: (0, i))
    return pl.pallas_call(
        hidden_grads_kernel,
        grid=(dim // block,),
        in_specs=[columns, columns] + [full(act.shape)] * 3,
        out_specs=[pl.BlockSpec((block // rows, 3, rows, width), lambda i: (i, 0, 0, 0))] * n,
        out_shape=[jax.ShapeDtypeStruct((dim // rows, 3, rows, width), bf)] * n,
        compiler_params=params(),
        cost_estimate=cost(25),
        name="hidden_grads",
    )(normed, cot, d_gate, d_up, act)


def on_device(
    tokens,
    segments,
    cotangent,
    attn_gain,
    w_query,
    w_key,
    w_value,
    w_output,
    mlp_gain,
    w_gate,
    w_up,
    w_down,
):
    nb, nu = lax.axis_size("blk"), lax.axis_size("uly")
    b, u = lax.axis_index("blk"), lax.axis_index("uly")
    tok, dim = tokens.shape
    seq = segments.shape[0]
    rows, feats_u = w_query.shape
    group = feats_u * nu // nb
    strided = (feats_u // HD) % nb == 0 and rows % LANES == 0
    count = nb * tok
    tile = 2
    both = ("blk", "uly")
    block = rows if strided else 2 * LANES
    blocks = dim // block
    pieces = nu if strided else 1
    piece = group // nu if strided else -(-group // LANES) * LANES
    feats = pieces * piece
    step = 2 * tok

    seg_mine = pick(jnp.swapaxes(segments.reshape(nb, nu, tok), 0, 1), u).reshape(count)
    index = (
        jnp.arange(nb, dtype=jnp.int32)[:, None] * (nu * tok)
        + u * tok
        + jnp.arange(tok, dtype=jnp.int32)[None, :]
    ).reshape(count)
    first = jnp.sum((segments[None, :] < seg_mine[:, None]).astype(jnp.int32), axis=1)
    lane = jnp.arange(LANES, dtype=jnp.int32)
    freq = theta_base ** (-((lane % (HD // 2)).astype(f32) * 2.0) / HD)
    angles = (index - first).astype(f32)[:, None] * freq[None, :]
    cosine = jnp.cos(angles)
    sine = jnp.sin(angles) * jnp.where(lane % HD < HD // 2, -1.0, 1.0)[None, :]
    low = first.reshape(nb // tile, 1, tile * tok)
    high = index.reshape(nb // tile, 1, tile * tok)

    ff_u = w_gate.shape[1]
    ff_piece = ff_u // nb
    tokens_plan = gather_plan(tokens, "blk")

    def prepared():
        yield []
        (value,) = yield [prepare(w_gate, w_up, w_down, nb)]
        return value

    def swapped(parts, spare=0):
        got = swap(parts, "blk")
        yield from idle(spare)
        (got,) = yield [got]
        return got

    if strided:
        sent, out_flipped = flip(w_query, w_key, w_value, w_output, attn_gain, mlp_gain, nb)
        x_all, ff_sent, w_qkv = together(
            tokens_plan,
            prepared(),
            chain(swapped(sent, 1), lambda got: gather_plan(got, "uly")),
        )
    else:
        gains = jnp.stack([attn_gain, mlp_gain]).astype(bf)
        flipped = [jnp.transpose(w.astype(bf)) for w in (w_query, w_key, w_value, w_output)]
        out_flipped = flipped[3]
        sent = gather(jnp.stack(flipped[:3])[None], "uly")
        sent = jnp.transpose(sent, (0, 2, 1, 3)).reshape(nb, group, 3, rows)
        x_all, ff_sent, got = together(tokens_plan, prepared(), swapped(sent))
        got = jnp.transpose(got, (2, 1, 0, 3)).reshape(3, group, dim)
        got = jnp.pad(got, ((0, 0), (0, piece - group), (0, 0))).reshape(3 * piece, dim)
        all_gains = jnp.transpose(gather(gains[None], "blk"), (1, 0, 2)).reshape(2, dim)
        got = jnp.concatenate([got, jnp.pad(all_gains, ((0, PAD - 2), (0, 0)))])
        w_qkv = jnp.transpose(got.reshape(3 * piece + PAD, blocks, block), (1, 0, 2))[None]
    x_all = x_all.reshape(count, dim)
    gain1, gain2 = [
        w_qkv[0, :, 3 * piece + i, :].reshape(1, dim).astype(f32) for i in range(2)
    ]

    ff_got = swap(after(ff_sent, x_all), "blk")
    w_out = gather(after(out_flipped, x_all)[None], both)
    cot_all = gather(after(cotangent, x_all, w_out), "blk")
    if strided:
        w_out = w_out.reshape(nb, nu, nb, piece, rows)
    else:
        w_out = jnp.transpose(w_out.reshape(nb, nu * feats_u, rows), (1, 0, 2))
        w_out = jnp.pad(
            w_out.reshape(nb, group, dim), ((0, 0), (0, piece - group), (0, 0))
        )
        w_out = jnp.transpose(w_out.reshape(nb, piece, blocks, block), (2, 0, 1, 3))[:, None]

    q, kv, normed = project(x_all, w_qkv, cosine, sine, piece, step)
    (kv_all,) = together(gather_plan(kv.reshape(2, nb, tok, feats), "uly"))
    o, lse = attend(low, high, q, kv_all, tile)
    ff_got, o = lax.optimization_barrier((ff_got, o))
    rounds = Rounds()
    rounds.add(o=gather_plan(o, "blk"), ff=gather_near_plan(ff_got, "uly", nb // 4))
    (o_all,) = rounds.until("o")
    x1, normed2 = output_project(x_all, o_all, w_out, gain2, step)

    (w_ff,) = rounds.until("ff")

    act, d_gate, d_up = hidden(normed2, cot_all, w_ff, step)
    order, plain = scatter_order("blk"), jnp.arange(nb, dtype=jnp.int32)
    d_norm2 = mix([d_gate, d_up], w_ff, (0, 1), order)

    def mlp_plan():
        yield []
        (out,) = yield [mix([act], w_ff, (2,), plain)]
        return out

    def hidden_grads_plan():
        grads = yield hidden_grads(
            after(normed2, d_norm2), cot_all, d_gate, d_up, act, rows
        )
        return (yield from scatter_near_plan(grads, "uly", 2 * nb))

    rounds = Rounds()
    rounds.add(
        d_norm2=scatter_plan(d_norm2, "blk", True),
        mlp=mlp_plan(),
        ff=hidden_grads_plan(),
    )
    d_norm2, mlp_out = rounds.until("d_norm2", "mlp")
    x1_own = lax.dynamic_slice_in_dim(x1, b * tok, tok, 0)
    mlp_out = scatter(after(mlp_out, d_norm2).reshape(count, dim), "blk")
    r2_own = rms_scale(x1_own)
    gain2_part = jnp.sum(d_norm2 * x1_own * r2_own, axis=0, keepdims=True)
    z_two = gain2 * d_norm2
    dx1 = (
        cotangent.astype(f32)
        + r2_own * z_two
        - x1_own * r2_own * r2_own * r2_own * jnp.mean(z_two * x1_own, axis=-1, keepdims=True)
    )
    d_attn = dx1.astype(bf)

    d_o = output_back(d_attn, w_out)
    d_columns = jnp.transpose(d_attn.reshape(tok, nb, rows), (1, 0, 2))
    rounds.add(d_o=swap_plan(d_o, "blk"))
    (got,) = rounds.until("d_o")
    d_o = got.reshape(count, feats)
    d_columns = swap(after(d_columns, d_o), "blk")
    dq, dkv = attend_back(low, high, cosine, sine, q, d_o, o, lse, kv_all, tile)
    dkv, mlp_out, d_columns = lax.optimization_barrier((dkv, mlp_out, d_columns))
    rounds.add(dkv=scatter_plan(dkv, "uly"))
    (ff_mine,) = rounds.until("ff")
    ff_got = swap(ff_mine, "blk")
    out_grads = output_grads(o_all, d_columns.reshape(count, rows), pieces)
    if not strided:
        out_grads = out_grads[:, :, :group]
    (dkv,) = rounds.until("dkv")
    dkv, out_grads = lax.optimization_barrier((dkv, out_grads))
    rounds.add(out=scatter_plan(out_grads.reshape(nu, feats_u, rows), "uly"))
    dkv = dkv.astype(bf).reshape(2, count, feats)
    d_qkv, d_norm1, gain1_part = project_back(x_all, w_qkv, cosine, sine, dq, dkv, piece, order)
    gain_parts = jnp.pad(jnp.concatenate([gain1_part, gain2_part]), ((0, PAD - 2), (0, 0)))
    grads = projection_grads(d_qkv, after(normed, d_norm1), gain_parts, pieces, block)
    last = scatter_plan(d_norm1, "blk", True)
    if strided:
        rounds.add(
            last=last,
            grads=chain(scatter_plan(grads, "uly"), lambda mine: swapped(mine.astype(bf))),
        )
        d_norm1, got, out_grads = rounds.until("last", "grads", "out")
        gain_sums = jnp.sum(got[:, 3 * piece : 3 * piece + 2].astype(f32), axis=0)
        heads = [got[:, i * piece : (i + 1) * piece].reshape(feats_u, rows) for i in range(3)]
    else:
        wanted = grads[0, :, : 3 * piece].reshape(blocks, 3, piece, block)[:, :, :group]
        wanted = jnp.transpose(wanted, (1, 2, 0, 3)).reshape(3, group, nb, rows)
        rounds.add(last=last, grads=swapped(jnp.transpose(wanted, (2, 1, 0, 3))))
        d_norm1, got, out_grads = rounds.until("last", "grads", "out")
        got = scatter(got.reshape(nu, feats_u, 3, rows), "uly")[0]
        heads = [got[:, i] for i in range(3)]
        gain_sums = lax.dynamic_slice_in_dim(lax.psum(gain_parts[:2], both), b * rows, rows, 1)
    grad_output = jnp.transpose(out_grads)
    grad_query, grad_key, grad_value = [jnp.transpose(h).astype(f32) for h in heads]
    x_own = tokens.astype(f32)
    r1_own = rms_scale(x_own)
    z_one = gain1 * d_norm1
    grad_tokens = (
        dx1
        + r1_own * z_one
        - x_own * r1_own * r1_own * r1_own * jnp.mean(z_one * x_own, axis=-1, keepdims=True)
    )
    output = x1_own + mlp_out.astype(f32)
    return (
        output,
        grad_tokens,
        gain_sums[0],
        grad_query,
        grad_key,
        grad_value,
        grad_output,
        gain_sums[1],
        *finish(ff_got),
    )


def solution(mesh):
    tokens_split = P(("blk", "uly"), None)
    weights = P("blk", "uly")
    return jax.shard_map(
        on_device,
        mesh=mesh,
        in_specs=(
            tokens_split,
            P(),
            tokens_split,
            P("blk"),
            weights,
            weights,
            weights,
            weights,
            P("blk"),
            weights,
            weights,
            weights,
        ),
        out_specs=(
            tokens_split,
            tokens_split,
            P("blk"),
            weights,
            weights,
            weights,
            weights,
            P("blk"),
            weights,
            weights,
            weights,
        ),
        check_vma=False,
    )
```

```python
import functools
import math

import jax
import jax.numpy as jnp
from jax import lax
from jax.experimental import pallas as pl
from jax.experimental.pallas import tpu as pltpu
from jax.sharding import PartitionSpec as P

H = 32
HD = 64
LANES = 128
PAD = 16

theta_base = 130000.0
epsilon = 1e-05
bf = jnp.bfloat16
f32 = jnp.float32
NEG = -1e30


def dot_t(left, right):
    return lax.dot_general(left, right, (((1,), (1,)), ((), ())), preferred_element_type=f32)


def dot_n(left, right):
    return jnp.dot(left, right, preferred_element_type=f32)


def dot_c(left, right):
    return lax.dot_general(left, right, (((0,), (0,)), ((), ())), preferred_element_type=f32)


def rms_scale(value):
    return lax.rsqrt(jnp.mean(value * value, axis=-1, keepdims=True) + epsilon)


def params(mib=56):
    return pltpu.CompilerParams(vmem_limit_bytes=mib * 2**20)


def cost(micros):
    return pl.CostEstimate(flops=int(micros * 0.25 * 1.1e9), bytes_accessed=0, transcendentals=0)


def full(shape):
    return pl.BlockSpec(shape, lambda *grid: (0,) * len(shape))


def after(value, *others):
    return lax.optimization_barrier((value, *others))[0]


def hop(value, axis, slow, fast):
    size = lax.axis_size(axis)
    ring = size // 2
    pairs = [(i, ((i // 2 + slow) % ring) * 2 + (i % 2 ^ fast)) for i in range(size)]
    return lax.ppermute(value, axis, pairs)


def near(axis, slow, fast):
    ring = lax.axis_size(axis) // 2
    i = lax.axis_index(axis)
    return ((i // 2 + slow + ring) % ring) * 2 + (i % 2 ^ fast)


def place(out, piece, at):
    return lax.dynamic_update_slice_in_dim(out, piece[None], at, 0)


def pick(parts, at):
    return lax.dynamic_index_in_dim(parts, at, 0, False)


class Rounds:
    def __init__(self):
        self.live, self.results = {}, {}

    def add(self, **plans):
        for name, plan in plans.items():
            self.advance(name, plan, None)

    def advance(self, name, plan, value):
        try:
            self.live[name] = (plan, list(plan.send(value)))
        except StopIteration as end:
            self.live.pop(name, None)
            self.results[name] = end.value

    def round(self, *also):
        waiting = list(self.live.items())
        flat = [v for _, (_, values) in waiting for v in values] + list(also)
        if flat:
            flat = list(lax.optimization_barrier(tuple(flat)))
        for name, (plan, values) in waiting:
            self.advance(name, plan, [flat.pop(0) for _ in values])
        return flat

    def until(self, *names):
        while any(name in self.live for name in names):
            self.round()
        return [self.results[name] for name in names]


def together(*plans):
    rounds = Rounds()
    names = [str(i) for i in range(len(plans))]
    rounds.add(**dict(zip(names, plans)))
    return rounds.until(*names)


def idle(count):
    for _ in range(count):
        yield []


def chain(first, *rest):
    value = yield from first
    for plan in rest:
        value = yield from plan(value)
    return value


def gather_plan(value, axis):
    size = lax.axis_size(axis)
    ring = size // 2
    out = jnp.zeros((size, *value.shape), value.dtype)
    fresh = {0: value}
    crossing = {0: hop(value, axis, 0, 1)}
    for s in range(1, ring // 2 + 1):
        arriving = {-s: hop(fresh[1 - s], axis, 1, 0)}
        if s <= (ring - 1) // 2:
            arriving[s] = hop(fresh[s - 1], axis, -1, 0)
        got = yield [*arriving.values(), *crossing.values()]
        for at, piece in zip(crossing, got[len(arriving) :]):
            out = place(out, piece, near(axis, at, 1))
        fresh = dict(zip(arriving, got))
        for at, piece in fresh.items():
            out = place(out, piece, near(axis, at, 0))
        crossing = {at: hop(piece, axis, 0, 1) for at, piece in fresh.items()}
        if s == 1:
            out = place(out, value, near(axis, 0, 0))
    got = yield list(crossing.values())
    for at, piece in zip(crossing, got):
        out = place(out, piece, near(axis, at, 1))
    return out


def scatter_steps(axis):
    ring = lax.axis_size(axis) // 2
    far, back = ring // 2, (ring - 1) // 2
    steps = [[s] + ([-s] if s <= back else []) for s in range(far, 0, -1)]
    if ring == 4:
        steps = [[2, -1], [1]]
    steps[-1] = steps[-1] + [0]
    return steps


def scatter_order(axis):
    steps = sum(scatter_steps(axis), [])
    return jnp.stack([near(axis, s, fast) for fast in (1, 0) for s in steps]).astype(jnp.int32)


def scatter_plan(parts, axis, ordered=False):
    steps = scatter_steps(axis)
    places = sum(steps, [])

    def part(s, fast):
        if ordered:
            return parts[places.index(s) + (0 if fast else len(places))]
        return pick(parts, near(axis, s, fast))

    def column(offsets, fast):
        if ordered:
            at = places.index(offsets[0])
            return parts[at : at + len(offsets)]
        return jnp.stack([part(s, fast) for s in offsets])

    up = down = None
    for offsets in steps:
        crossed = hop(column(offsets, 1), axis, 0, 1)
        got = yield [crossed, *[v for v in (up, down) if v is not None]]
        crossed, carried = got[0], got[1:]
        totals = {
            s: part(s, 0).astype(f32) + crossed[k].astype(f32)
            for k, s in enumerate(offsets)
        }
        if up is not None:
            up = carried.pop(0).astype(f32)
        if down is not None:
            down = carried.pop(0).astype(f32)
        ups = [s for s in offsets if s > 0]
        downs = [s for s in offsets if s < 0]
        held = down
        if ups:
            total = totals[ups[0]] if up is None else totals[ups[0]] + up
            up = hop(total.astype(bf), axis, 1, 0)
        if downs:
            total = totals[downs[0]] if down is None else totals[downs[0]] + down
            down = hop(total.astype(bf), axis, -1, 0)
            held = None
        own = totals.get(0)
    if held is not None:
        own = own + held
        down = None
    for piece in (yield [v for v in (up, down) if v is not None]):
        own = own + piece.astype(f32)
    return own


def swap_plan(parts, axis):
    ring = lax.axis_size(axis) // 2
    fast = lax.axis_index(axis) % 2
    slow = lax.axis_index(axis) // 2
    columns = jnp.swapaxes(parts.reshape(ring, 2, *parts.shape[1:]), 0, 1)
    kept = pick(columns, fast)
    (given,) = yield [hop(pick(columns, 1 - fast), axis, 0, 1)]
    pairs = jnp.stack([jnp.where(fast == 0, kept, given), jnp.where(fast == 0, given, kept)], 1)
    out = place(jnp.zeros_like(pairs), pick(pairs, slow), slow)
    arrived = yield [hop(pick(pairs, (slow + s) % ring), axis, s, 0) for s in range(1, ring)]
    for s, piece in enumerate(arrived, 1):
        out = place(out, piece, (slow - s + ring) % ring)
    return out.reshape(parts.shape)


def gather_near_plan(value, axis, spare=0):
    ring = lax.axis_size(axis) // 2
    crossed = [hop(value, axis, 0, 1)]
    got = [hop(value, axis, s, 0) for s in range(1, ring)]
    yield from idle(spare)
    got = yield got
    crossed += [hop(piece, axis, 0, 1) for piece in got]
    crossed = yield crossed
    return [value, *got, *crossed]


def scatter_near_plan(parts, axis, spare=0):
    ring = lax.axis_size(axis) // 2
    crossed = yield [hop(part, axis, 0, 1) for part in parts[ring:]]
    sums = [mine.astype(f32) + piece.astype(f32) for mine, piece in zip(parts, crossed)]
    total = sums[0].astype(bf)
    got = [hop(sums[s].astype(bf), axis, -s, 0) for s in range(1, ring)]
    yield from idle(spare)
    total = total.astype(f32)
    for piece in (yield got):
        total = total + piece.astype(f32)
    return total.astype(bf)


def swap(parts, axis):
    return lax.all_to_all(parts, axis, 0, 0, tiled=True)


def gather(value, axis):
    return lax.all_gather(value, axis, axis=0, tiled=True)


def scatter(value, axis):
    return lax.psum_scatter(value, axis, scatter_dimension=0, tiled=True)


def turned(value):
    width = value.shape[1]
    lane = lax.broadcasted_iota(jnp.int32, value.shape, 1)
    return jnp.where(
        lane % HD < HD // 2,
        pltpu.roll(value, width - HD // 2, 1),
        pltpu.roll(value, HD // 2, 1),
    )


def wide(table, width):
    return jnp.concatenate([table] * (width // LANES), axis=1)


def weight_block(w_ref, block, part, piece):
    w = w_ref[:, block, part * piece : (part + 1) * piece, :]
    return w.reshape(w.shape[0] * piece, w.shape[2])


def project_kernel(piece, x_ref, w_ref, cos_ref, sin_ref, q_ref, kv_ref, normed_ref):
    blocks, width = w_ref.shape[1], w_ref.shape[3]
    x = x_ref[...].astype(f32)
    r1 = rms_scale(x)
    total = [0.0, 0.0, 0.0]
    for block in range(blocks):
        at = slice(block * width, (block + 1) * width)
        gain = w_ref[0, block, 3 * piece : 3 * piece + PAD, :][0:1].astype(f32)
        normed = (x[:, at] * r1 * gain).astype(bf)
        normed_ref[:, at] = normed
        for part in range(3):
            total[part] = total[part] + dot_t(normed, weight_block(w_ref, block, part, piece))
    feats = total[0].shape[1]
    cosine, sine = wide(cos_ref[...], feats), wide(sin_ref[...], feats)

    def rotate(value):
        value = value.astype(bf).astype(f32)
        return (value * cosine + turned(value) * sine).astype(bf)

    q_ref[...] = rotate(total[0])
    kv_ref[0] = rotate(total[1])
    kv_ref[1] = total[2].astype(bf)


def project(x_all, w, cosine, sine, piece, rows):
    count, dim = x_all.shape
    feats = w.shape[0] * piece
    tiled = lambda n: pl.BlockSpec((rows, n), lambda i: (i, 0))
    return pl.pallas_call(
        functools.partial(project_kernel, piece),
        grid=(count // rows,),
        in_specs=[tiled(dim), full(w.shape), tiled(LANES), tiled(LANES)],
        out_specs=[
            tiled(feats),
            pl.BlockSpec((2, rows, feats), lambda i: (0, i, 0)),
            tiled(dim),
        ],
        out_shape=[
            jax.ShapeDtypeStruct((count, feats), bf),
            jax.ShapeDtypeStruct((2, count, feats), bf),
            jax.ShapeDtypeStruct((count, dim), bf),
        ],
        compiler_params=params(),
        cost_estimate=cost(count * 0.009),
        name="project",
    )(x_all, w, cosine, sine)


def flip_kernel(piece, q_ref, k_ref, v_ref, o_ref, ga_ref, gm_ref, sent_ref, out_ref):
    size = sent_ref.shape[0]
    for i, ref in enumerate((q_ref, k_ref, v_ref)):
        sent_ref[:, i * piece : (i + 1) * piece, :] = (
            ref[...].T.astype(bf).reshape(size, piece, ref.shape[0])
        )
    row = lax.broadcasted_iota(jnp.int32, (PAD, q_ref.shape[0]), 0)
    gains = jnp.where(row == 0, ga_ref[...], gm_ref[...]).astype(bf)
    for j in range(size):
        sent_ref[j, 3 * piece :, :] = gains
    out_ref[...] = o_ref[...].T.astype(bf)


def flip(w_query, w_key, w_value, w_output, attn_gain, mlp_gain, size):
    rows, feats = w_query.shape
    piece = feats // size
    return pl.pallas_call(
        functools.partial(flip_kernel, piece),
        out_shape=[
            jax.ShapeDtypeStruct((size, 3 * piece + PAD, rows), bf),
            jax.ShapeDtypeStruct((feats, rows), bf),
        ],
        compiler_params=params(),
        cost_estimate=cost(5),
        name="flip",
    )(w_query, w_key, w_value, w_output, attn_gain[None], mlp_gain[None])


def head_lanes(rows, head):
    lane = lax.broadcasted_iota(jnp.int32, (rows, LANES), 1)
    return (lane < HD) if head == 0 else (lane >= HD)


def attend_kernel(tile, low_ref, high_ref, q_ref, kv_ref, o_ref, lse_ref, vt_ref):
    nu, _, nb, tok, feats = kv_ref.shape
    width = nu * tok
    rows = tile * tok
    pairs = feats // LANES
    heads = range(2 * pairs)
    lanes = [slice(h // 2 * LANES, (h // 2 + 1) * LANES) for h in heads]
    j = pl.program_id(0)

    @pl.when(j == 0)
    def _():
        for c in range(nb):
            vt_ref[c] = kv_ref[:, 1, c].reshape(width, feats).T

    low, high = low_ref[0], high_ref[0]
    q = q_ref[...] * jnp.asarray(1.0 / math.sqrt(HD), bf)
    q_heads = [
        jnp.where(head_lanes(rows, h % 2), q[:, lanes[h]], jnp.zeros((rows, LANES), bf))
        for h in heads
    ]
    place_k = lax.broadcasted_iota(jnp.int32, (width, rows), 0)

    def step(chunk, state):
        k = kv_ref[:, 0, chunk].reshape(width, feats)
        start = chunk * width
        ok = (place_k >= low - start) & (place_k <= high - start)
        scores = [jnp.where(ok, dot_t(k[:, lanes[h]], q_heads[h]), NEG) for h in heads]
        new = []
        for h in heads:
            best, total, acc = state[h]
            best_new = jnp.maximum(best, jnp.max(scores[h], axis=0, keepdims=True))
            p = jnp.exp(scores[h] - best_new)
            factor = jnp.exp(best - best_new)
            total = total * factor + jnp.sum(p, axis=0, keepdims=True)
            acc = acc * factor + dot_n(vt_ref[chunk, h * HD : (h + 1) * HD], p.astype(bf))
            new.append((best_new, total, acc))
        return tuple(new)

    start = (
        jnp.full((1, rows), NEG, f32),
        jnp.zeros((1, rows), f32),
        jnp.zeros((HD, rows), f32),
    )
    state = lax.fori_loop(0, (j + 1) * tile, step, (start,) * len(heads))
    o_ref[...] = jnp.concatenate([acc / total for _, total, acc in state], axis=0).T.astype(bf)
    lse_ref[0] = jnp.concatenate([best + jnp.log(total) for best, total, _ in state], axis=0)


def attend(low, high, q, kv, tile):
    nu, _, nb, tok, feats = kv.shape
    rows = tile * tok
    nq = nb // tile
    heads = feats // HD
    row_spec = pl.BlockSpec((1, 1, rows), lambda j: (j, 0, 0))
    q_spec = pl.BlockSpec((rows, feats), lambda j: (j, 0))
    return pl.pallas_call(
        functools.partial(attend_kernel, tile),
        grid=(nq,),
        in_specs=[row_spec, row_spec, q_spec, full(kv.shape)],
        out_specs=[q_spec, pl.BlockSpec((1, heads, rows), lambda j: (j, 0, 0))],
        out_shape=[
            jax.ShapeDtypeStruct((nb * tok, feats), bf),
            jax.ShapeDtypeStruct((nq, heads, rows), f32),
        ],
        scratch_shapes=[pltpu.VMEM((nb, feats, nu * tok), bf)],
        compiler_params=params(),
        cost_estimate=cost(27 * nb * tok * nb / 8192),
        name="attend",
    )(low, high, q, kv)


def attend_back_kernel(
    tile,
    low_ref,
    high_ref,
    cos_ref,
    sin_ref,
    q_ref,
    do_ref,
    o_ref,
    lse_ref,
    kv_ref,
    dq_ref,
    dkv_ref,
    acc_ref,
    delta_ref,
    sums_ref,
):
    nu, _, _, tok, feats = kv_ref.shape
    nq, heads, rows = lse_ref.shape
    width = nu * tok
    pairs = feats // LANES
    chunk = pl.program_id(0)
    scale = jnp.asarray(1.0 / math.sqrt(HD), bf)

    @pl.when(chunk == 0)
    def _():
        acc_ref[...] = jnp.zeros_like(acc_ref)
        lane = lax.broadcasted_iota(jnp.int32, (8, feats), 1)
        row = lax.broadcasted_iota(jnp.int32, (8, feats), 0)
        mine = jnp.where(lane // HD == row, 1.0, 0.0).astype(f32)
        for j in range(nq):
            at = pl.ds(j * rows, rows)
            delta_ref[j] = lax.dot_general(
                mine,
                do_ref[at, :].astype(f32) * o_ref[at, :].astype(f32),
                (((1,), (1,)), ((), ())),
                preferred_element_type=f32,
                precision=lax.Precision.HIGHEST,
            )

    k_all = kv_ref[:, 0, 0].reshape(width, feats)
    v_all = kv_ref[:, 1, 0].reshape(width, feats)
    lanes = [slice(p * LANES, (p + 1) * LANES) for p in range(pairs)]
    k = [k_all[:, at] for at in lanes]
    v = [v_all[:, at] for at in lanes]
    k_turned = [part.T for part in k]
    place_k = lax.broadcasted_iota(jnp.int32, (width, rows), 0)
    start = chunk * width
    sums_ref[...] = jnp.zeros_like(sums_ref)

    def step(j, _):
        at = pl.ds(pl.multiple_of(j * rows, rows), rows)
        q = q_ref[at, :] * scale
        do = do_ref[at, :]
        ok = (place_k >= low_ref[j] - start) & (place_k <= high_ref[j] - start)
        q_heads, do_heads = [
            [
                jnp.where(head_lanes(rows, h % 2), part[:, lanes[h // 2]], jnp.zeros((rows, LANES), bf))
                for h in range(2 * pairs)
            ]
            for part in (q, do)
        ]
        scores = [dot_t(k[h // 2], q_heads[h]) for h in range(2 * pairs)]
        d_probs = [dot_t(v[h // 2], do_heads[h]) for h in range(2 * pairs)]
        for pair in range(pairs):
            dk = dv = 0.0
            dq = []
            for i in range(2):
                h = 2 * pair + i
                p = jnp.exp(jnp.where(ok, scores[h] - lse_ref[j, h : h + 1], NEG))
                ds = (p * (d_probs[h] - delta_ref[j, h : h + 1])).astype(bf)
                dv = dv + dot_n(p.astype(bf), do_heads[h])
                dk = dk + dot_n(ds, q_heads[h])
                dq.append(dot_n(k_turned[pair][i * HD : (i + 1) * HD], ds))
            acc_ref[j, lanes[pair]] = acc_ref[j, lanes[pair]] + jnp.concatenate(dq, axis=0)
            sums_ref[0, pair] = sums_ref[0, pair] + dk
            sums_ref[1, pair] = sums_ref[1, pair] + dv
        return 0

    lax.fori_loop(chunk // tile, nq, step, 0)
    for i in range(2):
        for pair in range(pairs):
            dkv_ref[:, i, 0, :, lanes[pair]] = (
                sums_ref[i, pair].astype(bf).reshape(nu, tok, LANES)
            )

    @pl.when(chunk == pl.num_programs(0) - 1)
    def _():
        dq = jnp.concatenate([acc_ref[j].T for j in range(nq)], axis=0) * (1.0 / math.sqrt(HD))
        cosine, sine = wide(cos_ref[...], feats), wide(sin_ref[...], feats)
        dq_ref[...] = (dq * cosine - turned(dq) * sine).astype(bf)


def attend_back(low, high, cosine, sine, q, do, o, lse, kv, tile):
    nu, _, nb, tok, feats = kv.shape
    rows = tile * tok
    nq = nb // tile
    kv_spec = pl.BlockSpec((nu, 2, 1, tok, feats), lambda c: (0, 0, c, 0, 0))
    return pl.pallas_call(
        functools.partial(attend_back_kernel, tile),
        grid=(nb,),
        in_specs=[
            *[full(part.shape) for part in (low, high, cosine, sine, q, do, o, lse)],
            kv_spec,
        ],
        out_specs=[full(q.shape), kv_spec],
        out_shape=[
            jax.ShapeDtypeStruct(q.shape, bf),
            jax.ShapeDtypeStruct(kv.shape, bf),
        ],
        scratch_shapes=[
            pltpu.VMEM((nq, feats, rows), f32),
            pltpu.VMEM((nq, 8, rows), f32),
            pltpu.VMEM((2, feats // LANES, nu * tok, LANES), f32),
        ],
        compiler_params=params(),
        cost_estimate=cost(41 * nb * tok * nb / 8192),
        name="attend_back",
    )(low, high, cosine, sine, q, do, o, lse, kv)


def output_kernel(x_ref, o_ref, w_ref, gain_ref, x1_ref, normed_ref):
    blocks, pieces, groups, piece, width = w_ref.shape
    square = 0.0
    for block in range(blocks):
        at = slice(block * width, (block + 1) * width)
        total = x_ref[:, at].astype(f32)
        for g in range(groups):
            total = total + dot_n(o_ref[g], w_ref[block, :, g].reshape(pieces * piece, width))
        x1_ref[:, at] = total
        square = square + jnp.sum(total * total, axis=1, keepdims=True)
    r2 = lax.rsqrt(square * (1.0 / (blocks * width)) + epsilon)
    normed_ref[...] = (x1_ref[...] * r2 * gain_ref[...]).astype(bf)


def output_project(x_all, o_all, w_out, gain, rows):
    count, dim = x_all.shape
    groups, _, feats = o_all.shape
    tiled = pl.BlockSpec((rows, dim), lambda i: (i, 0))
    return pl.pallas_call(
        output_kernel,
        grid=(count // rows,),
        in_specs=[
            tiled,
            pl.BlockSpec((groups, rows, feats), lambda i: (0, i, 0)),
            full(w_out.shape),
            full(gain.shape),
        ],
        out_specs=[tiled, tiled],
        out_shape=[
            jax.ShapeDtypeStruct((count, dim), f32),
            jax.ShapeDtypeStruct((count, dim), bf),
        ],
        compiler_params=params(),
        cost_estimate=cost(count * 0.015),
        name="output_project",
    )(x_all, o_all, w_out, gain)


def output_back_kernel(d_ref, w_ref, out_ref):
    blocks, pieces, _, piece, width = w_ref.shape
    total = 0.0
    for block in range(blocks):
        at = slice(block * width, (block + 1) * width)
        total = total + dot_t(d_ref[:, at], w_ref[block, :, 0].reshape(pieces * piece, width))
    out_ref[0] = total.astype(bf)


def output_back(d_attn, w_out):
    tok, dim = d_attn.shape
    blocks, pieces, groups, piece, width = w_out.shape
    return pl.pallas_call(
        output_back_kernel,
        grid=(groups,),
        in_specs=[
            full(d_attn.shape),
            pl.BlockSpec((blocks, pieces, 1, piece, width), lambda g: (0, 0, g, 0, 0)),
        ],
        out_specs=pl.BlockSpec((1, tok, pieces * piece), lambda g: (g, 0, 0)),
        out_shape=jax.ShapeDtypeStruct((groups, tok, pieces * piece), bf),
        compiler_params=params(),
        cost_estimate=cost(8),
        name="output_back",
    )(d_attn, w_out)


def project_back_kernel(
    piece, _, x_ref, w_ref, cos_ref, sin_ref, dq_ref, dkv_ref, all_ref, dn_ref, gain_ref
):
    blocks, width = w_ref.shape[1], w_ref.shape[3]
    feats = dq_ref.shape[1]
    cosine, sine = wide(cos_ref[...], feats), wide(sin_ref[...], feats)
    dk = dkv_ref[0].astype(f32)
    parts = (
        dq_ref[...],
        (dk * cosine - turned(dk) * sine).astype(bf),
        dkv_ref[1],
    )
    for i in range(3):
        all_ref[i] = parts[i]
    x = x_ref[...].astype(f32)
    r1 = rms_scale(x)

    @pl.when(pl.program_id(0) == 0)
    def _():
        gain_ref[...] = jnp.zeros_like(gain_ref)

    for block in range(blocks):
        at = slice(block * width, (block + 1) * width)
        total = 0.0
        for part in range(3):
            total = total + dot_n(parts[part], weight_block(w_ref, block, part, piece))
        dn_ref[0, :, at] = total.astype(bf)
        gain_ref[:, at] = gain_ref[:, at] + jnp.sum(total * (x[:, at] * r1), axis=0, keepdims=True)


def project_back(x_all, w, cosine, sine, dq, dkv, piece, order):
    count, dim = x_all.shape
    size = order.shape[0]
    rows = count // size
    feats = dq.shape[1]
    tiled = lambda width: pl.BlockSpec((rows, width), lambda i, at: (at[i], 0))
    return pl.pallas_call(
        functools.partial(project_back_kernel, piece),
        grid_spec=pltpu.PrefetchScalarGridSpec(
            num_scalar_prefetch=1,
            grid=(size,),
            in_specs=[
                tiled(dim),
                full(w.shape),
                tiled(LANES),
                tiled(LANES),
                tiled(feats),
                pl.BlockSpec((2, rows, feats), lambda i, at: (0, at[i], 0)),
            ],
            out_specs=[
                pl.BlockSpec((3, rows, feats), lambda i, at: (0, at[i], 0)),
                pl.BlockSpec((1, rows, dim), lambda i, _: (i, 0, 0)),
                full((1, dim)),
            ],
        ),
        out_shape=[
            jax.ShapeDtypeStruct((3, count, feats), bf),
            jax.ShapeDtypeStruct((size, rows, dim), bf),
            jax.ShapeDtypeStruct((1, dim), f32),
        ],
        compiler_params=params(),
        cost_estimate=cost(count * 0.01),
        name="project_back",
    )(order, x_all, w, cosine, sine, dq, dkv)


def projection_grads_kernel(left_ref, right_ref, gain_ref, out_ref, turned_ref):
    n, feats, _ = turned_ref.shape
    pieces = out_ref.shape[0]

    @pl.when(pl.program_id(0) == 0)
    def _():
        for i in range(n):
            turned_ref[i] = left_ref[i].T

    piece = feats // pieces
    right = right_ref[...]
    width = right.shape[1]
    for i in range(n):
        grad = dot_n(turned_ref[i], right).astype(bf)
        out_ref[:, 0, i * piece : (i + 1) * piece, :] = grad.reshape(pieces, piece, width)
    gain = gain_ref[...].astype(bf)
    for u in range(pieces):
        out_ref[u, 0, n * piece :, :] = gain


def projection_grads(lefts, right, gain, pieces, width):
    n, count, feats = lefts.shape
    dim = right.shape[1]
    rows = n * (feats // pieces) + PAD
    return pl.pallas_call(
        projection_grads_kernel,
        grid=(dim // width,),
        in_specs=[
            full(lefts.shape),
            pl.BlockSpec((count, width), lambda i: (0, i)),
            pl.BlockSpec((PAD, width), lambda i: (0, i)),
        ],
        out_specs=pl.BlockSpec((pieces, 1, rows, width), lambda i: (0, i, 0, 0)),
        out_shape=jax.ShapeDtypeStruct((pieces, dim // width, rows, width), bf),
        scratch_shapes=[pltpu.VMEM((n, feats, count), bf)],
        compiler_params=params(),
        cost_estimate=cost(2.5 * n),
        name="projection_grads",
    )(lefts, right, gain)


def output_grads_kernel(o_ref, d_ref, out_ref):
    pieces, _, piece, width = out_ref.shape
    grad = dot_n(o_ref[0].T, d_ref[...])
    out_ref[:, 0] = grad.astype(bf).reshape(pieces, piece, width)


def output_grads(o_all, d_columns, pieces):
    groups, count, feats = o_all.shape
    width = d_columns.shape[1]
    shape = (pieces, groups, feats // pieces, width)
    return pl.pallas_call(
        output_grads_kernel,
        grid=(groups,),
        in_specs=[
            pl.BlockSpec((1, count, feats), lambda g: (g, 0, 0)),
            full(d_columns.shape),
        ],
        out_specs=pl.BlockSpec((pieces, 1, *shape[2:]), lambda g: (0, g, 0, 0)),
        out_shape=jax.ShapeDtypeStruct(shape, bf),
        compiler_params=params(),
        cost_estimate=cost(6),
        name="output_grads",
    )(o_all, d_columns)


def prepare_kernel(wg_ref, wu_ref, wd_ref, out_ref):
    for i, ref in enumerate((wg_ref, wu_ref, wd_ref)):
        out_ref[0, i] = ref[...].astype(bf)


def prepare(w_gate, w_up, w_down, size):
    rows, columns = w_gate.shape
    width = columns // size
    if width % LANES:
        stacked = jnp.stack([w.astype(bf) for w in (w_gate, w_up, w_down)])
        return jnp.transpose(stacked.reshape(3, rows, size, width), (2, 0, 1, 3))
    spec = pl.BlockSpec((rows, width), lambda i: (0, i))
    return pl.pallas_call(
        prepare_kernel,
        grid=(size,),
        in_specs=[spec] * 3,
        out_specs=pl.BlockSpec((1, 3, rows, width), lambda i: (i, 0, 0, 0)),
        out_shape=jax.ShapeDtypeStruct((size, 3, rows, width), bf),
        compiler_params=params(),
        cost_estimate=cost(4),
        name="prepare",
    )(w_gate, w_up, w_down)


def finish_kernel(in_ref, *outs):
    n, _, _, width = in_ref.shape
    for k in range(n):
        for i in range(3):
            outs[i][:, k * width : (k + 1) * width] = in_ref[k, i].astype(f32)


def finish(parts):
    n, _, rows, width = parts.shape
    if width % LANES:
        out = jnp.transpose(parts, (1, 2, 0, 3)).reshape(3, rows, n * width).astype(f32)
        return [out[i] for i in range(3)]
    return pl.pallas_call(
        finish_kernel,
        out_shape=[jax.ShapeDtypeStruct((rows, n * width), f32)] * 3,
        compiler_params=params(),
        cost_estimate=cost(5),
        name="finish",
    )(parts)


def whole_weight(ref, k):
    w = ref[:, k]
    return w.reshape(w.shape[0] * w.shape[1], w.shape[2])


def hidden_kernel(n, *refs):
    n_ref, g_ref = refs[:2]
    act_ref, dg_ref, du_ref = refs[2 + n :]
    normed, cot = n_ref[...], g_ref[...]
    for i in range(n):
        w_ref = refs[2 + i]
        gate = dot_n(normed, whole_weight(w_ref, 0))
        up = dot_n(normed, whole_weight(w_ref, 1))
        d_act = dot_n(cot, whole_weight(w_ref, 2))
        sigma = jax.nn.sigmoid(gate)
        silu = gate * sigma
        act_ref[i] = (silu * up).astype(bf)
        du_ref[i] = (d_act * silu).astype(bf)
        dg_ref[i] = (d_act * up * (sigma * (1.0 + gate * (1.0 - sigma)))).astype(bf)


def hidden(normed, cot, weights, rows):
    count, dim = normed.shape
    n = len(weights)
    width = weights[0].shape[3]
    tiled = pl.BlockSpec((rows, dim), lambda i: (i, 0))
    out = pl.BlockSpec((n, rows, width), lambda i: (0, i, 0))
    return pl.pallas_call(
        functools.partial(hidden_kernel, n),
        grid=(count // rows,),
        in_specs=[tiled, tiled] + [full(w.shape) for w in weights],
        out_specs=[out] * 3,
        out_shape=[jax.ShapeDtypeStruct((n, count, width), bf)] * 3,
        compiler_params=params(),
        cost_estimate=cost(20),
        name="hidden",
    )(normed, cot, *weights)


def mix_kernel(which, n, _, *refs):
    m = len(which)
    lefts, weights, out_ref = refs[: 2 * m], refs[2 * m : -1], refs[-1]
    total = 0.0
    for k in range(m):
        for i in range(n):
            left = jnp.concatenate([lefts[2 * k][i], lefts[2 * k + 1][i]], axis=0)
            total = total + dot_t(left, whole_weight(weights[i], k))
    out_ref[...] = total.astype(bf).reshape(out_ref.shape)


def mix(lefts, weights, which, order):
    n, count, width = lefts[0].shape
    size = order.shape[0]
    rows = count // size
    blocks, _, rows_w, _ = weights[0].shape
    dim = blocks * rows_w
    chosen = pl.BlockSpec(
        (blocks, len(which), rows_w, width), lambda i, _: (0, which[0] // len(which), 0, 0)
    )
    pair = [
        pl.BlockSpec((n, rows, width), lambda i, at: (0, at[2 * i], 0)),
        pl.BlockSpec((n, rows, width), lambda i, at: (0, at[2 * i + 1], 0)),
    ]
    return pl.pallas_call(
        functools.partial(mix_kernel, which, n),
        grid_spec=pltpu.PrefetchScalarGridSpec(
            num_scalar_prefetch=1,
            grid=(size // 2,),
            in_specs=pair * len(which) + [chosen] * n,
            out_specs=pl.BlockSpec((2, rows, dim), lambda i, _: (i, 0, 0)),
        ),
        out_shape=jax.ShapeDtypeStruct((size, rows, dim), bf),
        compiler_params=params(),
        cost_estimate=cost(8 * len(which)),
        name="mix",
    )(order, *[left for left in lefts for _ in range(2)], *weights)


def hidden_grads_kernel(n_ref, g_ref, dg_ref, du_ref, act_ref, *outs):
    normed, cot = n_ref[...].T, g_ref[...].T
    for i, out_ref in enumerate(outs):
        for k, grad in enumerate(
            (dot_n(normed, dg_ref[i]), dot_n(normed, du_ref[i]), dot_n(cot, act_ref[i]))
        ):
            out_ref[:, k] = grad.astype(bf).reshape(out_ref.shape[0], *out_ref.shape[2:])


def hidden_grads(normed, cot, d_gate, d_up, act, rows):
    count, dim = normed.shape
    block = max(rows, LANES)
    n, _, width = act.shape
    columns = pl.BlockSpec((count, block), lambda i: (0, i))
    return pl.pallas_call(
        hidden_grads_kernel,
        grid=(dim // block,),
        in_specs=[columns, columns] + [full(act.shape)] * 3,
        out_specs=[pl.BlockSpec((block // rows, 3, rows, width), lambda i: (i, 0, 0, 0))] * n,
        out_shape=[jax.ShapeDtypeStruct((dim // rows, 3, rows, width), bf)] * n,
        compiler_params=params(),
        cost_estimate=cost(25),
        name="hidden_grads",
    )(normed, cot, d_gate, d_up, act)


def on_device(
    tokens,
    segments,
    cotangent,
    attn_gain,
    w_query,
    w_key,
    w_value,
    w_output,
    mlp_gain,
    w_gate,
    w_up,
    w_down,
):
    nb, nu = lax.axis_size("blk"), lax.axis_size("uly")
    b, u = lax.axis_index("blk"), lax.axis_index("uly")
    tok, dim = tokens.shape
    seq = segments.shape[0]
    rows, feats_u = w_query.shape
    group = feats_u * nu // nb
    strided = (feats_u // HD) % nb == 0 and rows % LANES == 0
    count = nb * tok
    tile = 2
    both = ("blk", "uly")
    block = rows if strided else 2 * LANES
    blocks = dim // block
    pieces = nu if strided else 1
    piece = group // nu if strided else -(-group // LANES) * LANES
    feats = pieces * piece
    step = 2 * tok

    seg_mine = pick(jnp.swapaxes(segments.reshape(nb, nu, tok), 0, 1), u).reshape(count)
    index = (
        jnp.arange(nb, dtype=jnp.int32)[:, None] * (nu * tok)
        + u * tok
        + jnp.arange(tok, dtype=jnp.int32)[None, :]
    ).reshape(count)
    first = jnp.sum((segments[None, :] < seg_mine[:, None]).astype(jnp.int32), axis=1)
    lane = jnp.arange(LANES, dtype=jnp.int32)
    freq = theta_base ** (-((lane % (HD // 2)).astype(f32) * 2.0) / HD)
    angles = (index - first).astype(f32)[:, None] * freq[None, :]
    cosine = jnp.cos(angles)
    sine = jnp.sin(angles) * jnp.where(lane % HD < HD // 2, -1.0, 1.0)[None, :]
    low = first.reshape(nb // tile, 1, tile * tok)
    high = index.reshape(nb // tile, 1, tile * tok)

    ff_u = w_gate.shape[1]
    ff_piece = ff_u // nb
    tokens_plan = gather_plan(tokens, "blk")

    tables = (cosine, sine, low, high)

    def prepared():
        yield []
        return (yield [prepare(w_gate, w_up, w_down, nb), *tables])

    def swapped(parts, spare=0):
        got = swap(parts, "blk")
        yield from idle(spare)
        (got,) = yield [got]
        return got

    if strided:
        sent, out_flipped = flip(w_query, w_key, w_value, w_output, attn_gain, mlp_gain, nb)
        x_all, (ff_sent, cosine, sine, low, high), w_qkv = together(
            tokens_plan,
            prepared(),
            chain(swapped(sent, 1), lambda got: gather_plan(got, "uly")),
        )
    else:
        gains = jnp.stack([attn_gain, mlp_gain]).astype(bf)
        flipped = [jnp.transpose(w.astype(bf)) for w in (w_query, w_key, w_value, w_output)]
        out_flipped = flipped[3]
        sent = gather(jnp.stack(flipped[:3])[None], "uly")
        sent = jnp.transpose(sent, (0, 2, 1, 3)).reshape(nb, group, 3, rows)
        x_all, (ff_sent, cosine, sine, low, high), got = together(tokens_plan, prepared(), swapped(sent))
        got = jnp.transpose(got, (2, 1, 0, 3)).reshape(3, group, dim)
        got = jnp.pad(got, ((0, 0), (0, piece - group), (0, 0))).reshape(3 * piece, dim)
        all_gains = jnp.transpose(gather(gains[None], "blk"), (1, 0, 2)).reshape(2, dim)
        got = jnp.concatenate([got, jnp.pad(all_gains, ((0, PAD - 2), (0, 0)))])
        w_qkv = jnp.transpose(got.reshape(3 * piece + PAD, blocks, block), (1, 0, 2))[None]
    x_all = x_all.reshape(count, dim)
    gain1, gain2 = [
        w_qkv[0, :, 3 * piece + i, :].reshape(1, dim).astype(f32) for i in range(2)
    ]

    ff_got = swap(after(ff_sent, x_all), "blk")
    w_out = gather(after(out_flipped, x_all)[None], both)
    cot_all = gather(after(cotangent, x_all, w_out), "blk")
    if strided:
        w_out = w_out.reshape(nb, nu, nb, piece, rows)
    else:
        w_out = jnp.transpose(w_out.reshape(nb, nu * feats_u, rows), (1, 0, 2))
        w_out = jnp.pad(
            w_out.reshape(nb, group, dim), ((0, 0), (0, piece - group), (0, 0))
        )
        w_out = jnp.transpose(w_out.reshape(nb, piece, blocks, block), (2, 0, 1, 3))[:, None]

    q, kv, normed = project(x_all, w_qkv, cosine, sine, piece, step)
    (kv_all,) = together(gather_plan(kv.reshape(2, nb, tok, feats), "uly"))
    o, lse = attend(low, high, q, kv_all, tile)
    ff_got, o = lax.optimization_barrier((ff_got, o))
    rounds = Rounds()
    rounds.add(o=gather_plan(o, "blk"), ff=gather_near_plan(ff_got, "uly", nb // 4))
    (o_all,) = rounds.until("o")
    x1, normed2 = output_project(x_all, o_all, w_out, gain2, step)

    (w_ff,) = rounds.until("ff")

    act, d_gate, d_up = hidden(normed2, cot_all, w_ff, step)
    order, plain = scatter_order("blk"), jnp.arange(nb, dtype=jnp.int32)
    d_norm2 = mix([d_gate, d_up], w_ff, (0, 1), order)

    def mlp_plan():
        yield []
        (out,) = yield [mix([act], w_ff, (2,), plain)]
        return out

    def hidden_grads_plan():
        grads = yield hidden_grads(
            after(normed2, d_norm2), cot_all, d_gate, d_up, act, rows
        )
        return (yield from scatter_near_plan(grads, "uly", 2 * nb))

    rounds = Rounds()
    rounds.add(
        d_norm2=scatter_plan(d_norm2, "blk", True),
        mlp=mlp_plan(),
        ff=hidden_grads_plan(),
    )
    d_norm2, mlp_out = rounds.until("d_norm2", "mlp")
    x1_own = lax.dynamic_slice_in_dim(x1, b * tok, tok, 0)
    mlp_out = scatter(after(mlp_out, d_norm2).reshape(count, dim), "blk")
    r2_own = rms_scale(x1_own)
    gain2_part = jnp.sum(d_norm2 * x1_own * r2_own, axis=0, keepdims=True)
    z_two = gain2 * d_norm2
    dx1 = (
        cotangent.astype(f32)
        + r2_own * z_two
        - x1_own * r2_own * r2_own * r2_own * jnp.mean(z_two * x1_own, axis=-1, keepdims=True)
    )
    d_attn = dx1.astype(bf)

    d_o = output_back(d_attn, w_out)
    d_columns = jnp.transpose(d_attn.reshape(tok, nb, rows), (1, 0, 2))
    rounds.add(d_o=swap_plan(d_o, "blk"))
    (got,) = rounds.until("d_o")
    d_o = got.reshape(count, feats)
    d_columns = swap(after(d_columns, d_o), "blk")
    dq, dkv = attend_back(low, high, cosine, sine, q, d_o, o, lse, kv_all, tile)
    dkv, mlp_out, d_columns = lax.optimization_barrier((dkv, mlp_out, d_columns))
    rounds.add(dkv=scatter_plan(dkv, "uly"))
    (ff_mine,) = rounds.until("ff")
    ff_got = swap(ff_mine, "blk")
    out_grads = output_grads(o_all, d_columns.reshape(count, rows), pieces)
    if not strided:
        out_grads = out_grads[:, :, :group]
    (dkv,) = rounds.until("dkv")
    dkv, out_grads = lax.optimization_barrier((dkv, out_grads))
    rounds.add(out=scatter_plan(out_grads.reshape(nu, feats_u, rows), "uly"))
    dkv = dkv.astype(bf).reshape(2, count, feats)
    d_qkv, d_norm1, gain1_part = project_back(x_all, w_qkv, cosine, sine, dq, dkv, piece, order)
    gain_parts = jnp.pad(jnp.concatenate([gain1_part, gain2_part]), ((0, PAD - 2), (0, 0)))
    grads = projection_grads(d_qkv, after(normed, d_norm1), gain_parts, pieces, block)
    last = scatter_plan(d_norm1, "blk", True)
    if strided:
        rounds.add(
            last=last,
            grads=chain(scatter_plan(grads, "uly"), lambda mine: swapped(mine.astype(bf))),
        )
        d_norm1, got, out_grads = rounds.until("last", "grads", "out")
        gain_sums = jnp.sum(got[:, 3 * piece : 3 * piece + 2].astype(f32), axis=0)
        heads = [got[:, i * piece : (i + 1) * piece].reshape(feats_u, rows) for i in range(3)]
    else:
        wanted = grads[0, :, : 3 * piece].reshape(blocks, 3, piece, block)[:, :, :group]
        wanted = jnp.transpose(wanted, (1, 2, 0, 3)).reshape(3, group, nb, rows)
        rounds.add(last=last, grads=swapped(jnp.transpose(wanted, (2, 1, 0, 3))))
        d_norm1, got, out_grads = rounds.until("last", "grads", "out")
        got = scatter(got.reshape(nu, feats_u, 3, rows), "uly")[0]
        heads = [got[:, i] for i in range(3)]
        gain_sums = lax.dynamic_slice_in_dim(lax.psum(gain_parts[:2], both), b * rows, rows, 1)
    grad_output = jnp.transpose(out_grads)
    grad_query, grad_key, grad_value = [jnp.transpose(h).astype(f32) for h in heads]
    x_own = tokens.astype(f32)
    r1_own = rms_scale(x_own)
    z_one = gain1 * d_norm1
    grad_tokens = (
        dx1
        + r1_own * z_one
        - x_own * r1_own * r1_own * r1_own * jnp.mean(z_one * x_own, axis=-1, keepdims=True)
    )
    output = x1_own + mlp_out.astype(f32)
    return (
        output,
        grad_tokens,
        gain_sums[0],
        grad_query,
        grad_key,
        grad_value,
        grad_output,
        gain_sums[1],
        *finish(ff_got),
    )


def solution(mesh):
    tokens_split = P(("blk", "uly"), None)
    weights = P("blk", "uly")
    return jax.shard_map(
        on_device,
        mesh=mesh,
        in_specs=(
            tokens_split,
            P(),
            tokens_split,
            P("blk"),
            weights,
            weights,
            weights,
            weights,
            P("blk"),
            weights,
            weights,
            weights,
        ),
        out_specs=(
            tokens_split,
            tokens_split,
            P("blk"),
            weights,
            weights,
            weights,
            weights,
            P("blk"),
            weights,
            weights,
            weights,
        ),
        check_vma=False,
    )
```

```python
import functools
import math

import jax
import jax.numpy as jnp
from jax import lax
from jax.experimental import pallas as pl
from jax.experimental.pallas import tpu as pltpu
from jax.sharding import PartitionSpec as P

H = 32
HD = 64
LANES = 128
PAD = 16

theta_base = 130000.0
epsilon = 1e-05
bf = jnp.bfloat16
f32 = jnp.float32
NEG = -1e30


def dot_t(left, right):
    return lax.dot_general(left, right, (((1,), (1,)), ((), ())), preferred_element_type=f32)


def dot_n(left, right):
    return jnp.dot(left, right, preferred_element_type=f32)


def dot_c(left, right):
    return lax.dot_general(left, right, (((0,), (0,)), ((), ())), preferred_element_type=f32)


def rms_scale(value):
    return lax.rsqrt(jnp.mean(value * value, axis=-1, keepdims=True) + epsilon)


def params(mib=56):
    return pltpu.CompilerParams(vmem_limit_bytes=mib * 2**20)


def cost(micros):
    return pl.CostEstimate(flops=int(micros * 0.25 * 1.1e9), bytes_accessed=0, transcendentals=0)


def full(shape):
    return pl.BlockSpec(shape, lambda *grid: (0,) * len(shape))


def after(value, *others):
    return lax.optimization_barrier((value, *others))[0]


def hop(value, axis, slow, fast):
    size = lax.axis_size(axis)
    ring = size // 2
    pairs = [(i, ((i // 2 + slow) % ring) * 2 + (i % 2 ^ fast)) for i in range(size)]
    return lax.ppermute(value, axis, pairs)


def near(axis, slow, fast):
    ring = lax.axis_size(axis) // 2
    i = lax.axis_index(axis)
    return ((i // 2 + slow + ring) % ring) * 2 + (i % 2 ^ fast)


def place(out, piece, at):
    return lax.dynamic_update_slice_in_dim(out, piece[None], at, 0)


def pick(parts, at):
    return lax.dynamic_index_in_dim(parts, at, 0, False)


class Rounds:
    def __init__(self):
        self.live, self.results = {}, {}

    def add(self, **plans):
        for name, plan in plans.items():
            self.advance(name, plan, None)

    def advance(self, name, plan, value):
        try:
            self.live[name] = (plan, list(plan.send(value)))
        except StopIteration as end:
            self.live.pop(name, None)
            self.results[name] = end.value

    def round(self, *also):
        waiting = list(self.live.items())
        flat = [v for _, (_, values) in waiting for v in values] + list(also)
        if flat:
            flat = list(lax.optimization_barrier(tuple(flat)))
        for name, (plan, values) in waiting:
            self.advance(name, plan, [flat.pop(0) for _ in values])
        return flat

    def until(self, *names):
        while any(name in self.live for name in names):
            self.round()
        return [self.results[name] for name in names]


def together(*plans):
    rounds = Rounds()
    names = [str(i) for i in range(len(plans))]
    rounds.add(**dict(zip(names, plans)))
    return rounds.until(*names)


def idle(count):
    for _ in range(count):
        yield []


def chain(first, *rest):
    value = yield from first
    for plan in rest:
        value = yield from plan(value)
    return value


def gather_plan(value, axis):
    size = lax.axis_size(axis)
    ring = size // 2
    out = jnp.zeros((size, *value.shape), value.dtype)
    fresh = {0: value}
    crossing = {0: hop(value, axis, 0, 1)}
    for s in range(1, ring // 2 + 1):
        arriving = {-s: hop(fresh[1 - s], axis, 1, 0)}
        if s <= (ring - 1) // 2:
            arriving[s] = hop(fresh[s - 1], axis, -1, 0)
        got = yield [*arriving.values(), *crossing.values()]
        for at, piece in zip(crossing, got[len(arriving) :]):
            out = place(out, piece, near(axis, at, 1))
        fresh = dict(zip(arriving, got))
        for at, piece in fresh.items():
            out = place(out, piece, near(axis, at, 0))
        crossing = {at: hop(piece, axis, 0, 1) for at, piece in fresh.items()}
        if s == 1:
            out = place(out, value, near(axis, 0, 0))
    got = yield list(crossing.values())
    for at, piece in zip(crossing, got):
        out = place(out, piece, near(axis, at, 1))
    return out


def scatter_steps(axis):
    ring = lax.axis_size(axis) // 2
    far, back = ring // 2, (ring - 1) // 2
    steps = [[s] + ([-s] if s <= back else []) for s in range(far, 0, -1)]
    if ring == 4:
        steps = [[2, -1], [1]]
    steps[-1] = steps[-1] + [0]
    return steps


def scatter_order(axis):
    steps = sum(scatter_steps(axis), [])
    return jnp.stack([near(axis, s, fast) for fast in (1, 0) for s in steps]).astype(jnp.int32)


def scatter_plan(parts, axis, ordered=False):
    steps = scatter_steps(axis)
    places = sum(steps, [])

    def part(s, fast):
        if ordered:
            return parts[places.index(s) + (0 if fast else len(places))]
        return pick(parts, near(axis, s, fast))

    def column(offsets, fast):
        if ordered:
            at = places.index(offsets[0])
            return parts[at : at + len(offsets)]
        return jnp.stack([part(s, fast) for s in offsets])

    up = down = None
    for offsets in steps:
        crossed = hop(column(offsets, 1), axis, 0, 1)
        got = yield [crossed, *[v for v in (up, down) if v is not None]]
        crossed, carried = got[0], got[1:]
        totals = {
            s: part(s, 0).astype(f32) + crossed[k].astype(f32)
            for k, s in enumerate(offsets)
        }
        if up is not None:
            up = carried.pop(0).astype(f32)
        if down is not None:
            down = carried.pop(0).astype(f32)
        ups = [s for s in offsets if s > 0]
        downs = [s for s in offsets if s < 0]
        held = down
        if ups:
            total = totals[ups[0]] if up is None else totals[ups[0]] + up
            up = hop(total.astype(bf), axis, 1, 0)
        if downs:
            total = totals[downs[0]] if down is None else totals[downs[0]] + down
            down = hop(total.astype(bf), axis, -1, 0)
            held = None
        own = totals.get(0)
    if held is not None:
        own = own + held
        down = None
    for piece in (yield [v for v in (up, down) if v is not None]):
        own = own + piece.astype(f32)
    return own


def swap_plan(parts, axis):
    ring = lax.axis_size(axis) // 2
    fast = lax.axis_index(axis) % 2
    slow = lax.axis_index(axis) // 2
    columns = jnp.swapaxes(parts.reshape(ring, 2, *parts.shape[1:]), 0, 1)
    kept = pick(columns, fast)
    (given,) = yield [hop(pick(columns, 1 - fast), axis, 0, 1)]
    pairs = jnp.stack([jnp.where(fast == 0, kept, given), jnp.where(fast == 0, given, kept)], 1)
    out = place(jnp.zeros_like(pairs), pick(pairs, slow), slow)
    arrived = yield [hop(pick(pairs, (slow + s) % ring), axis, s, 0) for s in range(1, ring)]
    for s, piece in enumerate(arrived, 1):
        out = place(out, piece, (slow - s + ring) % ring)
    return out.reshape(parts.shape)


def gather_near_plan(value, axis, spare=0):
    ring = lax.axis_size(axis) // 2
    crossed = [hop(value, axis, 0, 1)]
    got = [hop(value, axis, s, 0) for s in range(1, ring)]
    yield from idle(spare)
    got = yield got
    crossed += [hop(piece, axis, 0, 1) for piece in got]
    crossed = yield crossed
    return [value, *got, *crossed]


def scatter_near_plan(parts, axis, spare=0):
    ring = lax.axis_size(axis) // 2
    crossed = yield [hop(part, axis, 0, 1) for part in parts[ring:]]
    sums = [mine.astype(f32) + piece.astype(f32) for mine, piece in zip(parts, crossed)]
    total = sums[0].astype(bf)
    got = [hop(sums[s].astype(bf), axis, -s, 0) for s in range(1, ring)]
    yield from idle(spare)
    total = total.astype(f32)
    for piece in (yield got):
        total = total + piece.astype(f32)
    return total.astype(bf)


def swap(parts, axis):
    return lax.all_to_all(parts, axis, 0, 0, tiled=True)


def gather(value, axis):
    return lax.all_gather(value, axis, axis=0, tiled=True)


def scatter(value, axis):
    return lax.psum_scatter(value, axis, scatter_dimension=0, tiled=True)


def turned(value):
    width = value.shape[1]
    lane = lax.broadcasted_iota(jnp.int32, value.shape, 1)
    return jnp.where(
        lane % HD < HD // 2,
        pltpu.roll(value, width - HD // 2, 1),
        pltpu.roll(value, HD // 2, 1),
    )


def wide(table, width):
    return jnp.concatenate([table] * (width // LANES), axis=1)


def weight_block(w_ref, block, part, piece):
    w = w_ref[:, block, part * piece : (part + 1) * piece, :]
    return w.reshape(w.shape[0] * piece, w.shape[2])


def project_kernel(piece, x_ref, w_ref, cos_ref, sin_ref, q_ref, kv_ref, normed_ref):
    blocks, width = w_ref.shape[1], w_ref.shape[3]
    x = x_ref[...].astype(f32)
    r1 = rms_scale(x)
    total = [0.0, 0.0, 0.0]
    for block in range(blocks):
        at = slice(block * width, (block + 1) * width)
        gain = w_ref[0, block, 3 * piece : 3 * piece + PAD, :][0:1].astype(f32)
        normed = (x[:, at] * r1 * gain).astype(bf)
        normed_ref[:, at] = normed
        for part in range(3):
            total[part] = total[part] + dot_t(normed, weight_block(w_ref, block, part, piece))
    feats = total[0].shape[1]
    cosine, sine = wide(cos_ref[...], feats), wide(sin_ref[...], feats)

    def rotate(value):
        value = value.astype(bf).astype(f32)
        return (value * cosine + turned(value) * sine).astype(bf)

    q_ref[...] = rotate(total[0])
    kv_ref[0] = rotate(total[1])
    kv_ref[1] = total[2].astype(bf)


def project(x_all, w, cosine, sine, piece, rows):
    count, dim = x_all.shape
    feats = w.shape[0] * piece
    tiled = lambda n: pl.BlockSpec((rows, n), lambda i: (i, 0))
    return pl.pallas_call(
        functools.partial(project_kernel, piece),
        grid=(count // rows,),
        in_specs=[tiled(dim), full(w.shape), tiled(LANES), tiled(LANES)],
        out_specs=[
            tiled(feats),
            pl.BlockSpec((2, rows, feats), lambda i: (0, i, 0)),
            tiled(dim),
        ],
        out_shape=[
            jax.ShapeDtypeStruct((count, feats), bf),
            jax.ShapeDtypeStruct((2, count, feats), bf),
            jax.ShapeDtypeStruct((count, dim), bf),
        ],
        compiler_params=params(),
        cost_estimate=cost(count * 0.009),
        name="project",
    )(x_all, w, cosine, sine)


def flip_kernel(piece, q_ref, k_ref, v_ref, o_ref, ga_ref, gm_ref, sent_ref, out_ref):
    size = sent_ref.shape[0]
    for i, ref in enumerate((q_ref, k_ref, v_ref)):
        sent_ref[:, i * piece : (i + 1) * piece, :] = (
            ref[...].T.astype(bf).reshape(size, piece, ref.shape[0])
        )
    row = lax.broadcasted_iota(jnp.int32, (PAD, q_ref.shape[0]), 0)
    gains = jnp.where(row == 0, ga_ref[...], gm_ref[...]).astype(bf)
    for j in range(size):
        sent_ref[j, 3 * piece :, :] = gains
    out_ref[...] = o_ref[...].T.astype(bf)


def flip(w_query, w_key, w_value, w_output, attn_gain, mlp_gain, size):
    rows, feats = w_query.shape
    piece = feats // size
    return pl.pallas_call(
        functools.partial(flip_kernel, piece),
        out_shape=[
            jax.ShapeDtypeStruct((size, 3 * piece + PAD, rows), bf),
            jax.ShapeDtypeStruct((feats, rows), bf),
        ],
        compiler_params=params(),
        cost_estimate=cost(5),
        name="flip",
    )(w_query, w_key, w_value, w_output, attn_gain[None], mlp_gain[None])


def head_lanes(rows, head):
    lane = lax.broadcasted_iota(jnp.int32, (rows, LANES), 1)
    return (lane < HD) if head == 0 else (lane >= HD)


def attend_kernel(tile, low_ref, high_ref, q_ref, kv_ref, o_ref, lse_ref, vt_ref):
    nu, _, nb, tok, feats = kv_ref.shape
    width = nu * tok
    rows = tile * tok
    pairs = feats // LANES
    heads = range(2 * pairs)
    lanes = [slice(h // 2 * LANES, (h // 2 + 1) * LANES) for h in heads]
    j = pl.program_id(0)

    @pl.when(j == 0)
    def _():
        for c in range(nb):
            vt_ref[c] = kv_ref[:, 1, c].reshape(width, feats).T

    low, high = low_ref[0], high_ref[0]
    q = q_ref[...] * jnp.asarray(1.0 / math.sqrt(HD), bf)
    q_heads = [
        jnp.where(head_lanes(rows, h % 2), q[:, lanes[h]], jnp.zeros((rows, LANES), bf))
        for h in heads
    ]
    place_k = lax.broadcasted_iota(jnp.int32, (width, rows), 0)

    def step(chunk, state):
        k = kv_ref[:, 0, chunk].reshape(width, feats)
        start = chunk * width
        ok = (place_k >= low - start) & (place_k <= high - start)
        scores = [jnp.where(ok, dot_t(k[:, lanes[h]], q_heads[h]), NEG) for h in heads]
        new = []
        for h in heads:
            best, total, acc = state[h]
            best_new = jnp.maximum(best, jnp.max(scores[h], axis=0, keepdims=True))
            p = jnp.exp(scores[h] - best_new)
            factor = jnp.exp(best - best_new)
            total = total * factor + jnp.sum(p, axis=0, keepdims=True)
            acc = acc * factor + dot_n(vt_ref[chunk, h * HD : (h + 1) * HD], p.astype(bf))
            new.append((best_new, total, acc))
        return tuple(new)

    start = (
        jnp.full((1, rows), NEG, f32),
        jnp.zeros((1, rows), f32),
        jnp.zeros((HD, rows), f32),
    )
    state = lax.fori_loop(0, (j + 1) * tile, step, (start,) * len(heads))
    o_ref[...] = jnp.concatenate([acc / total for _, total, acc in state], axis=0).T.astype(bf)
    lse_ref[0] = jnp.concatenate([best + jnp.log(total) for best, total, _ in state], axis=0)


def attend(low, high, q, kv, tile):
    nu, _, nb, tok, feats = kv.shape
    rows = tile * tok
    nq = nb // tile
    heads = feats // HD
    row_spec = pl.BlockSpec((1, 1, rows), lambda j: (j, 0, 0))
    q_spec = pl.BlockSpec((rows, feats), lambda j: (j, 0))
    return pl.pallas_call(
        functools.partial(attend_kernel, tile),
        grid=(nq,),
        in_specs=[row_spec, row_spec, q_spec, full(kv.shape)],
        out_specs=[q_spec, pl.BlockSpec((1, heads, rows), lambda j: (j, 0, 0))],
        out_shape=[
            jax.ShapeDtypeStruct((nb * tok, feats), bf),
            jax.ShapeDtypeStruct((nq, heads, rows), f32),
        ],
        scratch_shapes=[pltpu.VMEM((nb, feats, nu * tok), bf)],
        compiler_params=params(),
        cost_estimate=cost(27 * nb * tok * nb / 8192),
        name="attend",
    )(low, high, q, kv)


def attend_back_kernel(
    tile,
    spots_ref,
    low_ref,
    high_ref,
    cos_ref,
    sin_ref,
    q_ref,
    do_ref,
    o_ref,
    lse_ref,
    kv_ref,
    dq_ref,
    dkv_ref,
    acc_ref,
    delta_ref,
    sums_ref,
):
    nu, _, _, tok, feats = kv_ref.shape
    nq, heads, rows = lse_ref.shape
    width = nu * tok
    pairs = feats // LANES
    chunk = pl.program_id(0)
    scale = jnp.asarray(1.0 / math.sqrt(HD), bf)

    @pl.when(chunk == 0)
    def _():
        acc_ref[...] = jnp.zeros_like(acc_ref)
        lane = lax.broadcasted_iota(jnp.int32, (8, feats), 1)
        row = lax.broadcasted_iota(jnp.int32, (8, feats), 0)
        mine = jnp.where(lane // HD == row, 1.0, 0.0).astype(f32)
        for j in range(nq):
            at = pl.ds(j * rows, rows)
            delta_ref[j] = lax.dot_general(
                mine,
                do_ref[at, :].astype(f32) * o_ref[at, :].astype(f32),
                (((1,), (1,)), ((), ())),
                preferred_element_type=f32,
                precision=lax.Precision.HIGHEST,
            )

    k_all = kv_ref[:, 0, 0].reshape(width, feats)
    v_all = kv_ref[:, 1, 0].reshape(width, feats)
    lanes = [slice(p * LANES, (p + 1) * LANES) for p in range(pairs)]
    k = [k_all[:, at] for at in lanes]
    v = [v_all[:, at] for at in lanes]
    k_turned = [part.T for part in k]
    place_k = lax.broadcasted_iota(jnp.int32, (width, rows), 0)
    start = chunk * width
    sums_ref[...] = jnp.zeros_like(sums_ref)

    def step(j, _):
        at = pl.ds(pl.multiple_of(j * rows, rows), rows)
        q = q_ref[at, :] * scale
        do = do_ref[at, :]
        ok = (place_k >= low_ref[j] - start) & (place_k <= high_ref[j] - start)
        q_heads, do_heads = [
            [
                jnp.where(head_lanes(rows, h % 2), part[:, lanes[h // 2]], jnp.zeros((rows, LANES), bf))
                for h in range(2 * pairs)
            ]
            for part in (q, do)
        ]
        scores = [dot_t(k[h // 2], q_heads[h]) for h in range(2 * pairs)]
        d_probs = [dot_t(v[h // 2], do_heads[h]) for h in range(2 * pairs)]
        for pair in range(pairs):
            dk = dv = 0.0
            dq = []
            for i in range(2):
                h = 2 * pair + i
                p = jnp.exp(jnp.where(ok, scores[h] - lse_ref[j, h : h + 1], NEG))
                ds = (p * (d_probs[h] - delta_ref[j, h : h + 1])).astype(bf)
                dv = dv + dot_n(p.astype(bf), do_heads[h])
                dk = dk + dot_n(ds, q_heads[h])
                dq.append(dot_n(k_turned[pair][i * HD : (i + 1) * HD], ds))
            acc_ref[j, lanes[pair]] = acc_ref[j, lanes[pair]] + jnp.concatenate(dq, axis=0)
            sums_ref[0, pair] = sums_ref[0, pair] + dk
            sums_ref[1, pair] = sums_ref[1, pair] + dv
        return 0

    lax.fori_loop(chunk // tile, nq, step, 0)
    for i in range(2):
        for pair in range(pairs):
            for u in range(nu):
                dkv_ref[spots_ref[u], i, 0, :, lanes[pair]] = (
                    sums_ref[i, pair, u * tok : (u + 1) * tok].astype(bf)
                )

    @pl.when(chunk == pl.num_programs(0) - 1)
    def _():
        dq = jnp.concatenate([acc_ref[j].T for j in range(nq)], axis=0) * (1.0 / math.sqrt(HD))
        cosine, sine = wide(cos_ref[...], feats), wide(sin_ref[...], feats)
        dq_ref[...] = (dq * cosine - turned(dq) * sine).astype(bf)


def attend_back(spots, low, high, cosine, sine, q, do, o, lse, kv, tile):
    nu, _, nb, tok, feats = kv.shape
    rows = tile * tok
    nq = nb // tile
    kv_spec = pl.BlockSpec((nu, 2, 1, tok, feats), lambda c, _: (0, 0, c, 0, 0))
    return pl.pallas_call(
        functools.partial(attend_back_kernel, tile),
        grid_spec=pltpu.PrefetchScalarGridSpec(
            num_scalar_prefetch=1,
            grid=(nb,),
            in_specs=[
                *[full(part.shape) for part in (low, high, cosine, sine, q, do, o, lse)],
                kv_spec,
            ],
            out_specs=[full(q.shape), kv_spec],
            scratch_shapes=[
                pltpu.VMEM((nq, feats, rows), f32),
                pltpu.VMEM((nq, 8, rows), f32),
                pltpu.VMEM((2, feats // LANES, nu * tok, LANES), f32),
            ],
        ),
        out_shape=[
            jax.ShapeDtypeStruct(q.shape, bf),
            jax.ShapeDtypeStruct(kv.shape, bf),
        ],
        compiler_params=params(),
        cost_estimate=cost(41 * nb * tok * nb / 8192),
        name="attend_back",
    )(spots, low, high, cosine, sine, q, do, o, lse, kv)


def output_kernel(x_ref, o_ref, w_ref, gain_ref, x1_ref, normed_ref):
    blocks, pieces, groups, piece, width = w_ref.shape
    square = 0.0
    for block in range(blocks):
        at = slice(block * width, (block + 1) * width)
        total = x_ref[:, at].astype(f32)
        for g in range(groups):
            total = total + dot_n(o_ref[g], w_ref[block, :, g].reshape(pieces * piece, width))
        x1_ref[:, at] = total
        square = square + jnp.sum(total * total, axis=1, keepdims=True)
    r2 = lax.rsqrt(square * (1.0 / (blocks * width)) + epsilon)
    normed_ref[...] = (x1_ref[...] * r2 * gain_ref[...]).astype(bf)


def output_project(x_all, o_all, w_out, gain, rows):
    count, dim = x_all.shape
    groups, _, feats = o_all.shape
    tiled = pl.BlockSpec((rows, dim), lambda i: (i, 0))
    return pl.pallas_call(
        output_kernel,
        grid=(count // rows,),
        in_specs=[
            tiled,
            pl.BlockSpec((groups, rows, feats), lambda i: (0, i, 0)),
            full(w_out.shape),
            full(gain.shape),
        ],
        out_specs=[tiled, tiled],
        out_shape=[
            jax.ShapeDtypeStruct((count, dim), f32),
            jax.ShapeDtypeStruct((count, dim), bf),
        ],
        compiler_params=params(),
        cost_estimate=cost(count * 0.015),
        name="output_project",
    )(x_all, o_all, w_out, gain)


def output_back_kernel(d_ref, w_ref, out_ref):
    blocks, pieces, _, piece, width = w_ref.shape
    total = 0.0
    for block in range(blocks):
        at = slice(block * width, (block + 1) * width)
        total = total + dot_t(d_ref[:, at], w_ref[block, :, 0].reshape(pieces * piece, width))
    out_ref[0] = total.astype(bf)


def output_back(d_attn, w_out):
    tok, dim = d_attn.shape
    blocks, pieces, groups, piece, width = w_out.shape
    return pl.pallas_call(
        output_back_kernel,
        grid=(groups,),
        in_specs=[
            full(d_attn.shape),
            pl.BlockSpec((blocks, pieces, 1, piece, width), lambda g: (0, 0, g, 0, 0)),
        ],
        out_specs=pl.BlockSpec((1, tok, pieces * piece), lambda g: (g, 0, 0)),
        out_shape=jax.ShapeDtypeStruct((groups, tok, pieces * piece), bf),
        compiler_params=params(),
        cost_estimate=cost(8),
        name="output_back",
    )(d_attn, w_out)


def turned_back(value, cos_ref, sin_ref):
    feats = value.shape[1]
    value = value.astype(f32)
    return (value * wide(cos_ref[...], feats) - turned(value) * wide(sin_ref[...], feats)).astype(bf)


def project_back_kernel(piece, _, w_ref, cos_ref, sin_ref, dq_ref, dkv_ref, dn_ref):
    blocks, width = w_ref.shape[1], w_ref.shape[3]
    parts = (dq_ref[...], turned_back(dkv_ref[0], cos_ref, sin_ref), dkv_ref[1])
    for block in range(blocks):
        total = 0.0
        for part in range(3):
            total = total + dot_n(parts[part], weight_block(w_ref, block, part, piece))
        dn_ref[0, :, block * width : (block + 1) * width] = total.astype(bf)


def project_back(w, cosine, sine, dq, dkv, piece, order):
    size = order.shape[0]
    count, feats = dq.shape
    rows = count // size
    dim = w.shape[1] * w.shape[3]
    tiled = lambda width: pl.BlockSpec((rows, width), lambda i, at: (at[i], 0))
    return pl.pallas_call(
        functools.partial(project_back_kernel, piece),
        grid_spec=pltpu.PrefetchScalarGridSpec(
            num_scalar_prefetch=1,
            grid=(size,),
            in_specs=[
                full(w.shape),
                tiled(LANES),
                tiled(LANES),
                tiled(feats),
                pl.BlockSpec((2, rows, feats), lambda i, at: (0, at[i], 0)),
            ],
            out_specs=pl.BlockSpec((1, rows, dim), lambda i, _: (i, 0, 0)),
        ),
        out_shape=jax.ShapeDtypeStruct((size, rows, dim), bf),
        compiler_params=params(),
        cost_estimate=cost(count * 0.01),
        name="project_back",
    )(order, w, cosine, sine, dq, dkv)


def projection_grads_kernel(
    piece, spots_ref, dq_ref, dkv_ref, cos_ref, sin_ref, w_ref, right_ref, gain_ref, out_ref, turned_ref
):
    n, feats, _ = turned_ref.shape
    pieces = out_ref.shape[0]

    @pl.when(pl.program_id(0) == 0)
    def _():
        turned_ref[0] = dq_ref[...].T
        turned_ref[1] = turned_back(dkv_ref[0], cos_ref, sin_ref).T
        turned_ref[2] = dkv_ref[1].T

    right = right_ref[...]
    total = 0.0
    for i in range(n):
        grad = dot_n(turned_ref[i], right)
        total = total + jnp.sum(
            grad * weight_block(w_ref, 0, i, piece).astype(f32), axis=0, keepdims=True
        )
        grad = grad.astype(bf)
        for u in range(pieces):
            out_ref[spots_ref[u], 0, i * piece : (i + 1) * piece, :] = (
                grad[u * piece : (u + 1) * piece]
            )
    gain = w_ref[0, 0, 3 * piece : 3 * piece + PAD, :][0:1].astype(f32)
    row = lax.broadcasted_iota(jnp.int32, (PAD, right.shape[1]), 0)
    gains = jnp.where(row == 0, total / gain, gain_ref[...]).astype(bf)
    for u in range(pieces):
        out_ref[u, 0, n * piece :, :] = gains


def projection_grads(spots, dq, dkv, cosine, sine, w, right, gain, piece):
    count, feats = dq.shape
    pieces, blocks, rows, width = w.shape
    return pl.pallas_call(
        functools.partial(projection_grads_kernel, piece),
        grid_spec=pltpu.PrefetchScalarGridSpec(
            num_scalar_prefetch=1,
            grid=(blocks,),
            in_specs=[
                *[full(part.shape) for part in (dq, dkv, cosine, sine)],
                pl.BlockSpec((pieces, 1, rows, width), lambda i, _: (0, i, 0, 0)),
                pl.BlockSpec((count, width), lambda i, _: (0, i)),
                pl.BlockSpec((1, width), lambda i, _: (0, i)),
            ],
            out_specs=pl.BlockSpec((pieces, 1, rows, width), lambda i, _: (0, i, 0, 0)),
            scratch_shapes=[pltpu.VMEM((3, feats, count), bf)],
        ),
        out_shape=jax.ShapeDtypeStruct(w.shape, bf),
        compiler_params=params(),
        cost_estimate=cost(8),
        name="projection_grads",
    )(spots, dq, dkv, cosine, sine, w, right, gain)


def output_grads_kernel(o_ref, d_ref, out_ref):
    pieces, _, piece, width = out_ref.shape
    grad = dot_n(o_ref[0].T, d_ref[...])
    out_ref[:, 0] = grad.astype(bf).reshape(pieces, piece, width)


def output_grads(o_all, d_columns, pieces):
    groups, count, feats = o_all.shape
    width = d_columns.shape[1]
    shape = (pieces, groups, feats // pieces, width)
    return pl.pallas_call(
        output_grads_kernel,
        grid=(groups,),
        in_specs=[
            pl.BlockSpec((1, count, feats), lambda g: (g, 0, 0)),
            full(d_columns.shape),
        ],
        out_specs=pl.BlockSpec((pieces, 1, *shape[2:]), lambda g: (0, g, 0, 0)),
        out_shape=jax.ShapeDtypeStruct(shape, bf),
        compiler_params=params(),
        cost_estimate=cost(6),
        name="output_grads",
    )(o_all, d_columns)


def prepare_kernel(wg_ref, wu_ref, wd_ref, out_ref):
    for i, ref in enumerate((wg_ref, wu_ref, wd_ref)):
        out_ref[0, i] = ref[...].astype(bf)


def prepare(w_gate, w_up, w_down, size):
    rows, columns = w_gate.shape
    width = columns // size
    if width % LANES:
        stacked = jnp.stack([w.astype(bf) for w in (w_gate, w_up, w_down)])
        return jnp.transpose(stacked.reshape(3, rows, size, width), (2, 0, 1, 3))
    spec = pl.BlockSpec((rows, width), lambda i: (0, i))
    return pl.pallas_call(
        prepare_kernel,
        grid=(size,),
        in_specs=[spec] * 3,
        out_specs=pl.BlockSpec((1, 3, rows, width), lambda i: (i, 0, 0, 0)),
        out_shape=jax.ShapeDtypeStruct((size, 3, rows, width), bf),
        compiler_params=params(),
        cost_estimate=cost(4),
        name="prepare",
    )(w_gate, w_up, w_down)


def finish_kernel(in_ref, *outs):
    n, _, _, width = in_ref.shape
    for k in range(n):
        for i in range(3):
            outs[i][:, k * width : (k + 1) * width] = in_ref[k, i].astype(f32)


def finish(parts):
    n, _, rows, width = parts.shape
    if width % LANES:
        out = jnp.transpose(parts, (1, 2, 0, 3)).reshape(3, rows, n * width).astype(f32)
        return [out[i] for i in range(3)]
    return pl.pallas_call(
        finish_kernel,
        out_shape=[jax.ShapeDtypeStruct((rows, n * width), f32)] * 3,
        compiler_params=params(),
        cost_estimate=cost(5),
        name="finish",
    )(parts)


def whole_weight(ref, k):
    w = ref[:, k]
    return w.reshape(w.shape[0] * w.shape[1], w.shape[2])


def hidden_kernel(n, *refs):
    n_ref, g_ref = refs[:2]
    act_ref, dg_ref, du_ref = refs[2 + n :]
    normed, cot = n_ref[...], g_ref[...]
    for i in range(n):
        w_ref = refs[2 + i]
        gate = dot_n(normed, whole_weight(w_ref, 0))
        up = dot_n(normed, whole_weight(w_ref, 1))
        d_act = dot_n(cot, whole_weight(w_ref, 2))
        sigma = jax.nn.sigmoid(gate)
        silu = gate * sigma
        act_ref[i] = (silu * up).astype(bf)
        du_ref[i] = (d_act * silu).astype(bf)
        dg_ref[i] = (d_act * up * (sigma * (1.0 + gate * (1.0 - sigma)))).astype(bf)


def hidden(normed, cot, weights, rows):
    count, dim = normed.shape
    n = len(weights)
    width = weights[0].shape[3]
    tiled = pl.BlockSpec((rows, dim), lambda i: (i, 0))
    out = pl.BlockSpec((n, rows, width), lambda i: (0, i, 0))
    return pl.pallas_call(
        functools.partial(hidden_kernel, n),
        grid=(count // rows,),
        in_specs=[tiled, tiled] + [full(w.shape) for w in weights],
        out_specs=[out] * 3,
        out_shape=[jax.ShapeDtypeStruct((n, count, width), bf)] * 3,
        compiler_params=params(),
        cost_estimate=cost(20),
        name="hidden",
    )(normed, cot, *weights)


def mix_kernel(which, n, _, *refs):
    m = len(which)
    lefts, weights, out_ref = refs[: 2 * m], refs[2 * m : -1], refs[-1]
    total = 0.0
    for k in range(m):
        for i in range(n):
            left = jnp.concatenate([lefts[2 * k][i], lefts[2 * k + 1][i]], axis=0)
            total = total + dot_t(left, whole_weight(weights[i], k))
    out_ref[...] = total.astype(bf).reshape(out_ref.shape)


def mix(lefts, weights, which, order):
    n, count, width = lefts[0].shape
    size = order.shape[0]
    rows = count // size
    blocks, _, rows_w, _ = weights[0].shape
    dim = blocks * rows_w
    chosen = pl.BlockSpec(
        (blocks, len(which), rows_w, width), lambda i, _: (0, which[0] // len(which), 0, 0)
    )
    pair = [
        pl.BlockSpec((n, rows, width), lambda i, at: (0, at[2 * i], 0)),
        pl.BlockSpec((n, rows, width), lambda i, at: (0, at[2 * i + 1], 0)),
    ]
    return pl.pallas_call(
        functools.partial(mix_kernel, which, n),
        grid_spec=pltpu.PrefetchScalarGridSpec(
            num_scalar_prefetch=1,
            grid=(size // 2,),
            in_specs=pair * len(which) + [chosen] * n,
            out_specs=pl.BlockSpec((2, rows, dim), lambda i, _: (i, 0, 0)),
        ),
        out_shape=jax.ShapeDtypeStruct((size, rows, dim), bf),
        compiler_params=params(),
        cost_estimate=cost(8 * len(which)),
        name="mix",
    )(order, *[left for left in lefts for _ in range(2)], *weights)


def hidden_grads_kernel(n_ref, g_ref, dg_ref, du_ref, act_ref, *outs):
    normed, cot = n_ref[...].T, g_ref[...].T
    for i, out_ref in enumerate(outs):
        for k, grad in enumerate(
            (dot_n(normed, dg_ref[i]), dot_n(normed, du_ref[i]), dot_n(cot, act_ref[i]))
        ):
            out_ref[:, k] = grad.astype(bf).reshape(out_ref.shape[0], *out_ref.shape[2:])


def hidden_grads(normed, cot, d_gate, d_up, act, rows):
    count, dim = normed.shape
    block = max(rows, LANES)
    n, _, width = act.shape
    columns = pl.BlockSpec((count, block), lambda i: (0, i))
    return pl.pallas_call(
        hidden_grads_kernel,
        grid=(dim // block,),
        in_specs=[columns, columns] + [full(act.shape)] * 3,
        out_specs=[pl.BlockSpec((block // rows, 3, rows, width), lambda i: (i, 0, 0, 0))] * n,
        out_shape=[jax.ShapeDtypeStruct((dim // rows, 3, rows, width), bf)] * n,
        compiler_params=params(),
        cost_estimate=cost(25),
        name="hidden_grads",
    )(normed, cot, d_gate, d_up, act)


def on_device(
    tokens,
    segments,
    cotangent,
    attn_gain,
    w_query,
    w_key,
    w_value,
    w_output,
    mlp_gain,
    w_gate,
    w_up,
    w_down,
):
    nb, nu = lax.axis_size("blk"), lax.axis_size("uly")
    b, u = lax.axis_index("blk"), lax.axis_index("uly")
    tok, dim = tokens.shape
    seq = segments.shape[0]
    rows, feats_u = w_query.shape
    group = feats_u * nu // nb
    strided = (feats_u // HD) % nb == 0 and rows % LANES == 0
    count = nb * tok
    tile = 2
    both = ("blk", "uly")
    block = rows if strided else 2 * LANES
    blocks = dim // block
    pieces = nu if strided else 1
    piece = group // nu if strided else -(-group // LANES) * LANES
    feats = pieces * piece
    step = 2 * tok

    seg_mine = pick(jnp.swapaxes(segments.reshape(nb, nu, tok), 0, 1), u).reshape(count)
    index = (
        jnp.arange(nb, dtype=jnp.int32)[:, None] * (nu * tok)
        + u * tok
        + jnp.arange(tok, dtype=jnp.int32)[None, :]
    ).reshape(count)
    first = jnp.sum((segments[None, :] < seg_mine[:, None]).astype(jnp.int32), axis=1)
    lane = jnp.arange(LANES, dtype=jnp.int32)
    freq = theta_base ** (-((lane % (HD // 2)).astype(f32) * 2.0) / HD)
    angles = (index - first).astype(f32)[:, None] * freq[None, :]
    cosine = jnp.cos(angles)
    sine = jnp.sin(angles) * jnp.where(lane % HD < HD // 2, -1.0, 1.0)[None, :]
    low = first.reshape(nb // tile, 1, tile * tok)
    high = index.reshape(nb // tile, 1, tile * tok)

    ff_u = w_gate.shape[1]
    ff_piece = ff_u // nb
    tokens_plan = gather_plan(tokens, "blk")

    def prepared():
        yield []
        (value,) = yield [prepare(w_gate, w_up, w_down, nb)]
        return value

    def swapped(parts, spare=0):
        got = swap(parts, "blk")
        yield from idle(spare)
        (got,) = yield [got]
        return got

    if strided:
        sent, out_flipped = flip(w_query, w_key, w_value, w_output, attn_gain, mlp_gain, nb)
        x_all, ff_sent, w_qkv = together(
            tokens_plan,
            prepared(),
            chain(swapped(sent, 1), lambda got: gather_plan(got, "uly")),
        )
    else:
        gains = jnp.stack([attn_gain, mlp_gain]).astype(bf)
        flipped = [jnp.transpose(w.astype(bf)) for w in (w_query, w_key, w_value, w_output)]
        out_flipped = flipped[3]
        sent = gather(jnp.stack(flipped[:3])[None], "uly")
        sent = jnp.transpose(sent, (0, 2, 1, 3)).reshape(nb, group, 3, rows)
        x_all, ff_sent, got = together(tokens_plan, prepared(), swapped(sent))
        got = jnp.transpose(got, (2, 1, 0, 3)).reshape(3, group, dim)
        got = jnp.pad(got, ((0, 0), (0, piece - group), (0, 0))).reshape(3 * piece, dim)
        all_gains = jnp.transpose(gather(gains[None], "blk"), (1, 0, 2)).reshape(2, dim)
        got = jnp.concatenate([got, jnp.pad(all_gains, ((0, PAD - 2), (0, 0)))])
        w_qkv = jnp.transpose(got.reshape(3 * piece + PAD, blocks, block), (1, 0, 2))[None]
    x_all = x_all.reshape(count, dim)
    gain1, gain2 = [
        w_qkv[0, :, 3 * piece + i, :].reshape(1, dim).astype(f32) for i in range(2)
    ]

    ff_got = swap(after(ff_sent, x_all), "blk")
    w_out = gather(after(out_flipped, x_all)[None], both)
    cot_all = gather(after(cotangent, x_all, w_out), "blk")
    if strided:
        w_out = w_out.reshape(nb, nu, nb, piece, rows)
    else:
        w_out = jnp.transpose(w_out.reshape(nb, nu * feats_u, rows), (1, 0, 2))
        w_out = jnp.pad(
            w_out.reshape(nb, group, dim), ((0, 0), (0, piece - group), (0, 0))
        )
        w_out = jnp.transpose(w_out.reshape(nb, piece, blocks, block), (2, 0, 1, 3))[:, None]

    q, kv, normed = project(x_all, w_qkv, cosine, sine, piece, step)
    (kv_all,) = together(gather_plan(kv.reshape(2, nb, tok, feats), "uly"))
    o, lse = attend(low, high, q, kv_all, tile)
    ff_got, o = lax.optimization_barrier((ff_got, o))
    rounds = Rounds()
    rounds.add(o=gather_plan(o, "blk"), ff=gather_near_plan(ff_got, "uly", nb // 4))
    (o_all,) = rounds.until("o")
    x1, normed2 = output_project(x_all, o_all, w_out, gain2, step)

    (w_ff,) = rounds.until("ff")

    act, d_gate, d_up = hidden(normed2, cot_all, w_ff, step)
    order, plain = scatter_order("blk"), jnp.arange(nb, dtype=jnp.int32)
    uly_order, each = scatter_order("uly"), jnp.arange(nu, dtype=jnp.int32)
    spots = jnp.sum(jnp.where(uly_order[:, None] == each[None, :], each[:, None], 0), axis=0)
    d_norm2 = mix([d_gate, d_up], w_ff, (0, 1), order)

    def mlp_plan():
        yield []
        (out,) = yield [mix([act], w_ff, (2,), plain)]
        return out

    def hidden_grads_plan():
        grads = yield hidden_grads(
            after(normed2, d_norm2), cot_all, d_gate, d_up, act, rows
        )
        return (yield from scatter_near_plan(grads, "uly", 2 * nb))

    rounds = Rounds()
    rounds.add(
        d_norm2=scatter_plan(d_norm2, "blk", True),
        mlp=mlp_plan(),
        ff=hidden_grads_plan(),
    )
    d_norm2, mlp_out = rounds.until("d_norm2", "mlp")
    x1_own = lax.dynamic_slice_in_dim(x1, b * tok, tok, 0)
    mlp_out = scatter(after(mlp_out, d_norm2).reshape(count, dim), "blk")
    r2_own = rms_scale(x1_own)
    gain2_part = jnp.sum(d_norm2 * x1_own * r2_own, axis=0, keepdims=True)
    z_two = gain2 * d_norm2
    dx1 = (
        cotangent.astype(f32)
        + r2_own * z_two
        - x1_own * r2_own * r2_own * r2_own * jnp.mean(z_two * x1_own, axis=-1, keepdims=True)
    )
    d_attn = dx1.astype(bf)

    d_o = output_back(d_attn, w_out)
    d_columns = jnp.transpose(d_attn.reshape(tok, nb, rows), (1, 0, 2))
    rounds.add(d_o=swap_plan(d_o, "blk"))
    (got,) = rounds.until("d_o")
    d_o = got.reshape(count, feats)
    d_columns = swap(after(d_columns, d_o), "blk")
    dq, dkv = attend_back(spots, low, high, cosine, sine, q, d_o, o, lse, kv_all, tile)
    dkv, mlp_out, d_columns = lax.optimization_barrier((dkv, mlp_out, d_columns))
    rounds.add(dkv=scatter_plan(dkv, "uly", True))
    (ff_mine,) = rounds.until("ff")
    ff_got = swap(ff_mine, "blk")
    out_grads = output_grads(o_all, d_columns.reshape(count, rows), pieces)
    if not strided:
        out_grads = out_grads[:, :, :group]
    (dkv,) = rounds.until("dkv")
    dkv, out_grads = lax.optimization_barrier((dkv, out_grads))
    rounds.add(out=scatter_plan(out_grads.reshape(nu, feats_u, rows), "uly"))
    dkv = dkv.astype(bf).reshape(2, count, feats)
    grads = projection_grads(
        spots if strided else jnp.zeros((1,), jnp.int32),
        *(dq, dkv, cosine, sine, w_qkv, normed, gain2_part, piece),
    )
    d_norm1 = project_back(w_qkv, cosine, sine, after(dq, grads), dkv, piece, order)
    last = scatter_plan(d_norm1, "blk", True)
    if strided:
        rounds.add(
            last=last,
            grads=chain(scatter_plan(grads, "uly", True), lambda mine: swapped(mine.astype(bf))),
        )
        d_norm1, got, out_grads = rounds.until("last", "grads", "out")
        gain_sums = jnp.sum(got[:, 3 * piece : 3 * piece + 2].astype(f32), axis=0)
        heads = [got[:, i * piece : (i + 1) * piece].reshape(feats_u, rows) for i in range(3)]
    else:
        wanted = grads[0, :, : 3 * piece].reshape(blocks, 3, piece, block)[:, :, :group]
        wanted = jnp.transpose(wanted, (1, 2, 0, 3)).reshape(3, group, nb, rows)
        rounds.add(last=last, grads=swapped(jnp.transpose(wanted, (2, 1, 0, 3))))
        d_norm1, got, out_grads = rounds.until("last", "grads", "out")
        got = scatter(got.reshape(nu, feats_u, 3, rows), "uly")[0]
        heads = [got[:, i] for i in range(3)]
        gain_parts = jnp.transpose(grads[0, :, 3 * piece : 3 * piece + 2], (1, 0, 2)).astype(f32)
        gain_sums = lax.psum(gain_parts.reshape(2, dim), both)
        gain_sums = lax.dynamic_slice_in_dim(gain_sums, b * rows, rows, 1)
    grad_output = jnp.transpose(out_grads)
    grad_query, grad_key, grad_value = [jnp.transpose(h).astype(f32) for h in heads]
    x_own = tokens.astype(f32)
    r1_own = rms_scale(x_own)
    z_one = gain1 * d_norm1
    grad_tokens = (
        dx1
        + r1_own * z_one
        - x_own * r1_own * r1_own * r1_own * jnp.mean(z_one * x_own, axis=-1, keepdims=True)
    )
    output = x1_own + mlp_out.astype(f32)
    return (
        output,
        grad_tokens,
        gain_sums[0],
        grad_query,
        grad_key,
        grad_value,
        grad_output,
        gain_sums[1],
        *finish(ff_got),
    )


def solution(mesh):
    tokens_split = P(("blk", "uly"), None)
    weights = P("blk", "uly")
    return jax.shard_map(
        on_device,
        mesh=mesh,
        in_specs=(
            tokens_split,
            P(),
            tokens_split,
            P("blk"),
            weights,
            weights,
            weights,
            weights,
            P("blk"),
            weights,
            weights,
            weights,
        ),
        out_specs=(
            tokens_split,
            tokens_split,
            P("blk"),
            weights,
            weights,
            weights,
            weights,
            P("blk"),
            weights,
            weights,
            weights,
        ),
        check_vma=False,
    )
```
